32 devices in a mesh: tok: 4 (over z), hid: 8 (over y, x, core).
Axes of the slice: x: 2, y: 2, z: 4, core: 2. Of those that a mesh axis runs over, the one named last changes fastest.
Arguments:
- resid_in: bfloat16 [128, 8192], P('hid', 'tok'), may hold values from -64 to 64
- norm_gain: float32 [8192], P('tok'), may hold values from 0.1 to 1.9
- gate_weight: bfloat16 [8192, 28672], P('tok', 'hid'), may hold values from -0.0625 to 0.0625
- up_weight: bfloat16 [8192, 28672], P('tok', 'hid'), may hold values from -0.0625 to 0.0625
- down_weight: bfloat16 [28672, 8192], P('hid', 'tok'), may hold values from -0.046875 to 0.046875
- labels: int32 [128], replicated, may hold values from 0 to 63
Outputs:
- gram: float32 [8192, 8192], P(('tok', 'hid'))
- cross: float32 [8192, 64], P(('tok', 'hid'))
The draws below stay inside these ranges and needn't reach their ends.
All inputs are finite; a program needn't handle non-finite values.
Results may differ from the reference program's by a relative error of at most 0.014.
Values may be sent and summed in bfloat16 or wider, within the bound.
No kernel may reach another device: no remote copies, remote signals or barrier semaphores. Data moves between devices by JAX's collectives and lax.ppermute only.
A program may use at most 128 MiB of HBM per device.

```python
import math
import jax
import jax.numpy as jnp
from jax import lax

D = 8192
FF = 28672
CLASSES = 64
TOKENS = 128
N_TOK = 4


def draw_resid_in(key, part):
    keys = jax.random.split(key, 3)
    rowscale = jnp.exp(jax.random.uniform(keys[0], (TOKENS, 1), jnp.float32, math.log(0.3), math.log(3.0)))
    colrand = jnp.exp(jax.random.uniform(keys[1], (1, D), jnp.float32, math.log(0.5), math.log(2.0)))
    ramp = jnp.exp(math.log(3.0) * (jnp.arange(D, dtype=jnp.float32)[None, :] / float(D) - 0.5))
    colscale = colrand * ramp
    base = jax.random.normal(keys[2], (TOKENS, D), jnp.float32)
    values = jnp.clip(rowscale * colscale * base, -64.0, 64.0)
    return values.astype(jnp.bfloat16)


def draw_labels(key, part):
    keys = jax.random.split(jax.random.fold_in(key, 7), 4)
    middle = (1 + jax.random.permutation(keys[0], CLASSES - 2)).astype(jnp.int32)
    allowed = jnp.concatenate([jnp.array([0, CLASSES - 1], jnp.int32), middle[:CLASSES - 4]])
    first = jax.random.randint(keys[1], (TOKENS,), 0, CLASSES - 2)
    second = jax.random.randint(keys[2], (TOKENS,), 0, CLASSES - 2)
    labels = allowed[jnp.minimum(first, second)]
    places = jax.random.permutation(keys[3], TOKENS)
    labels = labels.at[places[0]].set(0).at[places[1]].set(CLASSES - 1)
    return labels.astype(jnp.int32)


def with_spikes(values, key, source, target, shards_of, factor):
    def block_of(axis_at):
        return (jnp.arange(values.shape[axis_at]) // (values.shape[axis_at] // shards_of)).reshape((-1,) + (1,) * (values.ndim - 1 - axis_at))

    first = jax.random.permutation(key, shards_of)[block_of(target)]
    other_side = (block_of(target) + shards_of // 2) % shards_of
    return jnp.where((block_of(source) == first) | (block_of(source) == other_side), factor * values, values)


def shard_levels(stream_key, dims, pieces, smallest, top_value):
    gain, own = 1.0, jax.random.fold_in(stream_key, 6)
    for dim, parts in pieces:
        draws = jnp.exp(jax.random.uniform(jax.random.fold_in(own, dim), (parts,), jnp.float32, smallest / len(pieces), top_value / len(pieces)))
        gain = gain * jnp.repeat(draws, dims[dim] // parts).reshape([-1 if axis == dim else 1 for axis in range(len(dims))])
    return gain


def centred(key, dims, scale, limit, pieces=(), held_as=jnp.bfloat16):
    drawn = scale * jax.random.normal(key, dims, jnp.float32)
    if pieces:
        drawn = drawn * shard_levels(key, dims, pieces, -0.22, 0.18)
    return jnp.clip(drawn, -limit, limit).astype(held_as)


def gaussian_with(own_key, extent, scale, most, pieces, heavy, kind=jnp.bfloat16):
    drawn = scale * jax.random.normal(own_key, extent, jnp.float32)
    if pieces:
        drawn = drawn * shard_levels(own_key, extent, pieces, -0.22, 0.18)
    return jnp.clip(with_spikes(drawn, jax.random.fold_in(own_key, 3), *heavy), -most, most).astype(kind)


def setup_inputs(seed: int = 0) -> dict:
    arg_keys = jax.random.split(jax.random.key(seed), 7)
    resid_in = draw_resid_in(jax.random.fold_in(arg_keys[6], 71), 0)
    norm_gain = jnp.clip(1.0 + 0.18 * jax.random.normal(arg_keys[1], (D,), jnp.float32), 0.1, 1.9)
    gate_weight = centred(arg_keys[2], (D, FF), D ** -0.5, 0.0625, ((0, 4), (1, 8)))
    up_weight = centred(arg_keys[3], (D, FF), D ** -0.5, 0.0625, ((0, 4), (1, 8)))
    down_weight = gaussian_with(arg_keys[4], (FF, D), FF ** -0.5, 0.046875, ((0, 8), (1, 4)), (0, 1, 8, 2.0))
    labels = draw_labels(jax.random.fold_in(arg_keys[6], 71), 0)
    return {"resid_in": resid_in, "norm_gain": norm_gain, "gate_weight": gate_weight, "up_weight": up_weight, "down_weight": down_weight, "labels": labels}


def reference(resid_in, norm_gain, gate_weight, up_weight, down_weight, labels):
    xf = resid_in.astype(jnp.float32)
    meansq = lax.optimization_barrier(jnp.mean(xf * xf, axis=1, keepdims=True))
    normed = (xf * lax.rsqrt(meansq + 1e-05) * norm_gain[None, :]).astype(jnp.bfloat16)
    width = D // N_TOK
    gate = jnp.zeros((resid_in.shape[0], FF), jnp.float32)
    up = jnp.zeros((resid_in.shape[0], FF), jnp.float32)
    for block in range(N_TOK):
        rows = normed[:, block * width:(block + 1) * width]
        term_g = lax.optimization_barrier(jnp.dot(rows, gate_weight[block * width:(block + 1) * width], preferred_element_type=jnp.float32).astype(jnp.bfloat16))
        term_u = lax.optimization_barrier(jnp.dot(rows, up_weight[block * width:(block + 1) * width], preferred_element_type=jnp.float32).astype(jnp.bfloat16))
        gate = gate + term_g.astype(jnp.float32)
        up = up + term_u.astype(jnp.float32)
    hidden = (jax.nn.silu(gate) * up).astype(jnp.bfloat16)
    mlp_out = jnp.dot(hidden, down_weight, preferred_element_type=jnp.float32)
    resid = (xf + mlp_out).astype(jnp.bfloat16)
    gram = jnp.dot(resid.T, resid, preferred_element_type=jnp.float32) / float(resid.shape[0])
    onehot = (labels[:, None] == jnp.arange(CLASSES, dtype=jnp.int32)[None, :]).astype(jnp.bfloat16)
    counts = lax.optimization_barrier(jnp.sum(onehot.astype(jnp.float32), axis=0))
    cross = jnp.dot(resid.T, onehot, preferred_element_type=jnp.float32) / jnp.maximum(counts, 1.0)[None, :]
    return (gram, cross)
```

```python
import functools
import jax
import jax.numpy as jnp
from jax import lax
from jax.experimental import pallas as pl
from jax.experimental.pallas import tpu as pltpu
from jax.sharding import PartitionSpec as P

D = 8192
CLASSES = 64
BF16 = jnp.bfloat16
F32 = jnp.float32


def swap(value, axis, size, mask):
    return lax.ppermute(value, axis, [(i, i ^ mask) for i in range(size)])


def pick(cases, key):
    out = cases[-1][1]
    for number, value in reversed(cases[:-1]):
        out = jnp.where(key == number, value, out)
    return out


def gather_tokens(own, h, n_hid):
    chips = n_hid // 2
    rows = own.shape[0]
    near = [own] + [swap(own, "hid", n_hid, 2 * e) for e in range(1, chips)]
    near = jnp.concatenate(near, axis=0)
    far = swap(near, "hid", n_hid, 1)
    both = jnp.concatenate([near, far], axis=0)
    ntok = both.shape[0]
    place = jnp.arange(ntok, dtype=jnp.int32)
    slot = place // rows
    owner = h ^ (2 * (slot % chips) + slot // chips)
    token = owner * rows + place % rows
    order = (jnp.arange(ntok, dtype=jnp.int32)[:, None] == token[None, :]).astype(BF16)
    return jnp.dot(order, both, preferred_element_type=F32)


def chain_sums(parts, rows, dist, n_tok, to_end):
    count = len(parts)
    sums = []
    got = None
    for t in range(count + n_tok - 1):
        cases = [(j, parts[t - j][rows]) for j in range(n_tok) if 0 <= t - j < count]
        value = pick(cases, dist).astype(F32)
        if got is not None:
            value = value + got.astype(F32)
        if t >= n_tok - 1:
            sums.append(value)
        if t <= count + n_tok - 3:
            pairs = [(to_end(j), to_end(j + 1)) for j in range(n_tok - 1) if 0 <= t - j < count]
            got = lax.ppermute(value.astype(BF16), "tok", pairs)
    return sums


def chain_copies(blocks, dist, n_tok, to_end):
    count = len(blocks)
    got = []
    for s in range(count + n_tok - 2):
        cases = []
        if s < count:
            cases.append((0, blocks[s]))
        if s > 0:
            cases.append((1, got[s - 1]))
        value = blocks[s] if s == 0 else (jnp.where(dist == 0, blocks[s], got[s - 1]) if s < count else got[s - 1])
        pairs = [(to_end(j), to_end(j + 1)) for j in range(n_tok - 1) if 0 <= s - j < count]
        got.append(lax.ppermute(value, "tok", pairs))
    return [
        pick([(0, blocks[k])] + [(j, got[k + j - 1]) for j in range(1, n_tok)], dist)
        for k in range(count)
    ]


def gram_kernel(n_hid, n_tok, ntok, own_ref, *refs):
    chips = n_hid // 2
    groups, (out_ref, tiles, sems) = refs[:-3], refs[-3:]
    z = lax.axis_index("tok")
    h = lax.axis_index("hid")
    width = own_ref.shape[1]
    left = own_ref[...].T
    copies = []
    for number, (zmask, hmask, ref, at) in enumerate(slots_of(groups, chips, n_tok)):
        tiles[number] = jnp.dot(left, ref[at], preferred_element_type=F32) * (1.0 / ntok)
        column = ((z ^ zmask) * n_hid + (h ^ hmask)) * width
        copy = pltpu.make_async_copy(
            tiles.at[number], out_ref.at[:, pl.ds(pl.multiple_of(column, width), width)], sems.at[number]
        )
        copy.start()
        copies.append(copy)
    for copy in copies:
        copy.wait()


def slots_of(groups, chips, n_tok):
    for core in range(2):
        for e in range(chips):
            yield 0, 2 * e + core, groups[core], e
    for core in range(2):
        for e in range(chips):
            for d in range(1, n_tok):
                yield d, 2 * e + core, groups[2 + core], e * (n_tok - 1) + d - 1


def gram_of(resid_cols, n_tok, n_hid):
    chips = n_hid // 2
    ntok, width = resid_cols.shape
    line = jnp.stack([swap(resid_cols, "tok", n_tok, d) for d in range(1, n_tok)])
    plane = jnp.stack([resid_cols] + [swap(resid_cols, "hid", n_hid, 2 * e) for e in range(1, chips)])
    plane_far = swap(plane, "hid", n_hid, 1)
    lines = jnp.concatenate([line] + [swap(line, "hid", n_hid, 2 * e) for e in range(1, chips)], axis=0)
    lines_far = swap(lines, "hid", n_hid, 1)
    vmem = pl.BlockSpec(memory_space=pltpu.VMEM)
    blocks = n_tok * n_hid
    return pl.pallas_call(
        functools.partial(gram_kernel, n_hid, n_tok, ntok),
        out_shape=jax.ShapeDtypeStruct((width, width * blocks), F32),
        in_specs=[vmem] * 5,
        out_specs=pl.BlockSpec(memory_space=pl.ANY),
        scratch_shapes=[pltpu.VMEM((blocks, width, width), F32), pltpu.SemaphoreType.DMA((blocks,))],
        compiler_params=pltpu.CompilerParams(vmem_limit_bytes=32 * 1024 * 1024),
        cost_estimate=pl.CostEstimate(
            flops=2 * ntok * width * width * blocks,
            bytes_accessed=4 * width * width * blocks,
            transcendentals=0,
        ),
        name="gram",
    )(resid_cols, plane, plane_far, lines, lines_far)


def on_device(n_tok, n_hid, resid_in, norm_gain, gate_weight, up_weight, down_weight, labels):
    z = lax.axis_index("tok")
    h = lax.axis_index("hid")
    core = h % 2
    chip = h // 2
    chips = n_hid // 2

    x = gather_tokens(resid_in, h, n_hid)
    ntok, block = x.shape
    half = ntok // 2
    total_sq = jnp.sum(x * x, axis=1, keepdims=True)
    d = 1
    while d < n_tok:
        total_sq = total_sq + swap(total_sq, "tok", n_tok, d)
        d *= 2
    scale_rows = lax.rsqrt(total_sq / float(D) + 1e-05)
    lhs = (x * norm_gain[None, :]).astype(BF16)

    shard_ff = gate_weight.shape[1]
    count = 4
    wide = shard_ff // count
    parts = []
    for k in range(count):
        cols = slice(k * wide, (k + 1) * wide)
        weights = jnp.concatenate([gate_weight[:, cols], up_weight[:, cols]], axis=1)
        parts.append(jnp.dot(lhs, weights, preferred_element_type=F32).astype(BF16))

    first, second = slice(0, half), slice(half, ntok)
    down_line, up_line = (lambda j: n_tok - 1 - j), (lambda j: j)
    sums_a = chain_sums(parts, first, n_tok - 1 - z, n_tok, down_line)
    sums_b = chain_sums(parts, second, z, n_tok, up_line)

    def hidden_of(sums, scale):
        both = sums * scale
        return (jax.nn.silu(both[:, :wide]) * both[:, wide:]).astype(BF16)

    hidden_a = chain_copies([hidden_of(s, scale_rows[first]) for s in sums_a], z, n_tok, up_line)
    hidden_b = chain_copies([hidden_of(s, scale_rows[second]) for s in sums_b], n_tok - 1 - z, n_tok, down_line)

    partial_out = None
    for k in range(count):
        rows = jnp.concatenate([hidden_a[k], hidden_b[k]], axis=0)
        term = jnp.dot(rows, down_weight[k * wide:(k + 1) * wide], preferred_element_type=F32)
        partial_out = term if partial_out is None else partial_out + term

    panel = block // n_hid
    by_panel = partial_out.reshape(ntok, chips, 2, panel)
    mine = jnp.where(core == 0, by_panel[:, :, 0], by_panel[:, :, 1]).reshape(ntok, chips * panel)
    other = jnp.where(core == 0, by_panel[:, :, 1], by_panel[:, :, 0]).reshape(ntok, chips * panel)
    chip_sum = mine + swap(other.astype(BF16), "hid", n_hid, 1).astype(F32)

    def panel_for(mask):
        return lax.dynamic_slice_in_dim(chip_sum, (chip ^ mask) * panel, panel, 1)

    summed = panel_for(0)
    for e in range(1, chips):
        summed = summed + swap(panel_for(e).astype(BF16), "hid", n_hid, 2 * e).astype(F32)
    x_cols = lax.dynamic_slice_in_dim(x, h * panel, panel, 1)
    resid_cols = (x_cols + summed).astype(BF16)

    if panel % 128 == 0:
        gram = gram_of(resid_cols, n_tok, n_hid)
    else:
        everyone = lax.all_gather(resid_cols, ("tok", "hid"), axis=1, tiled=True)
        gram = lax.dot_general(
            resid_cols, everyone, (((0,), (0,)), ((), ())), preferred_element_type=F32
        ) / float(ntok)

    onehot = (labels[:, None] == jnp.arange(CLASSES, dtype=jnp.int32)[None, :]).astype(BF16)
    counts = jnp.sum(onehot.astype(F32), axis=0)
    class_sums = lax.dot_general(
        resid_cols, onehot, (((0,), (0,)), ((), ())), preferred_element_type=F32
    )
    cross = class_sums / jnp.maximum(counts, 1.0)[None, :]
    return (gram, cross)


def solution(mesh):
    return jax.shard_map(
        functools.partial(on_device, mesh.shape["tok"], mesh.shape["hid"]),
        mesh=mesh,
        in_specs=(
            P("hid", "tok"),
            P("tok"),
            P("tok", "hid"),
            P("tok", "hid"),
            P("hid", "tok"),
            P(),
        ),
        out_specs=(P(("tok", "hid"), None), P(("tok", "hid"), None)),
        check_vma=False,
    )
```

```python
import functools
import jax
import jax.numpy as jnp
from jax import lax
from jax.experimental import pallas as pl
from jax.experimental.pallas import tpu as pltpu
from jax.sharding import PartitionSpec as P

D = 8192
CLASSES = 64
BF16 = jnp.bfloat16
F32 = jnp.float32


def swap(value, axis, size, mask):
    return lax.ppermute(value, axis, [(i, i ^ mask) for i in range(size)])


def gather_tokens(own, h, n_hid):
    chips = n_hid // 2
    rows = own.shape[0]
    near = [own] + [swap(own, "hid", n_hid, 2 * e) for e in range(1, chips)]
    near = jnp.concatenate(near, axis=0)
    far = swap(near, "hid", n_hid, 1)
    both = jnp.concatenate([near, far], axis=0)
    ntok = both.shape[0]
    place = jnp.arange(ntok, dtype=jnp.int32)
    slot = place // rows
    owner = h ^ (2 * (slot % chips) + slot // chips)
    token = owner * rows + place % rows
    order = (jnp.arange(ntok, dtype=jnp.int32)[:, None] == token[None, :]).astype(BF16)
    return jnp.dot(order, both, preferred_element_type=F32)


def tile_of(width):
    for tile in (256, 128):
        if width % tile == 0:
            return tile
    return width


def gate_up_kernel(lhs_ref, gate_ref, up_ref, out_ref):
    tile = gate_ref.shape[1]
    lhs = lhs_ref[...]
    out_ref[:, :tile] = jnp.dot(lhs, gate_ref[...], preferred_element_type=F32).astype(BF16)
    out_ref[:, tile:] = jnp.dot(lhs, up_ref[...], preferred_element_type=F32).astype(BF16)


def gate_up(lhs, gate_weight, up_weight, start, width, tile):
    ntok, depth = lhs.shape
    at = start // tile
    weight = pl.BlockSpec((depth, tile), lambda i: (0, at + i))
    return pl.pallas_call(
        gate_up_kernel,
        grid=(width // tile,),
        out_shape=jax.ShapeDtypeStruct((ntok, 2 * width), BF16),
        in_specs=[pl.BlockSpec((ntok, depth), lambda i: (0, 0)), weight, weight],
        out_specs=pl.BlockSpec((ntok, 2 * tile), lambda i: (0, i)),
        compiler_params=pltpu.CompilerParams(vmem_limit_bytes=24 * 1024 * 1024),
        cost_estimate=pl.CostEstimate(
            flops=4 * ntok * depth * width, bytes_accessed=4 * depth * width, transcendentals=0
        ),
        name="gate_up",
    )(lhs, gate_weight, up_weight)


def down_kernel(order_ref, lhs_ref, weight_ref, out_ref):
    out_ref[...] = jnp.dot(lhs_ref[...], weight_ref[...], preferred_element_type=F32).astype(out_ref.dtype)


def down(hidden, weight, order, panel, kind):
    ntok, depth = hidden.shape
    count = order.shape[0]
    return pl.pallas_call(
        down_kernel,
        grid_spec=pltpu.PrefetchScalarGridSpec(
            num_scalar_prefetch=1,
            grid=(count,),
            in_specs=[
                pl.BlockSpec((ntok, depth), lambda i, order: (0, 0)),
                pl.BlockSpec((depth, panel), lambda i, order: (0, order[i])),
            ],
            out_specs=pl.BlockSpec((None, ntok, panel), lambda i, order: (i, 0, 0)),
        ),
        out_shape=jax.ShapeDtypeStruct((count, ntok, panel), kind),
        compiler_params=pltpu.CompilerParams(vmem_limit_bytes=24 * 1024 * 1024),
        cost_estimate=pl.CostEstimate(
            flops=2 * ntok * depth * panel * count, bytes_accessed=2 * depth * panel * count, transcendentals=0
        ),
        name="down",
    )(order, hidden, weight)


def gram_kernel(core, n_hid, n_tok, ntok, own_ref, *refs):
    chips = n_hid // 2
    stacks, (out_ref, tiles, sems) = refs[:chips], refs[-3:]
    z = lax.axis_index("tok")
    h = lax.axis_index("hid")
    width = own_ref.shape[1]
    left = own_ref[...].T
    copies = []
    for e in range(chips):
        for d in range(n_tok):
            number = e * n_tok + d
            tiles[number] = jnp.dot(left, stacks[e][d], preferred_element_type=F32) * (1.0 / ntok)
            column = ((z ^ d) * n_hid + (h ^ (2 * e + core))) * width
            copy = pltpu.make_async_copy(
                tiles.at[number], out_ref.at[:, pl.ds(pl.multiple_of(column, width), width)], sems.at[number]
            )
            copy.start()
            copies.append(copy)
    for copy in copies:
        copy.wait()


def gram_part(resid_cols, stacks, core, n_tok, n_hid, before):
    ntok, width = resid_cols.shape
    blocks = n_tok * n_hid
    vmem = pl.BlockSpec(memory_space=pltpu.VMEM)
    anywhere = pl.BlockSpec(memory_space=pl.ANY)
    operands = [resid_cols, *stacks] + ([] if before is None else [before])
    return pl.pallas_call(
        functools.partial(gram_kernel, core, n_hid, n_tok, ntok),
        out_shape=jax.ShapeDtypeStruct((width, width * blocks), F32),
        in_specs=[vmem] * (1 + len(stacks)) + ([] if before is None else [anywhere]),
        out_specs=anywhere,
        input_output_aliases={} if before is None else {1 + len(stacks): 0},
        scratch_shapes=[pltpu.VMEM((blocks // 2, width, width), F32), pltpu.SemaphoreType.DMA((blocks // 2,))],
        compiler_params=pltpu.CompilerParams(vmem_limit_bytes=24 * 1024 * 1024),
        cost_estimate=pl.CostEstimate(
            flops=ntok * width * width * blocks, bytes_accessed=2 * width * width * blocks, transcendentals=0
        ),
        name="gram",
    )(*operands)


def gram_of(resid_cols, n_tok, n_hid):
    chips = n_hid // 2
    line = jnp.stack([resid_cols] + [swap(resid_cols, "tok", n_tok, d) for d in range(1, n_tok)])
    stacks = [line] + [swap(line, "hid", n_hid, 2 * e) for e in range(1, chips)]
    first_far = swap(line, "hid", n_hid, 1)
    rest_far = swap(jnp.stack(stacks[1:]), "hid", n_hid, 1)
    near = gram_part(resid_cols, stacks, 0, n_tok, n_hid, None)
    far = [first_far] + [rest_far[e - 1] for e in range(1, chips)]
    return gram_part(resid_cols, far, 1, n_tok, n_hid, near)


def on_device(n_tok, n_hid, resid_in, norm_gain, gate_weight, up_weight, down_weight, labels):
    h = lax.axis_index("hid")
    chips = n_hid // 2

    x = gather_tokens(resid_in, h, n_hid)
    ntok, block = x.shape
    total_sq = jnp.sum(x * x, axis=1, keepdims=True)
    d = 1
    while d < n_tok:
        total_sq = total_sq + swap(total_sq, "tok", n_tok, d)
        d *= 2
    scale_rows = lax.rsqrt(total_sq / float(D) + 1e-05)
    rows = ntok // n_tok
    own_scale = lax.dynamic_slice_in_dim(scale_rows, lax.axis_index("tok") * rows, rows, 0)
    lhs = (x * norm_gain[None, :]).astype(BF16)

    shard_ff = gate_weight.shape[1]
    tile = tile_of(shard_ff)
    count = 2 if shard_ff % (2 * tile) == 0 else 1
    wide = shard_ff // count
    hidden = []
    for k in range(count):
        pair = gate_up(lhs, gate_weight, up_weight, k * wide, wide, tile)
        sums = lax.psum_scatter(pair, "tok", scatter_dimension=0, tiled=True).astype(F32) * own_scale
        pieces = [
            jax.nn.silu(sums[:, at:at + tile]) * sums[:, at + tile:at + 2 * tile]
            for at in range(0, 2 * wide, 2 * tile)
        ]
        mine = jnp.concatenate(pieces, axis=1).astype(BF16)
        hidden.append(lax.all_gather(mine, "tok", axis=0, tiled=True))
    hidden = jnp.concatenate(hidden, axis=1)

    panel = block // n_hid
    x_cols = lax.dynamic_slice_in_dim(x, h * panel, panel, 1)
    if panel % 128 == 0:
        near_order = jnp.stack([h ^ (2 * e) for e in range(chips)]).astype(jnp.int32)
        other = down(hidden, down_weight, near_order ^ 1, panel, BF16)
        swapped = swap(other, "hid", n_hid, 1)
        mine = down(hidden, down_weight, near_order, panel, F32)
        chip_sum = mine + swapped.astype(F32)
        summed = chip_sum[0]
        for e in range(1, chips):
            summed = summed + swap(chip_sum[e].astype(BF16), "hid", n_hid, 2 * e).astype(F32)
        resid_cols = (x_cols + summed).astype(BF16)
        gram = gram_of(resid_cols, n_tok, n_hid)
    else:
        partial_out = jnp.dot(hidden, down_weight, preferred_element_type=F32).astype(BF16)
        summed = lax.psum_scatter(partial_out, "hid", scatter_dimension=1, tiled=True).astype(F32)
        resid_cols = (x_cols + summed).astype(BF16)
        everyone = lax.all_gather(resid_cols, ("tok", "hid"), axis=1, tiled=True)
        gram = lax.dot_general(
            resid_cols, everyone, (((0,), (0,)), ((), ())), preferred_element_type=F32
        ) / float(ntok)

    onehot = (labels[:, None] == jnp.arange(CLASSES, dtype=jnp.int32)[None, :]).astype(BF16)
    counts = jnp.sum(onehot.astype(F32), axis=0)
    class_sums = lax.dot_general(
        resid_cols, onehot, (((0,), (0,)), ((), ())), preferred_element_type=F32
    )
    cross = class_sums / jnp.maximum(counts, 1.0)[None, :]
    return (gram, cross)


def solution(mesh):
    return jax.shard_map(
        functools.partial(on_device, mesh.shape["tok"], mesh.shape["hid"]),
        mesh=mesh,
        in_specs=(
            P("hid", "tok"),
            P("tok"),
            P("tok", "hid"),
            P("tok", "hid"),
            P("hid", "tok"),
            P(),
        ),
        out_specs=(P(("tok", "hid"), None), P(("tok", "hid"), None)),
        check_vma=False,
    )
```

```python
import functools
import jax
import jax.numpy as jnp
from jax import lax
from jax.experimental import pallas as pl
from jax.experimental.pallas import tpu as pltpu
from jax.sharding import PartitionSpec as P

D = 8192
CLASSES = 64
BF16 = jnp.bfloat16
F32 = jnp.float32
STREAM = 52 * 1024 * 1024
SMALL = 16 * 1024 * 1024
WHOLE = pl.BlockSpec(memory_space=pltpu.VMEM)
ANYWHERE = pl.BlockSpec(memory_space=pl.ANY)


def swap(value, axis, size, mask):
    return lax.ppermute(value, axis, [(i, i ^ mask) for i in range(size)])


def params(limit):
    return pltpu.CompilerParams(vmem_limit_bytes=limit)


def cost(flops, bytes_accessed):
    return pl.CostEstimate(flops=flops, bytes_accessed=bytes_accessed, transcendentals=0)


def tile_of(width):
    for tile in (256, 128):
        if width % tile == 0:
            return tile
    return width


def tokens_kernel(chips, panel, *refs):
    near, (far, gain, lhs, cols, squares, x) = refs[:chips], refs[chips:]
    h = lax.axis_index("hid")
    rows = near[0].shape[0]
    for e in range(chips):
        for core, block in ((0, near[e][...]), (1, far[e * rows:(e + 1) * rows, :])):
            at = pl.multiple_of((h ^ (2 * e + core)) * rows, rows)
            x[pl.ds(at, rows), :] = block
    values = x[...].astype(F32)
    lhs[...] = (values * gain[...]).astype(BF16)
    squares[...] = jnp.sum(values * values, axis=1, keepdims=True)
    cols[...] = x[:, pl.ds(pl.multiple_of(h * panel, panel), panel)].astype(F32)


def gather_tokens(own, gain, n_hid):
    chips = n_hid // 2
    rows, block = own.shape
    ntok, panel = rows * n_hid, block // n_hid
    near = [own] + [swap(own, "hid", n_hid, 2 * e) for e in range(1, chips)]
    far = swap(jnp.concatenate(near, axis=0), "hid", n_hid, 1)
    if panel % 128 == 0:
        return pl.pallas_call(
            functools.partial(tokens_kernel, chips, panel),
            out_shape=(
                jax.ShapeDtypeStruct((ntok, block), BF16),
                jax.ShapeDtypeStruct((ntok, panel), F32),
                jax.ShapeDtypeStruct((ntok, 1), F32),
            ),
            in_specs=[WHOLE] * (chips + 2),
            out_specs=(WHOLE, WHOLE, WHOLE),
            scratch_shapes=[pltpu.VMEM((ntok, block), BF16)],
            compiler_params=params(SMALL),
            cost_estimate=cost(4 * ntok * block, 4 * ntok * block),
            name="tokens",
        )(*near, far, gain[None, :])
    h = lax.axis_index("hid")
    both = jnp.concatenate(near + [far], axis=0)
    place = jnp.arange(ntok, dtype=jnp.int32)
    slot = place // rows
    token = (h ^ (2 * (slot % chips) + slot // chips)) * rows + place % rows
    order = (place[:, None] == token[None, :]).astype(BF16)
    x = jnp.dot(order, both, preferred_element_type=F32)
    cols = lax.dynamic_slice_in_dim(x, h * panel, panel, 1)
    return (x * gain[None, :]).astype(BF16), cols, jnp.sum(x * x, axis=1, keepdims=True)


def gate_up_kernel(lhs_ref, gate_ref, up_ref, *refs):
    outs, both = refs[:-1], refs[-1]
    tile = gate_ref.shape[1]
    lhs = lhs_ref[...]
    both[:, :tile] = jnp.dot(lhs, gate_ref[...], preferred_element_type=F32)
    both[:, tile:] = jnp.dot(lhs, up_ref[...], preferred_element_type=F32)
    rows = outs[0].shape[0]
    for d, out in enumerate(outs):
        at = pl.multiple_of((lax.axis_index("tok") ^ d) * rows, rows) if len(outs) > 1 else 0
        out[...] = both[pl.ds(at, rows), :].astype(BF16)


def gate_up(lhs, gate_weight, up_weight, start, width, tile, blocks):
    ntok, depth = lhs.shape
    at = start // tile
    weight = pl.BlockSpec((depth, tile), lambda i: (0, at + i))
    return pl.pallas_call(
        gate_up_kernel,
        grid=(width // tile,),
        out_shape=[jax.ShapeDtypeStruct((ntok // blocks, 2 * width), BF16)] * blocks,
        in_specs=[pl.BlockSpec((ntok, depth), lambda i: (0, 0)), weight, weight],
        out_specs=[pl.BlockSpec((ntok // blocks, 2 * tile), lambda i: (0, i))] * blocks,
        scratch_shapes=[pltpu.VMEM((ntok, 2 * tile), F32)],
        compiler_params=params(STREAM),
        cost_estimate=cost(4 * ntok * depth * width, 4 * depth * width),
        name="gate_up",
    )(lhs, gate_weight, up_weight)


def copy_kernel(value_ref, after_ref, out_ref):
    out_ref[...] = value_ref[...]


def copy_after(value, after):
    return pl.pallas_call(
        copy_kernel,
        out_shape=jax.ShapeDtypeStruct(value.shape, value.dtype),
        in_specs=[WHOLE, ANYWHERE],
        out_specs=WHOLE,
        compiler_params=params(SMALL),
        cost_estimate=cost(0, 4 * value.size),
        name="copy",
    )(value, after)


def line_terms(mine, n_tok, after):
    def plus(one, two):
        return (one.astype(F32) + two.astype(F32)).astype(BF16)

    inward, middle = [(0, 1), (3, 2)], [(1, 2), (2, 1)]
    first = mine[3] if after is None else copy_after(mine[3], after)
    far_in = lax.ppermute(first, "tok", inward)
    far_over = lax.ppermute(plus(mine[2], far_in), "tok", middle)
    near_in = lax.ppermute(mine[2], "tok", inward)
    near_over = lax.ppermute(plus(mine[3], near_in), "tok", middle)
    last = swap(plus(mine[1], far_over), "tok", n_tok, 1)
    return last, near_over, far_in


def hidden_kernel(tile, own_ref, one_ref, two_ref, scale_ref, out_ref):
    scale = scale_ref[...]

    def total(at):
        cols = slice(at, at + tile)
        return (
            own_ref[:, cols].astype(F32) + one_ref[:, cols].astype(F32) + two_ref[:, cols].astype(F32)
        ) * scale

    for at in range(0, out_ref.shape[1], tile):
        gate, up = total(2 * at), total(2 * at + tile)
        out_ref[:, at:at + tile] = (jax.nn.silu(gate) * up).astype(BF16)


def hidden_rows(own, one, two, scale, tile):
    rows, width = one.shape
    return pl.pallas_call(
        functools.partial(hidden_kernel, tile),
        out_shape=jax.ShapeDtypeStruct((rows, width // 2), BF16),
        in_specs=[WHOLE] * 4,
        out_specs=WHOLE,
        compiler_params=params(SMALL),
        cost_estimate=cost(10 * rows * width, 8 * rows * width),
        name="hidden",
    )(own, one, two, scale)


def line_gather(own, z, n_tok):
    beside = swap(own, "tok", n_tok, 1)
    over = lax.ppermute(jnp.stack([own, beside]), "tok", [(1, 2), (2, 1)])
    out = lax.ppermute(over, "tok", [(1, 0), (2, 3)])
    inner = (z == 1) | (z == 2)
    return [own, beside, jnp.where(inner, over[1], out[0]), jnp.where(inner, over[0], out[1])]


def token_blocks(own, n_tok):
    if n_tok == 4:
        return jnp.concatenate(line_gather(own, lax.axis_index("tok"), n_tok), axis=0)
    return lax.all_gather(own, "tok", axis=0, tiled=True)


def down_kernel(order_ref, lhs_ref, weight_ref, *refs):
    total = jnp.dot(lhs_ref[...], weight_ref[...], preferred_element_type=F32)
    if len(refs) == 2:
        total = total + refs[0][...]
    refs[-1][...] = total.astype(refs[-1].dtype)


def down(hidden, weight, order, panel, kind, chunk, before, skip=0):
    ntok, depth = hidden.shape
    count = order.shape[0]
    each = pl.BlockSpec((None, ntok, panel), lambda i, order: (i, 0, 0))
    added = [] if before is None else [before]
    return pl.pallas_call(
        down_kernel,
        grid_spec=pltpu.PrefetchScalarGridSpec(
            num_scalar_prefetch=1,
            grid=(count,),
            in_specs=[
                pl.BlockSpec((ntok, depth), lambda i, order: (0, 0)),
                pl.BlockSpec((depth, panel), lambda i, order: (chunk, order[i])),
            ] + [pl.BlockSpec((None, ntok, panel), lambda i, order: (i + skip, 0, 0))] * len(added),
            out_specs=each,
        ),
        out_shape=jax.ShapeDtypeStruct((count, ntok, panel), kind),
        compiler_params=params(STREAM),
        cost_estimate=cost(2 * ntok * depth * panel * count, 2 * depth * panel * count),
        name="down",
    )(order, hidden, weight, *added)


def gram_kernel(masks, n_hid, ntok, own_ref, *refs):
    stacks, (out_ref, tiles, sems) = refs[:len(masks)], refs[-3:]
    z = lax.axis_index("tok")
    h = lax.axis_index("hid")
    width = own_ref.shape[1]
    left = own_ref[...].T
    copies = []
    for stack, here in zip(stacks, masks):
        for at, mask in enumerate(here):
            for d in range(stack.shape[1]):
                number = len(copies)
                tiles[number] = jnp.dot(left, stack[at, d], preferred_element_type=F32) * (1.0 / ntok)
                column = ((z ^ d) * n_hid + (h ^ mask)) * width
                copy = pltpu.make_async_copy(
                    tiles.at[number], out_ref.at[:, pl.ds(pl.multiple_of(column, width), width)], sems.at[number]
                )
                copy.start()
                copies.append(copy)
    for copy in copies:
        copy.wait()


def gram_part(resid_cols, stacks, masks, n_tok, n_hid, before):
    ntok, width = resid_cols.shape
    here = n_tok * sum(len(m) for m in masks)
    operands = [resid_cols, *stacks] + ([] if before is None else [before])
    return pl.pallas_call(
        functools.partial(gram_kernel, masks, n_hid, ntok),
        out_shape=jax.ShapeDtypeStruct((width, width * n_tok * n_hid), F32),
        in_specs=[WHOLE] * (1 + len(stacks)) + ([] if before is None else [ANYWHERE]),
        out_specs=ANYWHERE,
        input_output_aliases={} if before is None else {1 + len(stacks): 0},
        scratch_shapes=[pltpu.VMEM((here, width, width), F32), pltpu.SemaphoreType.DMA((here,))],
        compiler_params=params(SMALL),
        cost_estimate=cost(2 * ntok * width * width * here, 4 * width * width * here),
        name="gram",
    )(*operands)


def gram_of(resid_cols, n_tok, n_hid):
    masks = range(2, n_hid, 2)
    line = jnp.stack([resid_cols] + [swap(resid_cols, "tok", n_tok, d) for d in range(1, n_tok)])
    others = [swap(line, "hid", n_hid, mask) for mask in masks]
    line_far = swap(line, "hid", n_hid, 1)
    others_far = swap(jnp.stack(others), "hid", n_hid, 1)
    gram = gram_part(resid_cols, [line[None], line_far[None]], [[0], [1]], n_tok, n_hid, None)
    gram = gram_part(resid_cols, [o[None] for o in others], [[m] for m in masks], n_tok, n_hid, gram)
    return gram_part(resid_cols, [others_far], [[m + 1 for m in masks]], n_tok, n_hid, gram)


def on_device(n_tok, n_hid, resid_in, norm_gain, gate_weight, up_weight, down_weight, labels):
    z = lax.axis_index("tok")
    h = lax.axis_index("hid")
    chips = n_hid // 2

    lhs, x_cols, total_sq = gather_tokens(resid_in, norm_gain, n_hid)
    ntok, block = lhs.shape
    d = 1
    while d < n_tok:
        total_sq = total_sq + swap(total_sq, "tok", n_tok, d)
        d *= 2
    rows = ntok // n_tok
    own_scale = lax.rsqrt(lax.dynamic_slice_in_dim(total_sq, z * rows, rows, 0) / float(D) + 1e-05)

    shard_ff = gate_weight.shape[1]
    tile = tile_of(shard_ff)
    count = 2 if shard_ff % (2 * tile) == 0 else 1
    wide = shard_ff // count
    hidden, after = [], None
    for k in range(count):
        pair = gate_up(lhs, gate_weight, up_weight, k * wide, wide, tile, 4 if n_tok == 4 else 1)
        if n_tok == 4:
            one, two, after = line_terms(pair, n_tok, after)
            own = hidden_rows(pair[0], one, two, own_scale, tile)
        else:
            sums = lax.psum_scatter(pair[0], "tok", scatter_dimension=0, tiled=True).astype(F32) * own_scale
            pieces = [
                jax.nn.silu(sums[:, at:at + tile]) * sums[:, at + tile:at + 2 * tile]
                for at in range(0, 2 * wide, 2 * tile)
            ]
            own = jnp.concatenate(pieces, axis=1).astype(BF16)
        hidden.append(token_blocks(own, n_tok))

    panel = block // n_hid
    if n_tok == 4 and panel % 128 == 0:
        order = jnp.stack([h ^ m for m in [2 * e + 1 for e in range(chips)] + [2 * e for e in range(chips)]])
        order = order.astype(jnp.int32)
        before = None
        for k in range(count - 1):
            before = down(hidden[k], down_weight, order, panel, F32, k, before)
        other = down(hidden[-1], down_weight, order[:chips], panel, BF16, count - 1, before)
        mine = down(hidden[-1], down_weight, order[chips:], panel, F32, count - 1, before, chips)
        chip_sum = mine + swap(other, "hid", n_hid, 1).astype(F32)
        summed = chip_sum[0]
        for e in range(1, chips):
            summed = summed + swap(chip_sum[e].astype(BF16), "hid", n_hid, 2 * e).astype(F32)
        summed = jnp.concatenate(
            [lax.dynamic_slice_in_dim(summed, (z ^ d) * rows, rows, 0) for d in range(n_tok)], axis=0
        )
        resid_cols = (x_cols + summed).astype(BF16)
        gram = gram_of(resid_cols, n_tok, n_hid)
    else:
        partial_out = jnp.dot(jnp.concatenate(hidden, axis=1), down_weight, preferred_element_type=F32)
        summed = lax.psum_scatter(
            partial_out.astype(BF16), "hid", scatter_dimension=1, tiled=True
        ).astype(F32)
        if n_tok == 4:
            summed = jnp.concatenate(
                [lax.dynamic_slice_in_dim(summed, (z ^ d) * rows, rows, 0) for d in range(n_tok)], axis=0
            )
        resid_cols = (x_cols + summed).astype(BF16)
        everyone = lax.all_gather(resid_cols, ("tok", "hid"), axis=1, tiled=True)
        gram = lax.dot_general(
            resid_cols, everyone, (((0,), (0,)), ((), ())), preferred_element_type=F32
        ) / float(ntok)

    onehot = (labels[:, None] == jnp.arange(CLASSES, dtype=jnp.int32)[None, :]).astype(BF16)
    counts = jnp.sum(onehot.astype(F32), axis=0)
    class_sums = lax.dot_general(
        resid_cols, onehot, (((0,), (0,)), ((), ())), preferred_element_type=F32
    )
    cross = class_sums / jnp.maximum(counts, 1.0)[None, :]
    return (gram, cross)


def solution(mesh):
    return jax.shard_map(
        functools.partial(on_device, mesh.shape["tok"], mesh.shape["hid"]),
        mesh=mesh,
        in_specs=(
            P("hid", "tok"),
            P("tok"),
            P("tok", "hid"),
            P("tok", "hid"),
            P("hid", "tok"),
            P(),
        ),
        out_specs=(P(("tok", "hid"), None), P(("tok", "hid"), None)),
        check_vma=False,
    )
```

```python
import functools
import jax
import jax.numpy as jnp
from jax import lax
from jax.experimental import pallas as pl
from jax.experimental.pallas import tpu as pltpu
from jax.sharding import PartitionSpec as P

D = 8192
CLASSES = 64
TILE = 256
CHUNKS = 2
BF16 = jnp.bfloat16
F32 = jnp.float32
WHOLE = pl.BlockSpec(memory_space=pltpu.VMEM)
ANYWHERE = pl.BlockSpec(memory_space=pl.ANY)
INWARD, MIDDLE, OUTWARD = [(0, 1), (3, 2)], [(1, 2), (2, 1)], [(1, 0), (2, 3)]


def swap(value, axis, size, mask):
    return lax.ppermute(value, axis, [(i, i ^ mask) for i in range(size)])


def run(body, name, out_shape, operands, flops, bytes_accessed, in_specs=None, out_specs=WHOLE, **more):
    return pl.pallas_call(
        body,
        out_shape=out_shape,
        in_specs=[WHOLE] * len(operands) if in_specs is None else in_specs,
        out_specs=out_specs,
        compiler_params=pltpu.CompilerParams(vmem_limit_bytes=16 * 1024 * 1024),
        cost_estimate=pl.CostEstimate(flops=flops, bytes_accessed=bytes_accessed, transcendentals=0),
        name=name,
        **more,
    )(*operands)


def fetch(pieces, after, name):
    count = len(pieces)
    copies = []
    for number, (array, row, rows, column, columns) in enumerate(pieces):
        step = min(rows, 256)
        copies += [(number, at, step, row + at, column, columns) for at in range(0, rows, step)]

    def body(*refs):
        sources, targets, sems = refs[:count], refs[-1 - count:-1], refs[-1]
        started = []
        for sem, (number, at, step, row, column, columns) in enumerate(copies):
            copy = pltpu.make_async_copy(
                sources[number].at[pl.ds(row, step), pl.ds(column, columns)],
                targets[number].at[pl.ds(at, step), :],
                sems.at[sem],
            )
            copy.start()
            started.append(copy)
        for copy in started:
            copy.wait()

    size = sum(rows * columns * array.dtype.itemsize for array, _, rows, _, columns in pieces)
    return run(
        body, name,
        [pltpu.VMEM((rows, columns), array.dtype) for array, _, rows, _, columns in pieces],
        [pltpu.with_memory_space_constraint(piece[0], pltpu.HBM) for piece in pieces] + list(after),
        0, 2 * size,
        in_specs=[ANYWHERE] * (count + len(after)),
        out_specs=[WHOLE] * count,
        scratch_shapes=[pltpu.SemaphoreType.DMA((len(copies),))],
    )


def tokens_kernel(masks, panel, *refs):
    blocks, (gain, lhs, cols, squares, x) = refs[:len(masks)], refs[len(masks):]
    h = lax.axis_index("hid")
    rows = blocks[0].shape[0]
    for mask, block in zip(masks, blocks):
        x[pl.ds(pl.multiple_of((h ^ mask) * rows, rows), rows), :] = block[...]
    values = x[...].astype(F32)
    lhs[...] = (values * gain[...]).astype(BF16)
    squares[...] = jnp.sum(values * values, axis=1, keepdims=True)
    cols[...] = x[:, pl.ds(pl.multiple_of(h * panel, panel), panel)].astype(F32)


def gate_up_kernel(lhs_ref, gate_ref, up_ref, *refs):
    outs, both = refs[:-1], refs[-1]
    rows = outs[0].shape[0]
    z = lax.axis_index("tok")
    lhs = lhs_ref[...]
    for tile in range(gate_ref.shape[1] // TILE):
        cols = slice(tile * TILE, (tile + 1) * TILE)
        both[:, :TILE] = jnp.dot(lhs, gate_ref[:, cols], preferred_element_type=F32)
        both[:, TILE:] = jnp.dot(lhs, up_ref[:, cols], preferred_element_type=F32)
        for d, out in enumerate(outs):
            at = pl.multiple_of((z ^ d) * rows, rows)
            out[:, 2 * tile * TILE:2 * (tile + 1) * TILE] = both[pl.ds(at, rows), :].astype(BF16)


def gate_up(lhs, gate, up, n_tok):
    ntok, depth = lhs.shape
    width = gate.shape[1]
    return run(
        gate_up_kernel, "gate_up",
        [jax.ShapeDtypeStruct((ntok // n_tok, 2 * width), BF16)] * n_tok,
        [lhs, gate, up],
        4 * ntok * depth * width, 4 * depth * width,
        out_specs=[WHOLE] * n_tok,
        scratch_shapes=[pltpu.VMEM((ntok, 2 * TILE), F32)],
    )


def total_after(terms, after):
    count = len(terms)

    def body(*refs):
        total = refs[0][...]
        if count > 1:
            total = total.astype(F32)
            for ref in refs[1:count]:
                total = total + ref[...].astype(F32)
        refs[-1][...] = total.astype(BF16)

    size = terms[0].size
    return run(
        body, "total", jax.ShapeDtypeStruct(terms[0].shape, BF16), [*terms, *after],
        count * size, 2 * size * (count + 1),
        in_specs=[WHOLE] * count + [ANYWHERE] * len(after),
    )


def hidden_kernel(own_ref, one_ref, two_ref, square_ref, out_ref):
    rows = out_ref.shape[0]
    at = pl.multiple_of(lax.axis_index("tok") * rows, rows)
    scale = lax.rsqrt(square_ref[pl.ds(at, rows), :] / float(D) + 1e-05)

    def total(at):
        cols = slice(at, at + TILE)
        return (
            own_ref[:, cols].astype(F32) + one_ref[:, cols].astype(F32) + two_ref[:, cols].astype(F32)
        ) * scale

    for at in range(0, out_ref.shape[1], TILE):
        gate, up = total(2 * at), total(2 * at + TILE)
        out_ref[:, at:at + TILE] = (jax.nn.silu(gate) * up).astype(BF16)


def hidden_rows(own, one, two, squares):
    rows, width = one.shape
    return run(
        hidden_kernel, "hidden", jax.ShapeDtypeStruct((rows, width // 2), BF16),
        [own, one, two, squares], 10 * rows * width, 8 * rows * width,
    )


def down_kernel(masks, skip, panel, counts, *refs):
    blocks, refs = refs[:sum(counts)], refs[sum(counts):]
    weight, lhs, out = refs[0], refs[-1], refs[-2]
    before = refs[1] if len(refs) == 4 else None
    z = lax.axis_index("tok")
    h = lax.axis_index("hid")
    rows = blocks[0].shape[0]
    at = 0
    for d, count in enumerate(counts):
        block = blocks[at][...]
        for extra in blocks[at + 1:at + count]:
            block = block + extra[...]
        at += count
        lhs[pl.ds(pl.multiple_of((z ^ d) * rows, rows), rows), :] = block
    values = lhs[...]
    for slot, mask in enumerate(masks):
        column = pl.multiple_of((h ^ mask) * panel, panel)
        total = jnp.dot(values, weight[:, pl.ds(column, panel)], preferred_element_type=F32)
        if before is not None:
            total = total + before[skip + slot]
        out[slot] = total.astype(out.dtype)


def down(hidden, weight, masks, panel, kind, before=None, skip=0):
    blocks = [block for terms in hidden for block in terms]
    rows, depth = blocks[0].shape
    ntok = rows * len(hidden)
    counts = [len(terms) for terms in hidden]
    return run(
        functools.partial(down_kernel, masks, skip, panel, counts), "down",
        jax.ShapeDtypeStruct((len(masks), ntok, panel), kind),
        blocks + [weight] + ([] if before is None else [before]),
        2 * ntok * depth * panel * len(masks), 2 * depth * panel * len(masks),
        scratch_shapes=[pltpu.VMEM((ntok, depth), BF16)],
    )


def chip_sum_kernel(mine_ref, other_ref, own_ref, *outs):
    own_ref[...] = mine_ref[0] + other_ref[0].astype(F32)
    for e, out in enumerate(outs):
        out[...] = (mine_ref[e + 1] + other_ref[e + 1].astype(F32)).astype(BF16)


def gram_kernel(masks, n_hid, ntok, own_ref, *refs):
    stacks, (out_ref, tiles, sems) = refs[:len(masks)], refs[-3:]
    z = lax.axis_index("tok")
    h = lax.axis_index("hid")
    width = own_ref.shape[1]
    left = own_ref[...].T
    copies = []
    for mask, stack in zip(masks, stacks):
        for d in range(stack.shape[0]):
            number = len(copies)
            tiles[number] = jnp.dot(left, stack[d], preferred_element_type=F32) * (1.0 / ntok)
            column = ((z ^ d) * n_hid + (h ^ mask)) * width
            copy = pltpu.make_async_copy(
                tiles.at[number], out_ref.at[:, pl.ds(pl.multiple_of(column, width), width)], sems.at[number]
            )
            copy.start()
            copies.append(copy)
    for copy in copies:
        copy.wait()


def gram_part(resid_cols, stacks, masks, n_tok, n_hid, before):
    ntok, width = resid_cols.shape
    here = n_tok * len(stacks)
    return run(
        functools.partial(gram_kernel, masks, n_hid, ntok), "gram",
        pltpu.HBM((width, width * n_tok * n_hid), F32),
        [resid_cols, *stacks] + ([] if before is None else [before]),
        2 * ntok * width * width * here, 4 * width * width * here,
        in_specs=[WHOLE] * (1 + len(stacks)) + ([] if before is None else [ANYWHERE]),
        out_specs=ANYWHERE,
        input_output_aliases={} if before is None else {1 + len(stacks): 0},
        scratch_shapes=[pltpu.VMEM((here, width, width), F32), pltpu.SemaphoreType.DMA((here,))],
    )


def class_means(resid_cols, labels):
    onehot = (labels[:, None] == jnp.arange(CLASSES, dtype=jnp.int32)[None, :]).astype(BF16)
    counts = jnp.sum(onehot.astype(F32), axis=0)
    class_sums = lax.dot_general(
        resid_cols, onehot, (((0,), (0,)), ((), ())), preferred_element_type=F32
    )
    return class_sums / jnp.maximum(counts, 1.0)[None, :]


def on_line(n_tok, n_hid, resid_in, norm_gain, gate_weight, up_weight, down_weight, labels):
    rows, block = resid_in.shape
    ntok, panel = rows * n_hid, block // n_hid
    depth, shard_ff = gate_weight.shape
    wide = shard_ff // CHUNKS
    chip_masks = list(range(2, n_hid, 2))

    def weights(k, after):
        part = (0, depth, k * wide, wide)
        return fetch([(gate_weight, *part), (up_weight, *part)], after, "fetch_gate_up")

    near = [resid_in] + [swap(resid_in, "hid", n_hid, mask) for mask in chip_masks]
    gate, up, own_x, gain = fetch(
        [
            (gate_weight, 0, depth, 0, wide),
            (up_weight, 0, depth, 0, wide),
            (resid_in, 0, rows, 0, block),
            (norm_gain[None, :], 0, 1, 0, block),
        ],
        (), "fetch_first",
    )
    far = [near[0], total_after([near[1]], (gain,)), *near[2:]]
    far = [swap(piece, "hid", n_hid, 1) for piece in far]
    masks = [0] + chip_masks + [1] + [mask + 1 for mask in chip_masks]
    lhs, x_cols, squares = run(
        functools.partial(tokens_kernel, masks, panel), "tokens",
        (
            jax.ShapeDtypeStruct((ntok, block), BF16),
            jax.ShapeDtypeStruct((ntok, panel), F32),
            jax.ShapeDtypeStruct((ntok, 1), F32),
        ),
        [own_x, *near[1:], *far, gain],
        4 * ntok * block, 4 * ntok * block,
        out_specs=(WHOLE, WHOLE, WHOLE),
        scratch_shapes=[pltpu.VMEM((ntok, block), BF16)],
    )
    squares = sum([swap(squares, "tok", n_tok, d) for d in range(1, n_tok)], squares)

    a = gate_up(lhs, gate, up, n_tok)
    a_far = lax.ppermute(a[3], "tok", INWARD)
    a_near = lax.ppermute(a[2], "tok", INWARD)
    b = gate_up(lhs, *weights(1, (a[3],)), n_tok)
    send = total_after([a[2], a_far], ())
    a_far = lax.ppermute(send, "tok", MIDDLE)
    send = total_after([b[3]], (send,))
    b_far = lax.ppermute(send, "tok", INWARD)
    send = total_after([a[3], a_near], (send,))
    a_near = lax.ppermute(send, "tok", MIDDLE)
    send = total_after([b[2]], (send,))
    b_near = lax.ppermute(send, "tok", INWARD)
    down_a, = fetch([(down_weight, 0, wide, 0, block)], (send,), "fetch_down")
    send = total_after([a[1], a_far], (send,))
    a_last = swap(send, "tok", n_tok, 1)
    send = total_after([b[2], b_far], (send,))
    b_far = lax.ppermute(send, "tok", MIDDLE)
    down_b, = fetch([(down_weight, wide, wide, 0, block)], (send,), "fetch_down")
    send = total_after([b[3], b_near], (send,))
    b_near = lax.ppermute(send, "tok", MIDDLE)
    send = total_after([b[1], b_far], (send,))
    b_last = swap(send, "tok", n_tok, 1)

    own = hidden_rows(a[0], a_last, a_near, squares)
    beside = swap(own, "tok", n_tok, 1)
    over_own = lax.ppermute(own, "tok", MIDDLE)
    over_beside = lax.ppermute(beside, "tok", MIDDLE)
    out_own = lax.ppermute(over_own, "tok", OUTWARD)
    out_beside = lax.ppermute(over_beside, "tok", OUTWARD)
    hidden_a = [[own], [beside], [over_beside, out_own], [over_own, out_beside]]
    own = hidden_rows(b[0], b_last, b_near, squares)
    hidden_b = [[own]] + [[swap(own, "tok", n_tok, d)] for d in range(1, n_tok)]

    here = [0] + chip_masks
    there = [mask + 1 for mask in here]
    first = down(hidden_a, down_a, there + here, panel, F32)
    other = down(hidden_b, down_b, there, panel, BF16, first, 0)
    other = swap(other, "hid", n_hid, 1)
    mine = down(hidden_b, down_b, here, panel, F32, first, len(there))
    summed, *sends = run(
        chip_sum_kernel, "chip_sum",
        [jax.ShapeDtypeStruct((ntok, panel), F32)] + [jax.ShapeDtypeStruct((ntok, panel), BF16)] * len(chip_masks),
        [mine, other], mine.size, 8 * mine.size,
        out_specs=[WHOLE] * len(here),
    )
    for mask, value in zip(chip_masks, sends):
        summed = summed + swap(value, "hid", n_hid, mask).astype(F32)
    resid_cols = (x_cols + summed).astype(BF16)
    cross = class_means(resid_cols, labels)

    line = jnp.stack([resid_cols] + [swap(resid_cols, "tok", n_tok, d) for d in range(1, n_tok)])
    others = [swap(line, "hid", n_hid, mask) for mask in chip_masks]
    line_far = swap(line, "hid", n_hid, 1)
    gram = gram_part(resid_cols, [line, line_far], [0, 1], n_tok, n_hid, None)
    others_far = [swap(total_after([others[0]], (pltpu.with_memory_space_constraint(gram, pltpu.HBM),)), "hid", n_hid, 1)]
    others_far += [swap(piece, "hid", n_hid, 1) for piece in others[1:]]
    gram = gram_part(resid_cols, others, chip_masks, n_tok, n_hid, gram)
    gram = gram_part(resid_cols, others_far, [mask + 1 for mask in chip_masks], n_tok, n_hid, gram)
    return (gram, cross)


def plain(n_tok, n_hid, resid_in, norm_gain, gate_weight, up_weight, down_weight, labels):
    x = lax.all_gather(resid_in, "hid", axis=0, tiled=True).astype(F32)
    ntok, block = x.shape
    total_sq = lax.psum(jnp.sum(x * x, axis=1), "tok")
    normed = (x * lax.rsqrt(total_sq / float(D) + 1e-05)[:, None] * norm_gain[None, :]).astype(BF16)

    def summed_over_tok(weight):
        product = jnp.dot(normed, weight, preferred_element_type=F32).astype(BF16)
        return lax.psum_scatter(product, "tok", scatter_dimension=0, tiled=True).astype(F32)

    hidden = (jax.nn.silu(summed_over_tok(gate_weight)) * summed_over_tok(up_weight)).astype(BF16)
    hidden = lax.all_gather(hidden, "tok", axis=0, tiled=True)
    partial_out = jnp.dot(hidden, down_weight, preferred_element_type=F32).astype(BF16)
    summed = lax.psum_scatter(partial_out, "hid", scatter_dimension=1, tiled=True).astype(F32)
    panel = block // n_hid
    x_cols = lax.dynamic_slice_in_dim(x, lax.axis_index("hid") * panel, panel, 1)
    resid_cols = (x_cols + summed).astype(BF16)
    everyone = lax.all_gather(resid_cols, ("tok", "hid"), axis=1, tiled=True)
    gram = lax.dot_general(
        resid_cols, everyone, (((0,), (0,)), ((), ())), preferred_element_type=F32
    ) / float(ntok)
    return (gram, class_means(resid_cols, labels))


def on_device(n_tok, n_hid, resid_in, norm_gain, gate_weight, *rest):
    panel = resid_in.shape[1] // n_hid
    fits = n_tok == 4 and n_hid == 8 and panel % 128 == 0 and gate_weight.shape[1] % (CHUNKS * TILE) == 0
    body = on_line if fits else plain
    return body(n_tok, n_hid, resid_in, norm_gain, gate_weight, *rest)


def solution(mesh):
    return jax.shard_map(
        functools.partial(on_device, mesh.shape["tok"], mesh.shape["hid"]),
        mesh=mesh,
        in_specs=(
            P("hid", "tok"),
            P("tok"),
            P("tok", "hid"),
            P("tok", "hid"),
            P("hid", "tok"),
            P(),
        ),
        out_specs=(P(("tok", "hid"), None), P(("tok", "hid"), None)),
        check_vma=False,
    )
```

```python
import functools
import jax
import jax.numpy as jnp
from jax import lax
from jax.experimental import pallas as pl
from jax.experimental.pallas import tpu as pltpu
from jax.sharding import PartitionSpec as P

D = 8192
CLASSES = 64
TILE = 256
BF16 = jnp.bfloat16
F32 = jnp.float32
WHOLE = pl.BlockSpec(memory_space=pltpu.VMEM)
ANYWHERE = pl.BlockSpec(memory_space=pl.ANY)
SIDE = 128


def swap(value, axis, size, mask):
    return lax.ppermute(value, axis, [(i, i ^ mask) for i in range(size)])


def run(body, name, out_shape, operands, flops, bytes_accessed, in_specs=None, out_specs=WHOLE, **more):
    return pl.pallas_call(
        body,
        out_shape=out_shape,
        in_specs=[WHOLE] * len(operands) if in_specs is None else in_specs,
        out_specs=out_specs,
        compiler_params=pltpu.CompilerParams(vmem_limit_bytes=16 * 1024 * 1024),
        cost_estimate=pl.CostEstimate(flops=flops, bytes_accessed=bytes_accessed, transcendentals=0),
        name=name,
        **more,
    )(*operands)


def fetch(pieces, after, name):
    count = len(pieces)
    copies = []
    for number, (array, row, rows, column, columns) in enumerate(pieces):
        step = min(rows, 256)
        copies += [(number, at, step, row + at, column, columns) for at in range(0, rows, step)]

    def body(*refs):
        sources, targets, sems = refs[:count], refs[-1 - count:-1], refs[-1]
        started = []
        for sem, (number, at, step, row, column, columns) in enumerate(copies):
            copy = pltpu.make_async_copy(
                sources[number].at[pl.ds(row, step), pl.ds(column, columns)],
                targets[number].at[pl.ds(at, step), :],
                sems.at[sem],
            )
            copy.start()
            started.append(copy)
        for copy in started:
            copy.wait()

    size = sum(rows * columns * array.dtype.itemsize for array, _, rows, _, columns in pieces)
    return run(
        body, name,
        [pltpu.VMEM((rows, columns), array.dtype) for array, _, rows, _, columns in pieces],
        [pltpu.with_memory_space_constraint(piece[0], pltpu.HBM) for piece in pieces] + list(after),
        0, 0,
        in_specs=[ANYWHERE] * (count + len(after)),
        out_specs=[WHOLE] * count,
        scratch_shapes=[pltpu.SemaphoreType.DMA((len(copies),))],
    )


def tokens_kernel(masks, panel, *refs):
    blocks, gain, (lhs, cols, squares, x) = refs[:len(masks)], refs[len(masks)], refs[-4:]
    h = lax.axis_index("hid")
    rows = blocks[0].shape[0]
    for mask, block in zip(masks, blocks):
        x[pl.ds(pl.multiple_of((h ^ mask) * rows, rows), rows), :] = block[...]
    values = x[...].astype(F32)
    lhs[...] = (values * gain[...]).astype(BF16)
    squares[...] = jnp.sum(values * values, axis=1, keepdims=True)
    cols[...] = x[:, pl.ds(pl.multiple_of(h * panel, panel), panel)].astype(F32)


def split(value):
    lane = lax.broadcasted_iota(jnp.int32, (value.shape[0], SIDE), 1)
    out = jnp.zeros((value.shape[0], SIDE), F32)
    for part in range(3):
        rounded = value.astype(BF16).astype(F32)
        out = jnp.where(lane == part, rounded, out)
        value = value - rounded
    return out


def joined(parts):
    return jnp.sum(parts.astype(F32), axis=1, keepdims=True)


def gate_up_kernel(lhs_ref, gate_ref, up_ref, *refs):
    send_ref, keep_ref, both, side = refs[-4:]
    places = ((keep_ref, 0), (send_ref, 0), (keep_ref, 1), (send_ref, 1))
    rows = send_ref.shape[1]
    z = lax.axis_index("tok")
    lhs = lhs_ref[...]

    def hand_out(source, start, width):
        for d, (out, slot) in enumerate(places):
            at = pl.multiple_of((z ^ d) * rows, rows)
            out[slot, :, start:start + width] = source[pl.ds(at, rows), :].astype(BF16)

    for tile in range(gate_ref.shape[1] // TILE):
        cols = slice(tile * TILE, (tile + 1) * TILE)
        both[:, :TILE] = jnp.dot(lhs, gate_ref[:, cols], preferred_element_type=F32)
        both[:, TILE:] = jnp.dot(lhs, up_ref[:, cols], preferred_element_type=F32)
        hand_out(both, 2 * tile * TILE, 2 * TILE)
    if send_ref.shape[2] > 2 * gate_ref.shape[1]:
        side[...] = split(refs[0][...])
        hand_out(side, 2 * gate_ref.shape[1], SIDE)


def gate_up(lhs, gate, up, squares, n_tok, after=()):
    ntok, depth = lhs.shape
    width = gate.shape[1]
    rows = ntok // n_tok
    extra = [] if squares is None else [squares]
    shape = jax.ShapeDtypeStruct((2, rows, 2 * width + SIDE * len(extra)), BF16)
    return run(
        gate_up_kernel, "gate_up", [shape, shape], [lhs, gate, up, *extra, *after],
        0, 0,
        in_specs=[WHOLE] * (3 + len(extra)) + [ANYWHERE] * len(after),
        out_specs=[WHOLE] * 2,
        scratch_shapes=[pltpu.VMEM((ntok, 2 * TILE), F32), pltpu.VMEM((ntok, SIDE), F32)],
    )


def pair_total(keep, got, main, after):
    def body(keep_ref, got_ref, *refs):
        out = refs[-1]
        out[:, :main] = (keep_ref[1, :, :main].astype(F32) + got_ref[1, :, :main].astype(F32)).astype(BF16)
        if out.shape[1] > main:
            out[:, main:] = split(joined(keep_ref[1, :, main:]) + joined(got_ref[1, :, main:])).astype(BF16)

    size = keep.size // 2
    return run(
        body, "pair_total", jax.ShapeDtypeStruct(keep.shape[1:], BF16), [keep, got, *after],
        size, 6 * size, in_specs=[WHOLE] * 2 + [ANYWHERE] * len(after),
    )


def copy_after(value, after):
    def body(value_ref, *refs):
        refs[-1][...] = value_ref[...]

    return run(
        body, "copy", jax.ShapeDtypeStruct(value.shape, value.dtype), [value, *after],
        0, 4 * value.size, in_specs=[WHOLE] + [ANYWHERE] * len(after),
    )


def stack_after(blocks, after):
    stacks = [block if block.ndim == 3 else block[None] for block in blocks]
    total = sum(stack.shape[0] for stack in stacks)

    def body(*refs):
        at = 0
        for ref in refs[:len(stacks)]:
            refs[-1][at:at + ref.shape[0]] = ref[...]
            at += ref.shape[0]

    shape = jax.ShapeDtypeStruct((total, *stacks[0].shape[1:]), blocks[0].dtype)
    return run(
        body, "stack", shape, [*stacks, *after], 0, 4 * sum(stack.size for stack in stacks),
        in_specs=[WHOLE] * len(stacks) + [ANYWHERE] * len(after),
    )


def hidden_rows(chunks, widths, scale, after):
    rows = chunks[0][0].shape[1]
    given = [] if scale is None else [scale]

    def body(*refs):
        out_ref, scale_ref = refs[-2:]
        keep_ref, got_ref, over_ref = refs[:3]
        if scale is None:
            tail = slice(2 * widths[0], 2 * widths[0] + SIDE)
            squares = joined(keep_ref[0, :, tail]) + joined(got_ref[0, :, tail]) + joined(over_ref[:, tail])
            factor = lax.rsqrt(squares / float(D) + 1e-05)
        else:
            factor = refs[3 * len(chunks)][...]
        scale_ref[...] = factor
        start = 0
        for k, width in enumerate(widths):
            keep_ref, got_ref, over_ref = refs[3 * k:3 * k + 3]

            def total(at):
                cols = slice(at, at + TILE)
                return (
                    keep_ref[0, :, cols].astype(F32) + got_ref[0, :, cols].astype(F32) + over_ref[:, cols].astype(F32)
                ) * factor

            for at in range(0, width, TILE):
                gate, up = total(2 * at), total(2 * at + TILE)
                out_ref[:, start + at:start + at + TILE] = (jax.nn.silu(gate) * up).astype(BF16)
            start += width

    size = rows * sum(widths)
    return run(
        body, "hidden",
        [jax.ShapeDtypeStruct((rows, sum(widths)), BF16), jax.ShapeDtypeStruct((rows, 1), F32)],
        [part for chunk in chunks for part in chunk] + given + list(after), 20 * size, 14 * size,
        in_specs=[WHOLE] * (3 * len(chunks) + len(given)) + [ANYWHERE] * len(after),
        out_specs=[WHOLE] * 2,
    )


def down_kernel(masks, skip, panel, n_blocks, *refs):
    blocks, weight, lhs, out = refs[:n_blocks], refs[n_blocks], refs[-1], refs[-2]
    before = refs[n_blocks + 1] if len(refs) == n_blocks + 4 else None
    z = lax.axis_index("tok")
    h = lax.axis_index("hid")
    rows = blocks[0].shape[0]
    for d, block in enumerate(blocks):
        lhs[pl.ds(pl.multiple_of((z ^ d) * rows, rows), rows), :] = block[...]
    values = lhs[...]
    for slot, mask in enumerate(masks):
        column = pl.multiple_of((h ^ mask) * panel, panel)
        total = jnp.dot(values, weight[:, pl.ds(column, panel)], preferred_element_type=F32)
        if before is not None:
            total = total + before[skip + slot]
        out[slot] = total.astype(out.dtype)


def down(blocks, weight, masks, panel, kind, before=None, skip=0):
    rows, depth = blocks[0].shape
    ntok = rows * len(blocks)
    return run(
        functools.partial(down_kernel, masks, skip, panel, len(blocks)), "down",
        jax.ShapeDtypeStruct((len(masks), ntok, panel), kind),
        [*blocks, weight] + ([] if before is None else [before]),
        2 * ntok * depth * panel * len(masks), 2 * depth * panel * len(masks),
        scratch_shapes=[pltpu.VMEM((ntok, depth), BF16)],
    )


def chip_sum_kernel(mine_ref, other_ref, own_ref, *outs):
    own_ref[...] = mine_ref[0] + other_ref[0].astype(F32)
    for e, out in enumerate(outs):
        out[...] = (mine_ref[e + 1] + other_ref[e + 1].astype(F32)).astype(BF16)


def gram_kernel(slots, n_hid, ntok, classes, own_ref, *refs):
    stacks = refs[:len(slots)]
    outs, (tiles, sems) = refs[:-2], refs[-2:]
    out_ref = outs[-2] if classes else outs[-1]
    z = lax.axis_index("tok")
    h = lax.axis_index("hid")
    width = own_ref.shape[1]
    left = own_ref[...].T
    copies = []
    for stack, places in zip(stacks, slots):
        for at, (d, mask) in enumerate(places):
            number = len(copies)
            tiles[number] = jnp.dot(left, stack[at], preferred_element_type=F32) * (1.0 / ntok)
            column = ((z ^ d) * n_hid + (h ^ mask)) * width
            copy = pltpu.make_async_copy(
                tiles.at[number], out_ref.at[:, pl.ds(pl.multiple_of(column, width), width)], sems.at[number]
            )
            copy.start()
            copies.append(copy)
    if classes:
        labels, cross_ref = refs[len(slots)], outs[-1]
        onehot = (labels[...] == lax.broadcasted_iota(jnp.int32, (classes, ntok), 0)).astype(F32)
        counts = jnp.sum(onehot, axis=1, keepdims=True)
        sums = jnp.dot(onehot.astype(BF16), own_ref[...], preferred_element_type=F32)
        cross_ref[...] = sums / jnp.maximum(counts, 1.0)
    for copy in copies:
        copy.wait()


def gram_part(resid_cols, stacks, slots, n_tok, n_hid, before, labels=None):
    ntok, width = resid_cols.shape
    here = sum(len(places) for places in slots)
    gram_shape = pltpu.HBM((width, width * n_tok * n_hid), F32)
    extra, extra_specs = ([], []) if labels is None else ([labels[None, :]], [WHOLE])
    if before is not None:
        extra, extra_specs = extra + [before], extra_specs + [ANYWHERE]
    return run(
        functools.partial(gram_kernel, slots, n_hid, ntok, 0 if labels is None else CLASSES), "gram",
        [gram_shape] + ([] if labels is None else [jax.ShapeDtypeStruct((CLASSES, width), F32)]),
        [resid_cols, *stacks, *extra],
        2 * ntok * width * width * here, 4 * width * width * here,
        in_specs=[WHOLE] * (1 + len(stacks)) + extra_specs,
        out_specs=[ANYWHERE] + ([] if labels is None else [WHOLE]),
        input_output_aliases={} if before is None else {len(stacks) + len(extra): 0},
        scratch_shapes=[pltpu.VMEM((here, width, width), F32), pltpu.SemaphoreType.DMA((here,))],
    )


def class_means(resid_cols, labels):
    onehot = (labels[:, None] == jnp.arange(CLASSES, dtype=jnp.int32)[None, :]).astype(BF16)
    counts = jnp.sum(onehot.astype(F32), axis=0)
    class_sums = lax.dot_general(
        resid_cols, onehot, (((0,), (0,)), ((), ())), preferred_element_type=F32
    )
    return class_sums / jnp.maximum(counts, 1.0)[None, :]


def on_line(n_tok, n_hid, resid_in, norm_gain, gate_weight, up_weight, down_weight, labels):
    rows, block = resid_in.shape
    ntok, panel = rows * n_hid, block // n_hid
    depth, shard_ff = gate_weight.shape
    tiles = shard_ff // TILE
    ends = [TILE * (tiles * k // 3) for k in range(4)]
    chip_masks = list(range(2, n_hid, 2))

    def part(weight, k):
        return weight, 0, depth, ends[k], ends[k + 1] - ends[k]

    near = [resid_in] + [swap(resid_in, "hid", n_hid, mask) for mask in chip_masks]
    gate_0, up_0, own_x, gain = fetch(
        [
            part(gate_weight, 0),
            part(up_weight, 0),
            (resid_in, 0, rows, 0, block),
            (norm_gain[None, :], 0, 1, 0, block),
        ],
        (), "fetch_first",
    )
    relayed = copy_after(near[1], (gain,))
    gate_1, up_1 = fetch([part(gate_weight, 1), part(up_weight, 1)], (relayed,), "fetch_gate_up")
    far = [swap(piece, "hid", n_hid, 1) for piece in [near[0], relayed, *near[2:]]]
    masks = [0] + chip_masks + [1] + [mask + 1 for mask in chip_masks]
    lhs, x_cols, squares = run(
        functools.partial(tokens_kernel, masks, panel), "tokens",
        (
            jax.ShapeDtypeStruct((ntok, block), BF16),
            jax.ShapeDtypeStruct((ntok, panel), F32),
            jax.ShapeDtypeStruct((ntok, 1), F32),
        ),
        [own_x, *near[1:], *far, gain, gate_1],
        4 * ntok * block, 4 * ntok * block,
        in_specs=[WHOLE] * (n_hid + 1) + [ANYWHERE],
        out_specs=(WHOLE, WHOLE, WHOLE),
        scratch_shapes=[pltpu.VMEM((ntok, block), BF16)],
    )

    widths = [ends[k + 1] - ends[k] for k in range(3)]
    send_0, keep_0 = gate_up(lhs, gate_0, up_0, squares, n_tok)
    got_0 = swap(send_0, "tok", n_tok, 1)
    send_1, keep_1 = gate_up(lhs, gate_1, up_1, None, n_tok, (send_0,))
    got_1 = swap(send_1, "tok", n_tok, 1)
    sum_0 = pair_total(keep_0, got_0, 2 * widths[0], (send_1,))
    over_0 = swap(sum_0, "tok", n_tok, 2)
    gate_2, up_2 = fetch([part(gate_weight, 2), part(up_weight, 2)], (sum_0,), "fetch_gate_up")
    send_2, keep_2 = gate_up(lhs, gate_2, up_2, None, n_tok)
    got_2 = swap(send_2, "tok", n_tok, 1)
    sum_1 = pair_total(keep_1, got_1, 2 * widths[1], (send_2,))
    over_1 = swap(sum_1, "tok", n_tok, 2)
    sum_2 = pair_total(keep_2, got_2, 2 * widths[2], (sum_1,))
    over_2 = swap(sum_2, "tok", n_tok, 2)
    down_a, = fetch([(down_weight, 0, ends[2], 0, block)], (sum_2,), "fetch_down")

    a_own, scale = hidden_rows([(keep_0, got_0, over_0), (keep_1, got_1, over_1)], widths[:2], None, (down_a,))
    a_two = swap(a_own, "tok", n_tok, 2)
    a_one = swap(a_own, "tok", n_tok, 1)
    down_b, = fetch([(down_weight, ends[2], widths[2], 0, block)], (a_own,), "fetch_down")
    b_own, _ = hidden_rows([(keep_2, got_2, over_2)], widths[2:], scale, (down_b, a_one))
    b_two = swap(b_own, "tok", n_tok, 2)
    b_one = swap(b_own, "tok", n_tok, 1)
    a_three = swap(copy_after(a_two, (b_own,)), "tok", n_tok, 1)
    b_three = swap(b_two, "tok", n_tok, 1)
    hidden_a = [a_own, a_one, a_two, a_three]
    hidden_b = [b_own, b_one, b_two, b_three]

    here = [0] + chip_masks
    there = [mask + 1 for mask in here]
    first = down(hidden_a, down_a, there + here, panel, F32)
    other = down(hidden_b, down_b, there, panel, BF16, first, 0)
    other = swap(other, "hid", n_hid, 1)
    mine = down(hidden_b, down_b, here, panel, F32, first, len(there))
    summed, *sends = run(
        chip_sum_kernel, "chip_sum",
        [jax.ShapeDtypeStruct((ntok, panel), F32)] + [jax.ShapeDtypeStruct((ntok, panel), BF16)] * len(chip_masks),
        [mine, other], mine.size, 8 * mine.size,
        out_specs=[WHOLE] * len(here),
    )
    for mask, value in zip(chip_masks, sends):
        summed = summed + swap(value, "hid", n_hid, mask).astype(F32)
    resid_cols = (x_cols + summed).astype(BF16)

    column = [swap(resid_cols, "tok", n_tok, d) for d in range(1, n_tok)]
    across = swap(resid_cols, "hid", n_hid, 6)
    line = stack_after([resid_cols, *column], (across,))
    beside = [swap(line, "hid", n_hid, mask) for mask in (2, 4)]
    across_line = [swap(across, "tok", n_tok, d) for d in range(1, n_tok)]
    line_far = swap(line, "hid", n_hid, 1)
    across_far = swap(across, "hid", n_hid, 1)
    line_slots = [[(d, mask) for d in range(n_tok)] for mask in range(n_hid)]
    gram, cross = gram_part(
        resid_cols, [line, line_far, across[None], across_far[None]],
        [line_slots[0], line_slots[1], [(0, 6)], [(0, 7)]], n_tok, n_hid, None, labels,
    )
    done = pltpu.with_memory_space_constraint(gram, pltpu.HBM)
    near = stack_after([*beside, *across_line], (done,))
    far = swap(near, "hid", n_hid, 1)
    for stack, core in ((near, 0), (far, 1)):
        slots = line_slots[2 + core] + line_slots[4 + core] + line_slots[6 + core][1:]
        gram, = gram_part(resid_cols, [stack], [slots], n_tok, n_hid, gram)
    return (gram, cross.T)


def plain(n_tok, n_hid, resid_in, norm_gain, gate_weight, up_weight, down_weight, labels):
    x = lax.all_gather(resid_in, "hid", axis=0, tiled=True).astype(F32)
    ntok, block = x.shape
    total_sq = lax.psum(jnp.sum(x * x, axis=1), "tok")
    normed = (x * lax.rsqrt(total_sq / float(D) + 1e-05)[:, None] * norm_gain[None, :]).astype(BF16)

    def summed_over_tok(weight):
        product = jnp.dot(normed, weight, preferred_element_type=F32).astype(BF16)
        return lax.psum_scatter(product, "tok", scatter_dimension=0, tiled=True).astype(F32)

    hidden = (jax.nn.silu(summed_over_tok(gate_weight)) * summed_over_tok(up_weight)).astype(BF16)
    hidden = lax.all_gather(hidden, "tok", axis=0, tiled=True)
    partial_out = jnp.dot(hidden, down_weight, preferred_element_type=F32).astype(BF16)
    summed = lax.psum_scatter(partial_out, "hid", scatter_dimension=1, tiled=True).astype(F32)
    panel = block // n_hid
    x_cols = lax.dynamic_slice_in_dim(x, lax.axis_index("hid") * panel, panel, 1)
    resid_cols = (x_cols + summed).astype(BF16)
    everyone = lax.all_gather(resid_cols, ("tok", "hid"), axis=1, tiled=True)
    gram = lax.dot_general(
        resid_cols, everyone, (((0,), (0,)), ((), ())), preferred_element_type=F32
    ) / float(ntok)
    return (gram, class_means(resid_cols, labels))


def on_device(n_tok, n_hid, resid_in, norm_gain, gate_weight, *rest):
    panel = resid_in.shape[1] // n_hid
    fits = n_tok == 4 and n_hid == 8 and panel % 128 == 0 and gate_weight.shape[1] % TILE == 0 and gate_weight.shape[1] >= 3 * TILE
    body = on_line if fits else plain
    return body(n_tok, n_hid, resid_in, norm_gain, gate_weight, *rest)


def solution(mesh):
    return jax.shard_map(
        functools.partial(on_device, mesh.shape["tok"], mesh.shape["hid"]),
        mesh=mesh,
        in_specs=(
            P("hid", "tok"),
            P("tok"),
            P("tok", "hid"),
            P("tok", "hid"),
            P("hid", "tok"),
            P(),
        ),
        out_specs=(P(("tok", "hid"), None), P(("tok", "hid"), None)),
        check_vma=False,
    )
```

```python
import functools
import jax
import jax.numpy as jnp
from jax import lax
from jax.experimental import pallas as pl
from jax.experimental.pallas import tpu as pltpu
from jax.sharding import PartitionSpec as P

D = 8192
CLASSES = 64
TILE = 256
BF16 = jnp.bfloat16
F32 = jnp.float32
WHOLE = pl.BlockSpec(memory_space=pltpu.VMEM)
ANYWHERE = pl.BlockSpec(memory_space=pl.ANY)
SIDE = 128


def swap(value, axis, size, mask):
    return lax.ppermute(value, axis, [(i, i ^ mask) for i in range(size)])


def run(body, name, out_shape, operands, flops, bytes_accessed, in_specs=None, out_specs=WHOLE, **more):
    return pl.pallas_call(
        body,
        out_shape=out_shape,
        in_specs=[WHOLE] * len(operands) if in_specs is None else in_specs,
        out_specs=out_specs,
        compiler_params=pltpu.CompilerParams(vmem_limit_bytes=16 * 1024 * 1024),
        cost_estimate=pl.CostEstimate(flops=flops, bytes_accessed=bytes_accessed, transcendentals=0),
        name=name,
        **more,
    )(*operands)


def fetch(pieces, after, name):
    count = len(pieces)
    copies = []
    for number, (array, row, rows, column, columns) in enumerate(pieces):
        step = min(rows, 256)
        copies += [(number, at, step, row + at, column, columns) for at in range(0, rows, step)]

    def body(*refs):
        sources, targets, sems = refs[:count], refs[-1 - count:-1], refs[-1]
        started = []
        for sem, (number, at, step, row, column, columns) in enumerate(copies):
            copy = pltpu.make_async_copy(
                sources[number].at[pl.ds(row, step), pl.ds(column, columns)],
                targets[number].at[pl.ds(at, step), :],
                sems.at[sem],
            )
            copy.start()
            started.append(copy)
        for copy in started:
            copy.wait()

    size = sum(rows * columns * array.dtype.itemsize for array, _, rows, _, columns in pieces)
    return run(
        body, name,
        [pltpu.VMEM((rows, columns), array.dtype) for array, _, rows, _, columns in pieces],
        [pltpu.with_memory_space_constraint(piece[0], pltpu.HBM) for piece in pieces] + list(after),
        0, 0,
        in_specs=[ANYWHERE] * (count + len(after)),
        out_specs=[WHOLE] * count,
        scratch_shapes=[pltpu.SemaphoreType.DMA((len(copies),))],
    )


def tokens_kernel(masks, panel, *refs):
    blocks, gain, (lhs, cols, squares, x) = refs[:len(masks)], refs[len(masks)], refs[-4:]
    h = lax.axis_index("hid")
    rows = blocks[0].shape[0]
    for mask, block in zip(masks, blocks):
        x[pl.ds(pl.multiple_of((h ^ mask) * rows, rows), rows), :] = block[...]
    values = x[...].astype(F32)
    lhs[...] = (values * gain[...]).astype(BF16)
    squares[...] = jnp.sum(values * values, axis=1, keepdims=True)
    cols[...] = x[:, pl.ds(pl.multiple_of(h * panel, panel), panel)].astype(F32)


def split(value):
    lane = lax.broadcasted_iota(jnp.int32, (value.shape[0], SIDE), 1)
    out = jnp.zeros((value.shape[0], SIDE), F32)
    for part in range(3):
        rounded = value.astype(BF16).astype(F32)
        out = jnp.where(lane == part, rounded, out)
        value = value - rounded
    return out


def joined(parts):
    return jnp.sum(parts.astype(F32), axis=1, keepdims=True)


def gate_up_kernel(lhs_ref, gate_ref, up_ref, *refs):
    send_ref, keep_ref, both, side = refs[-4:]
    places = ((keep_ref, 0), (send_ref, 0), (keep_ref, 1), (send_ref, 1))
    rows = send_ref.shape[1]
    z = lax.axis_index("tok")
    lhs = lhs_ref[...]

    def hand_out(source, start, width):
        for d, (out, slot) in enumerate(places):
            at = pl.multiple_of((z ^ d) * rows, rows)
            out[slot, :, start:start + width] = source[pl.ds(at, rows), :].astype(BF16)

    for tile in range(gate_ref.shape[1] // TILE):
        cols = slice(tile * TILE, (tile + 1) * TILE)
        both[:, :TILE] = jnp.dot(lhs, gate_ref[:, cols], preferred_element_type=F32)
        both[:, TILE:] = jnp.dot(lhs, up_ref[:, cols], preferred_element_type=F32)
        hand_out(both, 2 * tile * TILE, 2 * TILE)
    if send_ref.shape[2] > 2 * gate_ref.shape[1]:
        side[...] = split(refs[0][...])
        hand_out(side, 2 * gate_ref.shape[1], SIDE)


def gate_up(lhs, gate, up, squares, n_tok, after=()):
    ntok, depth = lhs.shape
    width = gate.shape[1]
    rows = ntok // n_tok
    extra = [] if squares is None else [squares]
    shape = jax.ShapeDtypeStruct((2, rows, 2 * width + SIDE * len(extra)), BF16)
    return run(
        gate_up_kernel, "gate_up", [shape, shape], [lhs, gate, up, *extra, *after],
        0, 0,
        in_specs=[WHOLE] * (3 + len(extra)) + [ANYWHERE] * len(after),
        out_specs=[WHOLE] * 2,
        scratch_shapes=[pltpu.VMEM((ntok, 2 * TILE), F32), pltpu.VMEM((ntok, SIDE), F32)],
    )


def pair_total(keep, got, main, after):
    def body(keep_ref, got_ref, *refs):
        out = refs[-1]
        out[:, :main] = (keep_ref[1, :, :main].astype(F32) + got_ref[1, :, :main].astype(F32)).astype(BF16)
        if out.shape[1] > main:
            out[:, main:] = split(joined(keep_ref[1, :, main:]) + joined(got_ref[1, :, main:])).astype(BF16)

    size = keep.size // 2
    return run(
        body, "pair_total", jax.ShapeDtypeStruct(keep.shape[1:], BF16), [keep, got, *after],
        size, 6 * size, in_specs=[WHOLE] * 2 + [ANYWHERE] * len(after),
    )


def copy_after(value, after):
    def body(value_ref, *refs):
        refs[-1][...] = value_ref[...]

    return run(
        body, "copy", jax.ShapeDtypeStruct(value.shape, value.dtype), [value, *after],
        0, 4 * value.size, in_specs=[WHOLE] + [ANYWHERE] * len(after),
    )


def stack_after(blocks, after):
    stacks = [block if block.ndim == 3 else block[None] for block in blocks]
    total = sum(stack.shape[0] for stack in stacks)

    def body(*refs):
        at = 0
        for ref in refs[:len(stacks)]:
            refs[-1][at:at + ref.shape[0]] = ref[...]
            at += ref.shape[0]

    shape = jax.ShapeDtypeStruct((total, *stacks[0].shape[1:]), blocks[0].dtype)
    return run(
        body, "stack", shape, [*stacks, *after], 0, 4 * sum(stack.size for stack in stacks),
        in_specs=[WHOLE] * len(stacks) + [ANYWHERE] * len(after),
    )


def hidden_rows(chunks, widths, scale, after):
    rows = chunks[0][0].shape[1]
    given = [] if scale is None else [scale]

    def body(*refs):
        out_ref, scale_ref = refs[-2:]
        keep_ref, got_ref, over_ref = refs[:3]
        if scale is None:
            tail = slice(2 * widths[0], 2 * widths[0] + SIDE)
            squares = joined(keep_ref[0, :, tail]) + joined(got_ref[0, :, tail]) + joined(over_ref[:, tail])
            factor = lax.rsqrt(squares / float(D) + 1e-05)
        else:
            factor = refs[3 * len(chunks)][...]
        scale_ref[...] = factor
        start = 0
        for k, width in enumerate(widths):
            keep_ref, got_ref, over_ref = refs[3 * k:3 * k + 3]

            def total(at):
                cols = slice(at, at + TILE)
                return (
                    keep_ref[0, :, cols].astype(F32) + got_ref[0, :, cols].astype(F32) + over_ref[:, cols].astype(F32)
                ) * factor

            for at in range(0, width, TILE):
                gate, up = total(2 * at), total(2 * at + TILE)
                out_ref[:, start + at:start + at + TILE] = (jax.nn.silu(gate) * up).astype(BF16)
            start += width

    size = rows * sum(widths)
    return run(
        body, "hidden",
        [jax.ShapeDtypeStruct((rows, sum(widths)), BF16), jax.ShapeDtypeStruct((rows, 1), F32)],
        [part for chunk in chunks for part in chunk] + given + list(after), 20 * size, 14 * size,
        in_specs=[WHOLE] * (3 * len(chunks) + len(given)) + [ANYWHERE] * len(after),
        out_specs=[WHOLE] * 2,
    )


def down_kernel(masks, skip, panel, n_blocks, *refs):
    blocks, weight, lhs, out = refs[:n_blocks], refs[n_blocks], refs[-1], refs[-2]
    before = refs[n_blocks + 1] if len(refs) == n_blocks + 4 else None
    z = lax.axis_index("tok")
    h = lax.axis_index("hid")
    rows = blocks[0].shape[0]
    for d, block in enumerate(blocks):
        lhs[pl.ds(pl.multiple_of((z ^ d) * rows, rows), rows), :] = block[...]
    values = lhs[...]
    for slot, mask in enumerate(masks):
        column = pl.multiple_of((h ^ mask) * panel, panel)
        total = jnp.dot(values, weight[:, pl.ds(column, panel)], preferred_element_type=F32)
        if before is not None:
            total = total + before[skip + slot]
        out[slot] = total.astype(out.dtype)


def down(blocks, weight, masks, panel, kind, before=None, skip=0):
    rows, depth = blocks[0].shape
    ntok = rows * len(blocks)
    return run(
        functools.partial(down_kernel, masks, skip, panel, len(blocks)), "down",
        jax.ShapeDtypeStruct((len(masks), ntok, panel), kind),
        [*blocks, weight] + ([] if before is None else [before]),
        2 * ntok * depth * panel * len(masks), 2 * depth * panel * len(masks),
        scratch_shapes=[pltpu.VMEM((ntok, depth), BF16)],
    )


def chip_sum_kernel(mine_ref, other_ref, own_ref, *outs):
    own_ref[...] = mine_ref[0] + other_ref[0].astype(F32)
    for e, out in enumerate(outs):
        out[...] = (mine_ref[e + 1] + other_ref[e + 1].astype(F32)).astype(BF16)


def gram_kernel(slots, n_hid, ntok, classes, own_ref, *refs):
    stacks = refs[:len(slots)]
    outs, (tiles, sems) = refs[:-2], refs[-2:]
    out_ref = outs[-2] if classes else outs[-1]
    z = lax.axis_index("tok")
    h = lax.axis_index("hid")
    width = own_ref.shape[1]
    left = own_ref[...].T
    copies = []
    for stack, places in zip(stacks, slots):
        for at, (d, mask) in enumerate(places):
            number = len(copies)
            tiles[number] = jnp.dot(left, stack[at], preferred_element_type=F32) * (1.0 / ntok)
            column = ((z ^ d) * n_hid + (h ^ mask)) * width
            copy = pltpu.make_async_copy(
                tiles.at[number], out_ref.at[:, pl.ds(pl.multiple_of(column, width), width)], sems.at[number]
            )
            copy.start()
            copies.append(copy)
    if classes:
        labels, cross_ref = refs[len(slots)], outs[-1]
        onehot = (labels[...] == lax.broadcasted_iota(jnp.int32, (classes, ntok), 0)).astype(F32)
        counts = jnp.sum(onehot, axis=1, keepdims=True)
        sums = jnp.dot(onehot.astype(BF16), own_ref[...], preferred_element_type=F32)
        cross_ref[...] = sums / jnp.maximum(counts, 1.0)
    for copy in copies:
        copy.wait()


def gram_part(resid_cols, stacks, slots, n_tok, n_hid, before, labels=None):
    ntok, width = resid_cols.shape
    here = sum(len(places) for places in slots)
    gram_shape = pltpu.HBM((width, width * n_tok * n_hid), F32)
    extra, extra_specs = ([], []) if labels is None else ([labels[None, :]], [WHOLE])
    if before is not None:
        extra, extra_specs = extra + [before], extra_specs + [ANYWHERE]
    return run(
        functools.partial(gram_kernel, slots, n_hid, ntok, 0 if labels is None else CLASSES), "gram",
        [gram_shape] + ([] if labels is None else [jax.ShapeDtypeStruct((CLASSES, width), F32)]),
        [resid_cols, *stacks, *extra],
        2 * ntok * width * width * here, 4 * width * width * here,
        in_specs=[WHOLE] * (1 + len(stacks)) + extra_specs,
        out_specs=[ANYWHERE] + ([] if labels is None else [WHOLE]),
        input_output_aliases={} if before is None else {len(stacks) + len(extra): 0},
        scratch_shapes=[pltpu.VMEM((here, width, width), F32), pltpu.SemaphoreType.DMA((here,))],
    )


def class_means(resid_cols, labels):
    onehot = (labels[:, None] == jnp.arange(CLASSES, dtype=jnp.int32)[None, :]).astype(BF16)
    counts = jnp.sum(onehot.astype(F32), axis=0)
    class_sums = lax.dot_general(
        resid_cols, onehot, (((0,), (0,)), ((), ())), preferred_element_type=F32
    )
    return class_sums / jnp.maximum(counts, 1.0)[None, :]


def on_line(n_tok, n_hid, resid_in, norm_gain, gate_weight, up_weight, down_weight, labels):
    rows, block = resid_in.shape
    ntok, panel = rows * n_hid, block // n_hid
    depth, shard_ff = gate_weight.shape
    tiles = shard_ff // TILE
    ends = [TILE * (tiles * k // 3) for k in range(4)]
    chip_masks = list(range(2, n_hid, 2))

    def part(weight, k):
        return weight, 0, depth, ends[k], ends[k + 1] - ends[k]

    near = [resid_in] + [swap(resid_in, "hid", n_hid, mask) for mask in chip_masks]
    gate_0, up_0, own_x, gain = fetch(
        [
            part(gate_weight, 0),
            part(up_weight, 0),
            (resid_in, 0, rows, 0, block),
            (norm_gain[None, :], 0, 1, 0, block),
        ],
        (), "fetch_first",
    )
    relayed = copy_after(near[1], (gain,))
    far = [swap(piece, "hid", n_hid, 1) for piece in [near[0], relayed, *near[2:]]]
    masks = [0] + chip_masks + [1] + [mask + 1 for mask in chip_masks]
    lhs, x_cols, squares = run(
        functools.partial(tokens_kernel, masks, panel), "tokens",
        (
            jax.ShapeDtypeStruct((ntok, block), BF16),
            jax.ShapeDtypeStruct((ntok, panel), F32),
            jax.ShapeDtypeStruct((ntok, 1), F32),
        ),
        [own_x, *near[1:], *far, gain],
        4 * ntok * block, 4 * ntok * block,
        out_specs=(WHOLE, WHOLE, WHOLE),
        scratch_shapes=[pltpu.VMEM((ntok, block), BF16)],
    )

    widths = [ends[k + 1] - ends[k] for k in range(3)]
    send_0, keep_0 = gate_up(lhs, gate_0, up_0, squares, n_tok)
    got_0 = swap(send_0, "tok", n_tok, 1)
    gate_1, up_1 = fetch([part(gate_weight, 1), part(up_weight, 1)], (send_0,), "fetch_gate_up")
    send_1, keep_1 = gate_up(lhs, gate_1, up_1, None, n_tok)
    got_1 = swap(send_1, "tok", n_tok, 1)
    sum_0 = pair_total(keep_0, got_0, 2 * widths[0], (send_1,))
    over_0 = swap(sum_0, "tok", n_tok, 2)
    gate_2, up_2 = fetch([part(gate_weight, 2), part(up_weight, 2)], (sum_0,), "fetch_gate_up")
    send_2, keep_2 = gate_up(lhs, gate_2, up_2, None, n_tok)
    got_2 = swap(send_2, "tok", n_tok, 1)
    sum_1 = pair_total(keep_1, got_1, 2 * widths[1], (send_2,))
    over_1 = swap(sum_1, "tok", n_tok, 2)
    down_b, = fetch([(down_weight, ends[2], widths[2], 0, block)], (sum_1,), "fetch_down")
    sum_2 = pair_total(keep_2, got_2, 2 * widths[2], (down_b,))
    over_2 = swap(sum_2, "tok", n_tok, 2)
    down_a, = fetch([(down_weight, 0, ends[2], 0, block)], (sum_2,), "fetch_down")

    a_own, scale = hidden_rows([(keep_0, got_0, over_0), (keep_1, got_1, over_1)], widths[:2], None, (down_a,))
    a_two = swap(a_own, "tok", n_tok, 2)
    a_one = swap(a_own, "tok", n_tok, 1)
    b_own, _ = hidden_rows([(keep_2, got_2, over_2)], widths[2:], scale, ())
    b_two = swap(b_own, "tok", n_tok, 2)
    b_one = swap(b_own, "tok", n_tok, 1)
    a_three = swap(copy_after(a_two, (b_own,)), "tok", n_tok, 1)
    b_three = swap(b_two, "tok", n_tok, 1)
    hidden_a = [a_own, a_one, a_two, a_three]
    hidden_b = [b_own, b_one, b_two, b_three]

    here = [0] + chip_masks
    there = [mask + 1 for mask in here]
    first = down(hidden_a, down_a, there + here, panel, F32)
    other = down(hidden_b, down_b, there, panel, BF16, first, 0)
    other = swap(other, "hid", n_hid, 1)
    mine = down(hidden_b, down_b, here, panel, F32, first, len(there))
    summed, *sends = run(
        chip_sum_kernel, "chip_sum",
        [jax.ShapeDtypeStruct((ntok, panel), F32)] + [jax.ShapeDtypeStruct((ntok, panel), BF16)] * len(chip_masks),
        [mine, other], mine.size, 8 * mine.size,
        out_specs=[WHOLE] * len(here),
    )
    for mask, value in reversed(list(zip(chip_masks, sends))):
        summed = summed + swap(value, "hid", n_hid, mask).astype(F32)
    resid_cols = (x_cols + summed).astype(BF16)

    column = [swap(resid_cols, "tok", n_tok, d) for d in range(1, n_tok)]
    across = swap(resid_cols, "hid", n_hid, 6)
    line = stack_after([resid_cols, *column], (across,))
    beside = [swap(line, "hid", n_hid, mask) for mask in (2, 4)]
    across_line = [swap(across, "tok", n_tok, d) for d in range(1, n_tok)]
    line_far = swap(line, "hid", n_hid, 1)
    across_far = swap(across, "hid", n_hid, 1)
    line_slots = [[(d, mask) for d in range(n_tok)] for mask in range(n_hid)]
    gram, cross = gram_part(
        resid_cols, [line, line_far, across[None], across_far[None]],
        [line_slots[0], line_slots[1], [(0, 6)], [(0, 7)]], n_tok, n_hid, None, labels,
    )
    done = pltpu.with_memory_space_constraint(gram, pltpu.HBM)
    near = stack_after([*beside, *across_line], (done,))
    far = swap(near, "hid", n_hid, 1)
    for stack, core in ((near, 0), (far, 1)):
        slots = line_slots[2 + core] + line_slots[4 + core] + line_slots[6 + core][1:]
        gram, = gram_part(resid_cols, [stack], [slots], n_tok, n_hid, gram)
    return (gram, cross.T)


def plain(n_tok, n_hid, resid_in, norm_gain, gate_weight, up_weight, down_weight, labels):
    x = lax.all_gather(resid_in, "hid", axis=0, tiled=True).astype(F32)
    ntok, block = x.shape
    total_sq = lax.psum(jnp.sum(x * x, axis=1), "tok")
    normed = (x * lax.rsqrt(total_sq / float(D) + 1e-05)[:, None] * norm_gain[None, :]).astype(BF16)

    def summed_over_tok(weight):
        product = jnp.dot(normed, weight, preferred_element_type=F32).astype(BF16)
        return lax.psum_scatter(product, "tok", scatter_dimension=0, tiled=True).astype(F32)

    hidden = (jax.nn.silu(summed_over_tok(gate_weight)) * summed_over_tok(up_weight)).astype(BF16)
    hidden = lax.all_gather(hidden, "tok", axis=0, tiled=True)
    partial_out = jnp.dot(hidden, down_weight, preferred_element_type=F32).astype(BF16)
    summed = lax.psum_scatter(partial_out, "hid", scatter_dimension=1, tiled=True).astype(F32)
    panel = block // n_hid
    x_cols = lax.dynamic_slice_in_dim(x, lax.axis_index("hid") * panel, panel, 1)
    resid_cols = (x_cols + summed).astype(BF16)
    everyone = lax.all_gather(resid_cols, ("tok", "hid"), axis=1, tiled=True)
    gram = lax.dot_general(
        resid_cols, everyone, (((0,), (0,)), ((), ())), preferred_element_type=F32
    ) / float(ntok)
    return (gram, class_means(resid_cols, labels))


def on_device(n_tok, n_hid, resid_in, norm_gain, gate_weight, *rest):
    panel = resid_in.shape[1] // n_hid
    fits = n_tok == 4 and n_hid == 8 and panel % 128 == 0 and gate_weight.shape[1] % TILE == 0 and gate_weight.shape[1] >= 3 * TILE
    body = on_line if fits else plain
    return body(n_tok, n_hid, resid_in, norm_gain, gate_weight, *rest)


def solution(mesh):
    return jax.shard_map(
        functools.partial(on_device, mesh.shape["tok"], mesh.shape["hid"]),
        mesh=mesh,
        in_specs=(
            P("hid", "tok"),
            P("tok"),
            P("tok", "hid"),
            P("tok", "hid"),
            P("hid", "tok"),
            P(),
        ),
        out_specs=(P(("tok", "hid"), None), P(("tok", "hid"), None)),
        check_vma=False,
    )
```

```python
import functools
import jax
import jax.numpy as jnp
from jax import lax
from jax.experimental import pallas as pl
from jax.experimental.pallas import tpu as pltpu
from jax.sharding import PartitionSpec as P

D = 8192
CLASSES = 64
TILE = 256
BF16 = jnp.bfloat16
F32 = jnp.float32
WHOLE = pl.BlockSpec(memory_space=pltpu.VMEM)
ANYWHERE = pl.BlockSpec(memory_space=pl.ANY)
SIDE = 128


def swap(value, axis, size, mask):
    return lax.ppermute(value, axis, [(i, i ^ mask) for i in range(size)])


def run(body, name, out_shape, operands, flops, bytes_accessed, in_specs=None, out_specs=WHOLE, **more):
    return pl.pallas_call(
        body,
        out_shape=out_shape,
        in_specs=[WHOLE] * len(operands) if in_specs is None else in_specs,
        out_specs=out_specs,
        compiler_params=pltpu.CompilerParams(vmem_limit_bytes=16 * 1024 * 1024),
        cost_estimate=pl.CostEstimate(flops=flops, bytes_accessed=bytes_accessed, transcendentals=0),
        name=name,
        **more,
    )(*operands)


def fetch(pieces, after, name):
    count = len(pieces)
    copies = []
    for number, (array, row, rows, column, columns) in enumerate(pieces):
        step = min(rows, 256)
        copies += [(number, at, step, row + at, column, columns) for at in range(0, rows, step)]

    def body(*refs):
        sources, targets, sems = refs[:count], refs[-1 - count:-1], refs[-1]
        started = []
        for sem, (number, at, step, row, column, columns) in enumerate(copies):
            copy = pltpu.make_async_copy(
                sources[number].at[pl.ds(row, step), pl.ds(column, columns)],
                targets[number].at[pl.ds(at, step), :],
                sems.at[sem],
            )
            copy.start()
            started.append(copy)
        for copy in started:
            copy.wait()

    size = sum(rows * columns * array.dtype.itemsize for array, _, rows, _, columns in pieces)
    return run(
        body, name,
        [pltpu.VMEM((rows, columns), array.dtype) for array, _, rows, _, columns in pieces],
        [pltpu.with_memory_space_constraint(piece[0], pltpu.HBM) for piece in pieces] + list(after),
        0, 0,
        in_specs=[ANYWHERE] * (count + len(after)),
        out_specs=[WHOLE] * count,
        scratch_shapes=[pltpu.SemaphoreType.DMA((len(copies),))],
    )


def tokens_kernel(masks, panel, *refs):
    blocks, gain, (lhs, cols, squares, x) = refs[:len(masks)], refs[len(masks)], refs[-4:]
    h = lax.axis_index("hid")
    rows = blocks[0].shape[0]
    for mask, block in zip(masks, blocks):
        x[pl.ds(pl.multiple_of((h ^ mask) * rows, rows), rows), :] = block[...]
    values = x[...].astype(F32)
    lhs[...] = (values * gain[...]).astype(BF16)
    squares[...] = jnp.sum(values * values, axis=1, keepdims=True)
    cols[...] = x[:, pl.ds(pl.multiple_of(h * panel, panel), panel)].astype(F32)


def split(value):
    lane = lax.broadcasted_iota(jnp.int32, (value.shape[0], SIDE), 1)
    out = jnp.zeros((value.shape[0], SIDE), F32)
    for part in range(3):
        rounded = value.astype(BF16).astype(F32)
        out = jnp.where(lane == part, rounded, out)
        value = value - rounded
    return out


def joined(parts):
    return jnp.sum(parts.astype(F32), axis=1, keepdims=True)


def gate_up_kernel(lhs_ref, gate_ref, up_ref, *refs):
    send_ref, keep_ref, both, side = refs[-4:]
    places = ((keep_ref, 0), (send_ref, 0), (keep_ref, 1), (send_ref, 1))
    rows = send_ref.shape[1]
    z = lax.axis_index("tok")
    lhs = lhs_ref[...]

    def hand_out(source, start, width):
        for d, (out, slot) in enumerate(places):
            at = pl.multiple_of((z ^ d) * rows, rows)
            out[slot, :, start:start + width] = source[pl.ds(at, rows), :].astype(BF16)

    for tile in range(gate_ref.shape[1] // TILE):
        cols = slice(tile * TILE, (tile + 1) * TILE)
        both[:, :TILE] = jnp.dot(lhs, gate_ref[:, cols], preferred_element_type=F32)
        both[:, TILE:] = jnp.dot(lhs, up_ref[:, cols], preferred_element_type=F32)
        hand_out(both, 2 * tile * TILE, 2 * TILE)
    if send_ref.shape[2] > 2 * gate_ref.shape[1]:
        side[...] = split(refs[0][...])
        hand_out(side, 2 * gate_ref.shape[1], SIDE)


def gate_up(lhs, gate, up, squares, n_tok, after=()):
    ntok, depth = lhs.shape
    width = gate.shape[1]
    rows = ntok // n_tok
    extra = [] if squares is None else [squares]
    shape = jax.ShapeDtypeStruct((2, rows, 2 * width + SIDE * len(extra)), BF16)
    return run(
        gate_up_kernel, "gate_up", [shape, shape], [lhs, gate, up, *extra, *after],
        0, 0,
        in_specs=[WHOLE] * (3 + len(extra)) + [ANYWHERE] * len(after),
        out_specs=[WHOLE] * 2,
        scratch_shapes=[pltpu.VMEM((ntok, 2 * TILE), F32), pltpu.VMEM((ntok, SIDE), F32)],
    )


def pair_total(keep, got, main, after):
    def body(keep_ref, got_ref, *refs):
        out = refs[-1]
        out[:, :main] = (keep_ref[1, :, :main].astype(F32) + got_ref[1, :, :main].astype(F32)).astype(BF16)
        if out.shape[1] > main:
            out[:, main:] = split(joined(keep_ref[1, :, main:]) + joined(got_ref[1, :, main:])).astype(BF16)

    size = keep.size // 2
    return run(
        body, "pair_total", jax.ShapeDtypeStruct(keep.shape[1:], BF16), [keep, got, *after],
        size, 6 * size, in_specs=[WHOLE] * 2 + [ANYWHERE] * len(after),
    )


def copy_after(value, after):
    def body(value_ref, *refs):
        refs[-1][...] = value_ref[...]

    return run(
        body, "copy", jax.ShapeDtypeStruct(value.shape, value.dtype), [value, *after],
        0, 4 * value.size, in_specs=[WHOLE] + [ANYWHERE] * len(after),
    )


def stack_after(blocks, after):
    stacks = [block if block.ndim == 3 else block[None] for block in blocks]
    total = sum(stack.shape[0] for stack in stacks)

    def body(*refs):
        at = 0
        for ref in refs[:len(stacks)]:
            refs[-1][at:at + ref.shape[0]] = ref[...]
            at += ref.shape[0]

    shape = jax.ShapeDtypeStruct((total, *stacks[0].shape[1:]), blocks[0].dtype)
    return run(
        body, "stack", shape, [*stacks, *after], 0, 4 * sum(stack.size for stack in stacks),
        in_specs=[WHOLE] * len(stacks) + [ANYWHERE] * len(after),
    )


def hidden_rows(chunks, widths, scale, after):
    rows = chunks[0][0].shape[1]
    given = [] if scale is None else [scale]

    def body(*refs):
        out_ref, scale_ref = refs[-2:]
        keep_ref, got_ref, over_ref = refs[:3]
        if scale is None:
            tail = slice(2 * widths[0], 2 * widths[0] + SIDE)
            squares = joined(keep_ref[0, :, tail]) + joined(got_ref[0, :, tail]) + joined(over_ref[:, tail])
            factor = lax.rsqrt(squares / float(D) + 1e-05)
        else:
            factor = refs[3 * len(chunks)][...]
        scale_ref[...] = factor
        start = 0
        for k, width in enumerate(widths):
            keep_ref, got_ref, over_ref = refs[3 * k:3 * k + 3]

            def total(at):
                cols = slice(at, at + TILE)
                return (
                    keep_ref[0, :, cols].astype(F32) + got_ref[0, :, cols].astype(F32) + over_ref[:, cols].astype(F32)
                ) * factor

            for at in range(0, width, TILE):
                gate, up = total(2 * at), total(2 * at + TILE)
                out_ref[:, start + at:start + at + TILE] = (jax.nn.silu(gate) * up).astype(BF16)
            start += width

    size = rows * sum(widths)
    return run(
        body, "hidden",
        [jax.ShapeDtypeStruct((rows, sum(widths)), BF16), jax.ShapeDtypeStruct((rows, 1), F32)],
        [part for chunk in chunks for part in chunk] + given + list(after), 20 * size, 14 * size,
        in_specs=[WHOLE] * (3 * len(chunks) + len(given)) + [ANYWHERE] * len(after),
        out_specs=[WHOLE] * 2,
    )


def down_kernel(masks, skip, panel, n_blocks, *refs):
    blocks, weight, lhs, out = refs[:n_blocks], refs[n_blocks], refs[-1], refs[-2]
    before = refs[n_blocks + 1] if len(refs) == n_blocks + 4 else None
    z = lax.axis_index("tok")
    h = lax.axis_index("hid")
    rows = blocks[0].shape[0]
    for d, block in enumerate(blocks):
        lhs[pl.ds(pl.multiple_of((z ^ d) * rows, rows), rows), :] = block[...]
    values = lhs[...]
    for slot, mask in enumerate(masks):
        column = pl.multiple_of((h ^ mask) * panel, panel)
        total = jnp.dot(values, weight[:, pl.ds(column, panel)], preferred_element_type=F32)
        if before is not None:
            total = total + before[skip + slot]
        out[slot] = total.astype(out.dtype)


def down(blocks, weight, masks, panel, kind, before=None, skip=0):
    rows, depth = blocks[0].shape
    ntok = rows * len(blocks)
    return run(
        functools.partial(down_kernel, masks, skip, panel, len(blocks)), "down",
        jax.ShapeDtypeStruct((len(masks), ntok, panel), kind),
        [*blocks, weight] + ([] if before is None else [before]),
        2 * ntok * depth * panel * len(masks), 2 * depth * panel * len(masks),
        scratch_shapes=[pltpu.VMEM((ntok, depth), BF16)],
    )


def chip_sum_kernel(mine_ref, other_ref, own_ref, *outs):
    own_ref[...] = mine_ref[0] + other_ref[0].astype(F32)
    for e, out in enumerate(outs):
        out[...] = (mine_ref[e + 1] + other_ref[e + 1].astype(F32)).astype(BF16)


def gram_kernel(slots, n_hid, ntok, classes, own_ref, *refs):
    stacks = refs[:len(slots)]
    outs, (tiles, sems) = refs[:-2], refs[-2:]
    out_ref = outs[-2] if classes else outs[-1]
    z = lax.axis_index("tok")
    h = lax.axis_index("hid")
    width = own_ref.shape[1]
    left = own_ref[...].T
    copies = []
    for stack, places in zip(stacks, slots):
        for at, (d, mask) in enumerate(places):
            number = len(copies)
            tiles[number] = jnp.dot(left, stack[at], preferred_element_type=F32) * (1.0 / ntok)
            column = ((z ^ d) * n_hid + (h ^ mask)) * width
            copy = pltpu.make_async_copy(
                tiles.at[number], out_ref.at[:, pl.ds(pl.multiple_of(column, width), width)], sems.at[number]
            )
            copy.start()
            copies.append(copy)
    if classes:
        labels, cross_ref = refs[len(slots)], outs[-1]
        onehot = (labels[...] == lax.broadcasted_iota(jnp.int32, (classes, ntok), 0)).astype(F32)
        counts = jnp.sum(onehot, axis=1, keepdims=True)
        sums = jnp.dot(onehot.astype(BF16), own_ref[...], preferred_element_type=F32)
        cross_ref[...] = sums / jnp.maximum(counts, 1.0)
    for copy in copies:
        copy.wait()


def gram_part(resid_cols, stacks, slots, n_tok, n_hid, before, labels=None):
    ntok, width = resid_cols.shape
    here = sum(len(places) for places in slots)
    gram_shape = pltpu.HBM((width, width * n_tok * n_hid), F32)
    extra, extra_specs = ([], []) if labels is None else ([labels[None, :]], [WHOLE])
    if before is not None:
        extra, extra_specs = extra + [before], extra_specs + [ANYWHERE]
    return run(
        functools.partial(gram_kernel, slots, n_hid, ntok, 0 if labels is None else CLASSES), "gram",
        [gram_shape] + ([] if labels is None else [jax.ShapeDtypeStruct((CLASSES, width), F32)]),
        [resid_cols, *stacks, *extra],
        2 * ntok * width * width * here, 4 * width * width * here,
        in_specs=[WHOLE] * (1 + len(stacks)) + extra_specs,
        out_specs=[ANYWHERE] + ([] if labels is None else [WHOLE]),
        input_output_aliases={} if before is None else {len(stacks) + len(extra): 0},
        scratch_shapes=[pltpu.VMEM((here, width, width), F32), pltpu.SemaphoreType.DMA((here,))],
    )


def class_means(resid_cols, labels):
    onehot = (labels[:, None] == jnp.arange(CLASSES, dtype=jnp.int32)[None, :]).astype(BF16)
    counts = jnp.sum(onehot.astype(F32), axis=0)
    class_sums = lax.dot_general(
        resid_cols, onehot, (((0,), (0,)), ((), ())), preferred_element_type=F32
    )
    return class_sums / jnp.maximum(counts, 1.0)[None, :]


def on_line(n_tok, n_hid, resid_in, norm_gain, gate_weight, up_weight, down_weight, labels):
    rows, block = resid_in.shape
    ntok, panel = rows * n_hid, block // n_hid
    depth, shard_ff = gate_weight.shape
    tiles = shard_ff // TILE
    ends = [TILE * (tiles * k // 3) for k in range(4)]
    chip_masks = list(range(2, n_hid, 2))

    def part(weight, k):
        return weight, 0, depth, ends[k], ends[k + 1] - ends[k]

    near = [resid_in] + [swap(resid_in, "hid", n_hid, mask) for mask in chip_masks]
    gate_0, up_0, own_x, gain = fetch(
        [
            part(gate_weight, 0),
            part(up_weight, 0),
            (resid_in, 0, rows, 0, block),
            (norm_gain[None, :], 0, 1, 0, block),
        ],
        (), "fetch_first",
    )
    relayed = copy_after(near[1], (gain,))
    far = [swap(piece, "hid", n_hid, 1) for piece in [near[0], relayed, *near[2:]]]
    masks = [0] + chip_masks + [1] + [mask + 1 for mask in chip_masks]
    lhs, x_cols, squares = run(
        functools.partial(tokens_kernel, masks, panel), "tokens",
        (
            jax.ShapeDtypeStruct((ntok, block), BF16),
            jax.ShapeDtypeStruct((ntok, panel), F32),
            jax.ShapeDtypeStruct((ntok, 1), F32),
        ),
        [own_x, *near[1:], *far, gain],
        4 * ntok * block, 4 * ntok * block,
        out_specs=(WHOLE, WHOLE, WHOLE),
        scratch_shapes=[pltpu.VMEM((ntok, block), BF16)],
    )

    widths = [ends[k + 1] - ends[k] for k in range(3)]
    send_0, keep_0 = gate_up(lhs, gate_0, up_0, squares, n_tok)
    got_0 = swap(send_0, "tok", n_tok, 1)
    gate_1, up_1 = fetch([part(gate_weight, 1), part(up_weight, 1)], (send_0,), "fetch_gate_up")
    send_1, keep_1 = gate_up(lhs, gate_1, up_1, None, n_tok)
    got_1 = swap(send_1, "tok", n_tok, 1)
    sum_0 = pair_total(keep_0, got_0, 2 * widths[0], (send_1,))
    over_0 = swap(sum_0, "tok", n_tok, 2)
    gate_2, up_2 = fetch([part(gate_weight, 2), part(up_weight, 2)], (sum_0,), "fetch_gate_up")
    send_2, keep_2 = gate_up(lhs, gate_2, up_2, None, n_tok)
    got_2 = swap(send_2, "tok", n_tok, 1)
    sum_1 = pair_total(keep_1, got_1, 2 * widths[1], (send_2,))
    over_1 = swap(sum_1, "tok", n_tok, 2)
    down_b, = fetch([(down_weight, ends[2], widths[2], 0, block)], (sum_1,), "fetch_down")
    sum_2 = pair_total(keep_2, got_2, 2 * widths[2], (down_b,))
    over_2 = swap(sum_2, "tok", n_tok, 2)
    down_a, = fetch([(down_weight, 0, ends[2], 0, block)], (sum_2,), "fetch_down")

    a_own, scale = hidden_rows([(keep_0, got_0, over_0), (keep_1, got_1, over_1)], widths[:2], None, (down_a,))
    a_two = swap(a_own, "tok", n_tok, 2)
    a_one = swap(a_own, "tok", n_tok, 1)
    b_own, _ = hidden_rows([(keep_2, got_2, over_2)], widths[2:], scale, (a_one,))
    b_two = swap(b_own, "tok", n_tok, 2)
    b_one = swap(b_own, "tok", n_tok, 1)
    a_three = swap(copy_after(a_two, (b_two, b_one)), "tok", n_tok, 1)
    b_three = swap(b_two, "tok", n_tok, 1)
    hidden_a = [a_own, a_one, a_two, a_three]
    hidden_b = [b_own, b_one, b_two, b_three]

    here = [0] + chip_masks
    there = [mask + 1 for mask in here]
    first = down(hidden_a, down_a, there + here, panel, F32)
    other = down(hidden_b, down_b, there, panel, BF16, first, 0)
    other = swap(other, "hid", n_hid, 1)
    mine = down(hidden_b, down_b, here, panel, F32, first, len(there))
    summed, *sends = run(
        chip_sum_kernel, "chip_sum",
        [jax.ShapeDtypeStruct((ntok, panel), F32)] + [jax.ShapeDtypeStruct((ntok, panel), BF16)] * len(chip_masks),
        [mine, other], mine.size, 8 * mine.size,
        out_specs=[WHOLE] * len(here),
    )
    for mask, value in reversed(list(zip(chip_masks, sends))):
        summed = summed + swap(value, "hid", n_hid, mask).astype(F32)
    resid_cols = (x_cols + summed).astype(BF16)

    column = [swap(resid_cols, "tok", n_tok, d) for d in range(1, n_tok)]
    across = swap(resid_cols, "hid", n_hid, 6)
    across_line = [swap(across, "tok", n_tok, d) for d in range(1, n_tok)]
    line = stack_after([resid_cols, *column], (across_line[0],))
    beside = [swap(line, "hid", n_hid, mask) for mask in (2, 4)]
    line_far = swap(line, "hid", n_hid, 1)
    across_far = swap(across, "hid", n_hid, 1)
    line_slots = [[(d, mask) for d in range(n_tok)] for mask in range(n_hid)]
    gram, cross = gram_part(
        resid_cols, [line, line_far, across[None], across_far[None]],
        [line_slots[0], line_slots[1], [(0, 6)], [(0, 7)]], n_tok, n_hid, None, labels,
    )
    done = pltpu.with_memory_space_constraint(gram, pltpu.HBM)
    near = stack_after([*beside, *across_line], (done,))
    far = swap(near, "hid", n_hid, 1)
    for stack, core in ((near, 0), (far, 1)):
        slots = line_slots[2 + core] + line_slots[4 + core] + line_slots[6 + core][1:]
        gram, = gram_part(resid_cols, [stack], [slots], n_tok, n_hid, gram)
    return (gram, cross.T)


def plain(n_tok, n_hid, resid_in, norm_gain, gate_weight, up_weight, down_weight, labels):
    x = lax.all_gather(resid_in, "hid", axis=0, tiled=True).astype(F32)
    ntok, block = x.shape
    total_sq = lax.psum(jnp.sum(x * x, axis=1), "tok")
    normed = (x * lax.rsqrt(total_sq / float(D) + 1e-05)[:, None] * norm_gain[None, :]).astype(BF16)

    def summed_over_tok(weight):
        product = jnp.dot(normed, weight, preferred_element_type=F32).astype(BF16)
        return lax.psum_scatter(product, "tok", scatter_dimension=0, tiled=True).astype(F32)

    hidden = (jax.nn.silu(summed_over_tok(gate_weight)) * summed_over_tok(up_weight)).astype(BF16)
    hidden = lax.all_gather(hidden, "tok", axis=0, tiled=True)
    partial_out = jnp.dot(hidden, down_weight, preferred_element_type=F32).astype(BF16)
    summed = lax.psum_scatter(partial_out, "hid", scatter_dimension=1, tiled=True).astype(F32)
    panel = block // n_hid
    x_cols = lax.dynamic_slice_in_dim(x, lax.axis_index("hid") * panel, panel, 1)
    resid_cols = (x_cols + summed).astype(BF16)
    everyone = lax.all_gather(resid_cols, ("tok", "hid"), axis=1, tiled=True)
    gram = lax.dot_general(
        resid_cols, everyone, (((0,), (0,)), ((), ())), preferred_element_type=F32
    ) / float(ntok)
    return (gram, class_means(resid_cols, labels))


def on_device(n_tok, n_hid, resid_in, norm_gain, gate_weight, *rest):
    panel = resid_in.shape[1] // n_hid
    fits = n_tok == 4 and n_hid == 8 and panel % 128 == 0 and gate_weight.shape[1] % TILE == 0 and gate_weight.shape[1] >= 3 * TILE
    body = on_line if fits else plain
    return body(n_tok, n_hid, resid_in, norm_gain, gate_weight, *rest)


def solution(mesh):
    return jax.shard_map(
        functools.partial(on_device, mesh.shape["tok"], mesh.shape["hid"]),
        mesh=mesh,
        in_specs=(
            P("hid", "tok"),
            P("tok"),
            P("tok", "hid"),
            P("tok", "hid"),
            P("hid", "tok"),
            P(),
        ),
        out_specs=(P(("tok", "hid"), None), P(("tok", "hid"), None)),
        check_vma=False,
    )
```

```python
import functools
import jax
import jax.numpy as jnp
from jax import lax
from jax.experimental import pallas as pl
from jax.experimental.pallas import tpu as pltpu
from jax.sharding import PartitionSpec as P

D = 8192
CLASSES = 64
TILE = 256
BF16 = jnp.bfloat16
F32 = jnp.float32
WHOLE = pl.BlockSpec(memory_space=pltpu.VMEM)
ANYWHERE = pl.BlockSpec(memory_space=pl.ANY)
SIDE = 128


def swap(value, axis, size, mask):
    return lax.ppermute(value, axis, [(i, i ^ mask) for i in range(size)])


def run(body, name, out_shape, operands, flops, bytes_accessed, in_specs=None, out_specs=WHOLE, **more):
    return pl.pallas_call(
        body,
        out_shape=out_shape,
        in_specs=[WHOLE] * len(operands) if in_specs is None else in_specs,
        out_specs=out_specs,
        compiler_params=pltpu.CompilerParams(vmem_limit_bytes=16 * 1024 * 1024),
        cost_estimate=pl.CostEstimate(flops=flops, bytes_accessed=bytes_accessed, transcendentals=0),
        name=name,
        **more,
    )(*operands)


def fetch(pieces, after, name):
    count = len(pieces)
    copies = []
    for number, (array, row, rows, column, columns) in enumerate(pieces):
        step = min(rows, 256)
        copies += [(number, at, step, row + at, column, columns) for at in range(0, rows, step)]

    def body(*refs):
        sources, targets, sems = refs[:count], refs[-1 - count:-1], refs[-1]
        started = []
        for sem, (number, at, step, row, column, columns) in enumerate(copies):
            copy = pltpu.make_async_copy(
                sources[number].at[pl.ds(row, step), pl.ds(column, columns)],
                targets[number].at[pl.ds(at, step), :],
                sems.at[sem],
            )
            copy.start()
            started.append(copy)
        for copy in started:
            copy.wait()

    size = sum(rows * columns * array.dtype.itemsize for array, _, rows, _, columns in pieces)
    return run(
        body, name,
        [pltpu.VMEM((rows, columns), array.dtype) for array, _, rows, _, columns in pieces],
        [pltpu.with_memory_space_constraint(piece[0], pltpu.HBM) for piece in pieces] + list(after),
        0, 0,
        in_specs=[ANYWHERE] * (count + len(after)),
        out_specs=[WHOLE] * count,
        scratch_shapes=[pltpu.SemaphoreType.DMA((len(copies),))],
    )


def tokens_kernel(masks, panel, *refs):
    blocks, gain, (lhs, cols, squares, x) = refs[:len(masks)], refs[len(masks)], refs[-4:]
    h = lax.axis_index("hid")
    rows = blocks[0].shape[0]
    for mask, block in zip(masks, blocks):
        x[pl.ds(pl.multiple_of((h ^ mask) * rows, rows), rows), :] = block[...]
    values = x[...].astype(F32)
    lhs[...] = (values * gain[...]).astype(BF16)
    squares[...] = jnp.sum(values * values, axis=1, keepdims=True)
    cols[...] = x[:, pl.ds(pl.multiple_of(h * panel, panel), panel)].astype(F32)


def split(value):
    lane = lax.broadcasted_iota(jnp.int32, (value.shape[0], SIDE), 1)
    out = jnp.zeros((value.shape[0], SIDE), F32)
    for part in range(3):
        rounded = value.astype(BF16).astype(F32)
        out = jnp.where(lane == part, rounded, out)
        value = value - rounded
    return out


def joined(parts):
    return jnp.sum(parts.astype(F32), axis=1, keepdims=True)


def gate_up_kernel(lhs_ref, gate_ref, up_ref, *refs):
    send_ref, keep_ref, both, side = refs[-4:]
    places = ((keep_ref, 0), (send_ref, 0), (keep_ref, 1), (send_ref, 1))
    rows = send_ref.shape[1]
    z = lax.axis_index("tok")
    lhs = lhs_ref[...]

    def hand_out(source, start, width):
        for d, (out, slot) in enumerate(places):
            at = pl.multiple_of((z ^ d) * rows, rows)
            out[slot, :, start:start + width] = source[pl.ds(at, rows), :].astype(BF16)

    for tile in range(gate_ref.shape[1] // TILE):
        cols = slice(tile * TILE, (tile + 1) * TILE)
        both[:, :TILE] = jnp.dot(lhs, gate_ref[:, cols], preferred_element_type=F32)
        both[:, TILE:] = jnp.dot(lhs, up_ref[:, cols], preferred_element_type=F32)
        hand_out(both, 2 * tile * TILE, 2 * TILE)
    if send_ref.shape[2] > 2 * gate_ref.shape[1]:
        side[...] = split(refs[0][...])
        hand_out(side, 2 * gate_ref.shape[1], SIDE)


def gate_up(lhs, gate, up, squares, n_tok, after=()):
    ntok, depth = lhs.shape
    width = gate.shape[1]
    rows = ntok // n_tok
    extra = [] if squares is None else [squares]
    shape = jax.ShapeDtypeStruct((2, rows, 2 * width + SIDE * len(extra)), BF16)
    return run(
        gate_up_kernel, "gate_up", [shape, shape], [lhs, gate, up, *extra, *after],
        0, 0,
        in_specs=[WHOLE] * (3 + len(extra)) + [ANYWHERE] * len(after),
        out_specs=[WHOLE] * 2,
        scratch_shapes=[pltpu.VMEM((ntok, 2 * TILE), F32), pltpu.VMEM((ntok, SIDE), F32)],
    )


def gate_up_from_hbm(lhs, gate_part, up_part, n_tok, after):
    ntok, depth = lhs.shape
    start, width = gate_part[3:]
    rows = ntok // n_tok
    tiles = width // TILE

    def body(lhs_ref, gate_hbm, up_hbm, *refs):
        send_ref, keep_ref, gate_ref, up_ref, both, sems = refs[-6:]
        places = ((keep_ref, 0), (send_ref, 0), (keep_ref, 1), (send_ref, 1))
        z = lax.axis_index("tok")
        copies = []
        for tile in range(tiles):
            for number, (source, target) in enumerate(((gate_hbm, gate_ref), (up_hbm, up_ref))):
                copy = pltpu.make_async_copy(
                    source.at[:, pl.ds(start + tile * TILE, TILE)], target.at[tile], sems.at[2 * tile + number]
                )
                copy.start()
                copies.append(copy)
        values = lhs_ref[...]
        for tile in range(tiles):
            copies[2 * tile].wait()
            both[:, :TILE] = jnp.dot(values, gate_ref[tile], preferred_element_type=F32)
            copies[2 * tile + 1].wait()
            both[:, TILE:] = jnp.dot(values, up_ref[tile], preferred_element_type=F32)
            for d, (out, slot) in enumerate(places):
                at = pl.multiple_of((z ^ d) * rows, rows)
                out[slot, :, 2 * tile * TILE:2 * (tile + 1) * TILE] = both[pl.ds(at, rows), :].astype(BF16)

    shape = jax.ShapeDtypeStruct((2, rows, 2 * width), BF16)
    in_hbm = [pltpu.with_memory_space_constraint(part[0], pltpu.HBM) for part in (gate_part, up_part)]
    return run(
        body, "gate_up_from_hbm", [shape, shape], [lhs, *in_hbm, *after], 0, 0,
        in_specs=[WHOLE] + [ANYWHERE] * (2 + len(after)),
        out_specs=[WHOLE] * 2,
        scratch_shapes=[
            pltpu.VMEM((tiles, depth, TILE), BF16),
            pltpu.VMEM((tiles, depth, TILE), BF16),
            pltpu.VMEM((ntok, 2 * TILE), F32),
            pltpu.SemaphoreType.DMA((2 * tiles,)),
        ],
    )


def pair_total(keep, got, main, after):
    def body(keep_ref, got_ref, *refs):
        out = refs[-1]
        out[:, :main] = (keep_ref[1, :, :main].astype(F32) + got_ref[1, :, :main].astype(F32)).astype(BF16)
        if out.shape[1] > main:
            out[:, main:] = split(joined(keep_ref[1, :, main:]) + joined(got_ref[1, :, main:])).astype(BF16)

    size = keep.size // 2
    return run(
        body, "pair_total", jax.ShapeDtypeStruct(keep.shape[1:], BF16), [keep, got, *after],
        size, 6 * size, in_specs=[WHOLE] * 2 + [ANYWHERE] * len(after),
    )


def copy_after(value, after):
    def body(value_ref, *refs):
        refs[-1][...] = value_ref[...]

    return run(
        body, "copy", jax.ShapeDtypeStruct(value.shape, value.dtype), [value, *after],
        0, 4 * value.size, in_specs=[WHOLE] + [ANYWHERE] * len(after),
    )


def stack_after(blocks, after):
    stacks = [block if block.ndim == 3 else block[None] for block in blocks]
    total = sum(stack.shape[0] for stack in stacks)

    def body(*refs):
        at = 0
        for ref in refs[:len(stacks)]:
            refs[-1][at:at + ref.shape[0]] = ref[...]
            at += ref.shape[0]

    shape = jax.ShapeDtypeStruct((total, *stacks[0].shape[1:]), blocks[0].dtype)
    return run(
        body, "stack", shape, [*stacks, *after], 0, 4 * sum(stack.size for stack in stacks),
        in_specs=[WHOLE] * len(stacks) + [ANYWHERE] * len(after),
    )


def hidden_rows(chunks, widths, scale, after):
    rows = chunks[0][0].shape[1]
    given = [] if scale is None else [scale]

    def body(*refs):
        out_ref, scale_ref = refs[-2:]
        keep_ref, got_ref, over_ref = refs[:3]
        if scale is None:
            tail = slice(2 * widths[0], 2 * widths[0] + SIDE)
            squares = joined(keep_ref[0, :, tail]) + joined(got_ref[0, :, tail]) + joined(over_ref[:, tail])
            factor = lax.rsqrt(squares / float(D) + 1e-05)
        else:
            factor = refs[3 * len(chunks)][...]
        scale_ref[...] = factor
        start = 0
        for k, width in enumerate(widths):
            keep_ref, got_ref, over_ref = refs[3 * k:3 * k + 3]

            def total(at):
                cols = slice(at, at + TILE)
                return (
                    keep_ref[0, :, cols].astype(F32) + got_ref[0, :, cols].astype(F32) + over_ref[:, cols].astype(F32)
                ) * factor

            for at in range(0, width, TILE):
                gate, up = total(2 * at), total(2 * at + TILE)
                out_ref[:, start + at:start + at + TILE] = (jax.nn.silu(gate) * up).astype(BF16)
            start += width

    size = rows * sum(widths)
    return run(
        body, "hidden",
        [jax.ShapeDtypeStruct((rows, sum(widths)), BF16), jax.ShapeDtypeStruct((rows, 1), F32)],
        [part for chunk in chunks for part in chunk] + given + list(after), 20 * size, 14 * size,
        in_specs=[WHOLE] * (3 * len(chunks) + len(given)) + [ANYWHERE] * len(after),
        out_specs=[WHOLE] * 2,
    )


def down_kernel(masks, skip, panel, n_blocks, *refs):
    blocks, weight, lhs, out = refs[:n_blocks], refs[n_blocks], refs[-1], refs[-2]
    before = refs[n_blocks + 1] if len(refs) == n_blocks + 4 else None
    z = lax.axis_index("tok")
    h = lax.axis_index("hid")
    rows = blocks[0].shape[0]
    for d, block in enumerate(blocks):
        lhs[pl.ds(pl.multiple_of((z ^ d) * rows, rows), rows), :] = block[...]
    values = lhs[...]
    for slot, mask in enumerate(masks):
        column = pl.multiple_of((h ^ mask) * panel, panel)
        total = jnp.dot(values, weight[:, pl.ds(column, panel)], preferred_element_type=F32)
        if before is not None:
            total = total + before[skip + slot]
        out[slot] = total.astype(out.dtype)


def down(blocks, weight, masks, panel, kind, before=None, skip=0):
    rows, depth = blocks[0].shape
    ntok = rows * len(blocks)
    return run(
        functools.partial(down_kernel, masks, skip, panel, len(blocks)), "down",
        jax.ShapeDtypeStruct((len(masks), ntok, panel), kind),
        [*blocks, weight] + ([] if before is None else [before]),
        2 * ntok * depth * panel * len(masks), 2 * depth * panel * len(masks),
        scratch_shapes=[pltpu.VMEM((ntok, depth), BF16)],
    )


def chip_sum_kernel(mine_ref, other_ref, own_ref, *outs):
    own_ref[...] = mine_ref[0] + other_ref[0].astype(F32)
    for e, out in enumerate(outs):
        out[...] = (mine_ref[e + 1] + other_ref[e + 1].astype(F32)).astype(BF16)


def gram_kernel(slots, n_hid, ntok, classes, own_ref, *refs):
    stacks = refs[:len(slots)]
    outs, (tiles, sems) = refs[:-2], refs[-2:]
    out_ref = outs[-2] if classes else outs[-1]
    z = lax.axis_index("tok")
    h = lax.axis_index("hid")
    width = own_ref.shape[1]
    left = own_ref[...].T
    copies = []
    for stack, places in zip(stacks, slots):
        for at, (d, mask) in enumerate(places):
            number = len(copies)
            tiles[number] = jnp.dot(left, stack[at], preferred_element_type=F32) * (1.0 / ntok)
            column = ((z ^ d) * n_hid + (h ^ mask)) * width
            copy = pltpu.make_async_copy(
                tiles.at[number], out_ref.at[:, pl.ds(pl.multiple_of(column, width), width)], sems.at[number]
            )
            copy.start()
            copies.append(copy)
    if classes:
        labels, cross_ref = refs[len(slots)], outs[-1]
        onehot = (labels[...] == lax.broadcasted_iota(jnp.int32, (classes, ntok), 0)).astype(F32)
        counts = jnp.sum(onehot, axis=1, keepdims=True)
        sums = jnp.dot(onehot.astype(BF16), own_ref[...], preferred_element_type=F32)
        cross_ref[...] = sums / jnp.maximum(counts, 1.0)
    for copy in copies:
        copy.wait()


def gram_part(resid_cols, stacks, slots, n_tok, n_hid, before, labels=None):
    ntok, width = resid_cols.shape
    here = sum(len(places) for places in slots)
    gram_shape = pltpu.HBM((width, width * n_tok * n_hid), F32)
    extra, extra_specs = ([], []) if labels is None else ([labels[None, :]], [WHOLE])
    if before is not None:
        extra, extra_specs = extra + [before], extra_specs + [ANYWHERE]
    return run(
        functools.partial(gram_kernel, slots, n_hid, ntok, 0 if labels is None else CLASSES), "gram",
        [gram_shape] + ([] if labels is None else [jax.ShapeDtypeStruct((CLASSES, width), F32)]),
        [resid_cols, *stacks, *extra],
        2 * ntok * width * width * here, 4 * width * width * here,
        in_specs=[WHOLE] * (1 + len(stacks)) + extra_specs,
        out_specs=[ANYWHERE] + ([] if labels is None else [WHOLE]),
        input_output_aliases={} if before is None else {len(stacks) + len(extra): 0},
        scratch_shapes=[pltpu.VMEM((here, width, width), F32), pltpu.SemaphoreType.DMA((here,))],
    )


def class_means(resid_cols, labels):
    onehot = (labels[:, None] == jnp.arange(CLASSES, dtype=jnp.int32)[None, :]).astype(BF16)
    counts = jnp.sum(onehot.astype(F32), axis=0)
    class_sums = lax.dot_general(
        resid_cols, onehot, (((0,), (0,)), ((), ())), preferred_element_type=F32
    )
    return class_sums / jnp.maximum(counts, 1.0)[None, :]


def on_line(n_tok, n_hid, resid_in, norm_gain, gate_weight, up_weight, down_weight, labels):
    rows, block = resid_in.shape
    ntok, panel = rows * n_hid, block // n_hid
    depth, shard_ff = gate_weight.shape
    tiles = shard_ff // TILE
    ends = [TILE * (tiles * k // 3) for k in range(4)]
    chip_masks = list(range(2, n_hid, 2))

    def part(weight, k):
        return weight, 0, depth, ends[k], ends[k + 1] - ends[k]

    near = [resid_in] + [swap(resid_in, "hid", n_hid, mask) for mask in chip_masks]
    gate_0, up_0, own_x, gain = fetch(
        [
            part(gate_weight, 0),
            part(up_weight, 0),
            (resid_in, 0, rows, 0, block),
            (norm_gain[None, :], 0, 1, 0, block),
        ],
        (), "fetch_first",
    )
    relayed = copy_after(near[1], (gain,))
    far = [swap(piece, "hid", n_hid, 1) for piece in [near[0], relayed, *near[2:]]]
    masks = [0] + chip_masks + [1] + [mask + 1 for mask in chip_masks]
    lhs, x_cols, squares = run(
        functools.partial(tokens_kernel, masks, panel), "tokens",
        (
            jax.ShapeDtypeStruct((ntok, block), BF16),
            jax.ShapeDtypeStruct((ntok, panel), F32),
            jax.ShapeDtypeStruct((ntok, 1), F32),
        ),
        [own_x, *near[1:], *far, gain],
        4 * ntok * block, 4 * ntok * block,
        out_specs=(WHOLE, WHOLE, WHOLE),
        scratch_shapes=[pltpu.VMEM((ntok, block), BF16)],
    )

    widths = [ends[k + 1] - ends[k] for k in range(3)]
    send_0, keep_0 = gate_up(lhs, gate_0, up_0, squares, n_tok)
    got_0 = swap(send_0, "tok", n_tok, 1)
    send_1, keep_1 = gate_up_from_hbm(lhs, part(gate_weight, 1), part(up_weight, 1), n_tok, (send_0,))
    got_1 = swap(send_1, "tok", n_tok, 1)
    sum_0 = pair_total(keep_0, got_0, 2 * widths[0], (send_1,))
    over_0 = swap(sum_0, "tok", n_tok, 2)
    send_2, keep_2 = gate_up_from_hbm(lhs, part(gate_weight, 2), part(up_weight, 2), n_tok, (sum_0,))
    got_2 = swap(send_2, "tok", n_tok, 1)
    sum_1 = pair_total(keep_1, got_1, 2 * widths[1], (send_2,))
    over_1 = swap(sum_1, "tok", n_tok, 2)
    down_b, = fetch([(down_weight, ends[2], widths[2], 0, block)], (sum_1,), "fetch_down")
    sum_2 = pair_total(keep_2, got_2, 2 * widths[2], (down_b,))
    over_2 = swap(sum_2, "tok", n_tok, 2)
    down_a, = fetch([(down_weight, 0, ends[2], 0, block)], (sum_2,), "fetch_down")

    a_own, scale = hidden_rows([(keep_0, got_0, over_0), (keep_1, got_1, over_1)], widths[:2], None, (down_a,))
    a_two = swap(a_own, "tok", n_tok, 2)
    a_one = swap(a_own, "tok", n_tok, 1)
    b_own, _ = hidden_rows([(keep_2, got_2, over_2)], widths[2:], scale, ())
    b_two = swap(b_own, "tok", n_tok, 2)
    b_one = swap(b_own, "tok", n_tok, 1)
    a_three = swap(copy_after(a_two, (b_own,)), "tok", n_tok, 1)
    b_three = swap(b_two, "tok", n_tok, 1)
    hidden_a = [a_own, a_one, a_two, a_three]
    hidden_b = [b_own, b_one, b_two, b_three]

    here = [0] + chip_masks
    there = [mask + 1 for mask in here]
    first = down(hidden_a, down_a, there + here, panel, F32)
    other = down(hidden_b, down_b, there, panel, BF16, first, 0)
    other = swap(other, "hid", n_hid, 1)
    mine = down(hidden_b, down_b, here, panel, F32, first, len(there))
    summed, *sends = run(
        chip_sum_kernel, "chip_sum",
        [jax.ShapeDtypeStruct((ntok, panel), F32)] + [jax.ShapeDtypeStruct((ntok, panel), BF16)] * len(chip_masks),
        [mine, other], mine.size, 8 * mine.size,
        out_specs=[WHOLE] * len(here),
    )
    for mask, value in reversed(list(zip(chip_masks, sends))):
        summed = summed + swap(value, "hid", n_hid, mask).astype(F32)
    resid_cols = (x_cols + summed).astype(BF16)

    column = [swap(resid_cols, "tok", n_tok, d) for d in range(1, n_tok)]
    across = swap(resid_cols, "hid", n_hid, 6)
    line = stack_after([resid_cols, *column], (across,))
    beside = [swap(line, "hid", n_hid, mask) for mask in (2, 4)]
    across_line = [swap(across, "tok", n_tok, d) for d in range(1, n_tok)]
    line_far = swap(line, "hid", n_hid, 1)
    across_far = swap(across, "hid", n_hid, 1)
    line_slots = [[(d, mask) for d in range(n_tok)] for mask in range(n_hid)]
    gram, cross = gram_part(
        resid_cols, [line, line_far, across[None], across_far[None]],
        [line_slots[0], line_slots[1], [(0, 6)], [(0, 7)]], n_tok, n_hid, None, labels,
    )
    done = pltpu.with_memory_space_constraint(gram, pltpu.HBM)
    near = stack_after([*beside, *across_line], (done,))
    far = swap(near, "hid", n_hid, 1)
    for stack, core in ((near, 0), (far, 1)):
        slots = line_slots[2 + core] + line_slots[4 + core] + line_slots[6 + core][1:]
        gram, = gram_part(resid_cols, [stack], [slots], n_tok, n_hid, gram)
    return (gram, cross.T)


def plain(n_tok, n_hid, resid_in, norm_gain, gate_weight, up_weight, down_weight, labels):
    x = lax.all_gather(resid_in, "hid", axis=0, tiled=True).astype(F32)
    ntok, block = x.shape
    total_sq = lax.psum(jnp.sum(x * x, axis=1), "tok")
    normed = (x * lax.rsqrt(total_sq / float(D) + 1e-05)[:, None] * norm_gain[None, :]).astype(BF16)

    def summed_over_tok(weight):
        product = jnp.dot(normed, weight, preferred_element_type=F32).astype(BF16)
        return lax.psum_scatter(product, "tok", scatter_dimension=0, tiled=True).astype(F32)

    hidden = (jax.nn.silu(summed_over_tok(gate_weight)) * summed_over_tok(up_weight)).astype(BF16)
    hidden = lax.all_gather(hidden, "tok", axis=0, tiled=True)
    partial_out = jnp.dot(hidden, down_weight, preferred_element_type=F32).astype(BF16)
    summed = lax.psum_scatter(partial_out, "hid", scatter_dimension=1, tiled=True).astype(F32)
    panel = block // n_hid
    x_cols = lax.dynamic_slice_in_dim(x, lax.axis_index("hid") * panel, panel, 1)
    resid_cols = (x_cols + summed).astype(BF16)
    everyone = lax.all_gather(resid_cols, ("tok", "hid"), axis=1, tiled=True)
    gram = lax.dot_general(
        resid_cols, everyone, (((0,), (0,)), ((), ())), preferred_element_type=F32
    ) / float(ntok)
    return (gram, class_means(resid_cols, labels))


def on_device(n_tok, n_hid, resid_in, norm_gain, gate_weight, *rest):
    panel = resid_in.shape[1] // n_hid
    fits = n_tok == 4 and n_hid == 8 and panel % 128 == 0 and gate_weight.shape[1] % TILE == 0 and gate_weight.shape[1] >= 3 * TILE
    body = on_line if fits else plain
    return body(n_tok, n_hid, resid_in, norm_gain, gate_weight, *rest)


def solution(mesh):
    return jax.shard_map(
        functools.partial(on_device, mesh.shape["tok"], mesh.shape["hid"]),
        mesh=mesh,
        in_specs=(
            P("hid", "tok"),
            P("tok"),
            P("tok", "hid"),
            P("tok", "hid"),
            P("hid", "tok"),
            P(),
        ),
        out_specs=(P(("tok", "hid"), None), P(("tok", "hid"), None)),
        check_vma=False,
    )
```

```python
import functools
import jax
import jax.numpy as jnp
from jax import lax
from jax.experimental import pallas as pl
from jax.experimental.pallas import tpu as pltpu
from jax.sharding import PartitionSpec as P

D = 8192
CLASSES = 64
TILE = 256
BF16 = jnp.bfloat16
F32 = jnp.float32
WHOLE = pl.BlockSpec(memory_space=pltpu.VMEM)
ANYWHERE = pl.BlockSpec(memory_space=pl.ANY)
SIDE = 128


def swap(value, axis, size, mask):
    return lax.ppermute(value, axis, [(i, i ^ mask) for i in range(size)])


def run(body, name, out_shape, operands, flops, bytes_accessed, in_specs=None, out_specs=WHOLE, **more):
    return pl.pallas_call(
        body,
        out_shape=out_shape,
        in_specs=[WHOLE] * len(operands) if in_specs is None else in_specs,
        out_specs=out_specs,
        compiler_params=pltpu.CompilerParams(vmem_limit_bytes=16 * 1024 * 1024),
        cost_estimate=pl.CostEstimate(flops=flops, bytes_accessed=bytes_accessed, transcendentals=0),
        name=name,
        **more,
    )(*operands)


def fetch(pieces, after, name):
    count = len(pieces)
    copies = []
    for number, (array, row, rows, column, columns) in enumerate(pieces):
        step = min(rows, 256)
        copies += [(number, at, step, row + at, column, columns) for at in range(0, rows, step)]

    def body(*refs):
        sources, targets, sems = refs[:count], refs[-1 - count:-1], refs[-1]
        started = []
        for sem, (number, at, step, row, column, columns) in enumerate(copies):
            copy = pltpu.make_async_copy(
                sources[number].at[pl.ds(row, step), pl.ds(column, columns)],
                targets[number].at[pl.ds(at, step), :],
                sems.at[sem],
            )
            copy.start()
            started.append(copy)
        for copy in started:
            copy.wait()

    size = sum(rows * columns * array.dtype.itemsize for array, _, rows, _, columns in pieces)
    return run(
        body, name,
        [pltpu.VMEM((rows, columns), array.dtype) for array, _, rows, _, columns in pieces],
        [pltpu.with_memory_space_constraint(piece[0], pltpu.HBM) for piece in pieces] + list(after),
        0, 0,
        in_specs=[ANYWHERE] * (count + len(after)),
        out_specs=[WHOLE] * count,
        scratch_shapes=[pltpu.SemaphoreType.DMA((len(copies),))],
    )


def tokens_kernel(masks, panel, *refs):
    blocks, gain, (lhs, cols, squares, x) = refs[:len(masks)], refs[len(masks)], refs[-4:]
    h = lax.axis_index("hid")
    rows = blocks[0].shape[0]
    for mask, block in zip(masks, blocks):
        x[pl.ds(pl.multiple_of((h ^ mask) * rows, rows), rows), :] = block[...]
    values = x[...].astype(F32)
    lhs[...] = (values * gain[...]).astype(BF16)
    squares[...] = jnp.sum(values * values, axis=1, keepdims=True)
    cols[...] = x[:, pl.ds(pl.multiple_of(h * panel, panel), panel)].astype(F32)


def split(value):
    lane = lax.broadcasted_iota(jnp.int32, (value.shape[0], SIDE), 1)
    out = jnp.zeros((value.shape[0], SIDE), F32)
    for part in range(3):
        rounded = value.astype(BF16).astype(F32)
        out = jnp.where(lane == part, rounded, out)
        value = value - rounded
    return out


def joined(parts):
    return jnp.sum(parts.astype(F32), axis=1, keepdims=True)


def gate_up_kernel(lhs_ref, gate_ref, up_ref, *refs):
    send_ref, keep_ref, both, side = refs[-4:]
    places = ((keep_ref, 0), (send_ref, 0), (keep_ref, 1), (send_ref, 1))
    rows = send_ref.shape[1]
    z = lax.axis_index("tok")
    lhs = lhs_ref[...]

    def hand_out(source, start, width):
        for d, (out, slot) in enumerate(places):
            at = pl.multiple_of((z ^ d) * rows, rows)
            out[slot, :, start:start + width] = source[pl.ds(at, rows), :].astype(BF16)

    for tile in range(gate_ref.shape[1] // TILE):
        cols = slice(tile * TILE, (tile + 1) * TILE)
        both[:, :TILE] = jnp.dot(lhs, gate_ref[:, cols], preferred_element_type=F32)
        both[:, TILE:] = jnp.dot(lhs, up_ref[:, cols], preferred_element_type=F32)
        hand_out(both, 2 * tile * TILE, 2 * TILE)
    if send_ref.shape[2] > 2 * gate_ref.shape[1]:
        side[...] = split(refs[0][...])
        hand_out(side, 2 * gate_ref.shape[1], SIDE)


def gate_up(lhs, gate, up, squares, n_tok, after=()):
    ntok, depth = lhs.shape
    width = gate.shape[1]
    rows = ntok // n_tok
    extra = [] if squares is None else [squares]
    shape = jax.ShapeDtypeStruct((2, rows, 2 * width + SIDE * len(extra)), BF16)
    return run(
        gate_up_kernel, "gate_up", [shape, shape], [lhs, gate, up, *extra, *after],
        0, 0,
        in_specs=[WHOLE] * (3 + len(extra)) + [ANYWHERE] * len(after),
        out_specs=[WHOLE] * 2,
        scratch_shapes=[pltpu.VMEM((ntok, 2 * TILE), F32), pltpu.VMEM((ntok, SIDE), F32)],
    )


def pair_total(keep, got, main, after):
    def body(keep_ref, got_ref, *refs):
        out = refs[-1]
        out[:, :main] = (keep_ref[1, :, :main].astype(F32) + got_ref[1, :, :main].astype(F32)).astype(BF16)
        if out.shape[1] > main:
            out[:, main:] = split(joined(keep_ref[1, :, main:]) + joined(got_ref[1, :, main:])).astype(BF16)

    size = keep.size // 2
    return run(
        body, "pair_total", jax.ShapeDtypeStruct(keep.shape[1:], BF16), [keep, got, *after],
        size, 6 * size, in_specs=[WHOLE] * 2 + [ANYWHERE] * len(after),
    )


def copy_after(value, after):
    def body(value_ref, *refs):
        refs[-1][...] = value_ref[...]

    return run(
        body, "copy", jax.ShapeDtypeStruct(value.shape, value.dtype), [value, *after],
        0, 4 * value.size, in_specs=[WHOLE] + [ANYWHERE] * len(after),
    )


def stack_after(blocks, after):
    stacks = [block if block.ndim == 3 else block[None] for block in blocks]
    total = sum(stack.shape[0] for stack in stacks)

    def body(*refs):
        at = 0
        for ref in refs[:len(stacks)]:
            refs[-1][at:at + ref.shape[0]] = ref[...]
            at += ref.shape[0]

    shape = jax.ShapeDtypeStruct((total, *stacks[0].shape[1:]), blocks[0].dtype)
    return run(
        body, "stack", shape, [*stacks, *after], 0, 4 * sum(stack.size for stack in stacks),
        in_specs=[WHOLE] * len(stacks) + [ANYWHERE] * len(after),
    )


def hidden_rows(chunks, widths, scale, after):
    rows = chunks[0][0].shape[1]
    given = [] if scale is None else [scale]

    def body(*refs):
        out_ref, scale_ref = refs[-2:]
        keep_ref, got_ref, over_ref = refs[:3]
        if scale is None:
            tail = slice(2 * widths[0], 2 * widths[0] + SIDE)
            squares = joined(keep_ref[0, :, tail]) + joined(got_ref[0, :, tail]) + joined(over_ref[:, tail])
            factor = lax.rsqrt(squares / float(D) + 1e-05)
        else:
            factor = refs[3 * len(chunks)][...]
        scale_ref[...] = factor
        start = 0
        for k, width in enumerate(widths):
            keep_ref, got_ref, over_ref = refs[3 * k:3 * k + 3]

            def total(at):
                cols = slice(at, at + TILE)
                return (
                    keep_ref[0, :, cols].astype(F32) + got_ref[0, :, cols].astype(F32) + over_ref[:, cols].astype(F32)
                ) * factor

            for at in range(0, width, TILE):
                gate, up = total(2 * at), total(2 * at + TILE)
                out_ref[:, start + at:start + at + TILE] = (jax.nn.silu(gate) * up).astype(BF16)
            start += width

    size = rows * sum(widths)
    return run(
        body, "hidden",
        [jax.ShapeDtypeStruct((rows, sum(widths)), BF16), jax.ShapeDtypeStruct((rows, 1), F32)],
        [part for chunk in chunks for part in chunk] + given + list(after), 20 * size, 14 * size,
        in_specs=[WHOLE] * (3 * len(chunks) + len(given)) + [ANYWHERE] * len(after),
        out_specs=[WHOLE] * 2,
    )


def down_kernel(masks, panel, n_blocks, add, *refs):
    blocks, weight, lhs, out = refs[:n_blocks], refs[n_blocks], refs[-1], refs[-2]
    before = refs[n_blocks + 1] if add else None
    z = lax.axis_index("tok")
    h = lax.axis_index("hid")
    rows = blocks[0].shape[0]
    for d, block in enumerate(blocks):
        lhs[pl.ds(pl.multiple_of((z ^ d) * rows, rows), rows), :] = block[...]
    values = lhs[...]
    for slot, mask in enumerate(masks):
        column = pl.multiple_of((h ^ mask) * panel, panel)
        total = jnp.dot(values, weight[:, pl.ds(column, panel)], preferred_element_type=F32)
        if before is not None:
            total = total + before[slot]
        out[slot] = total.astype(out.dtype)


def down(blocks, weight, masks, panel, kind, before=None, after=()):
    rows, depth = blocks[0].shape
    ntok = rows * len(blocks)
    return run(
        functools.partial(down_kernel, masks, panel, len(blocks), before is not None), "down",
        jax.ShapeDtypeStruct((len(masks), ntok, panel), kind),
        [*blocks, weight] + ([] if before is None else [before]) + list(after),
        2 * ntok * depth * panel * len(masks), 2 * depth * panel * len(masks),
        in_specs=[WHOLE] * (len(blocks) + 1 + (before is not None)) + [ANYWHERE] * len(after),
        scratch_shapes=[pltpu.VMEM((ntok, depth), BF16)],
    )


def chip_sum_kernel(mine_ref, other_ref, own_ref, *outs):
    own_ref[...] = mine_ref[0] + other_ref[0].astype(F32)
    for e, out in enumerate(outs):
        out[...] = (mine_ref[e + 1] + other_ref[e + 1].astype(F32)).astype(BF16)


def gram_kernel(slots, n_hid, ntok, classes, own_ref, *refs):
    stacks = refs[:len(slots)]
    outs, (tiles, sems) = refs[:-2], refs[-2:]
    out_ref = outs[-2] if classes else outs[-1]
    z = lax.axis_index("tok")
    h = lax.axis_index("hid")
    width = own_ref.shape[1]
    left = own_ref[...].T
    copies = []
    for stack, places in zip(stacks, slots):
        for at, (d, mask) in enumerate(places):
            number = len(copies)
            tiles[number] = jnp.dot(left, stack[at], preferred_element_type=F32) * (1.0 / ntok)
            column = ((z ^ d) * n_hid + (h ^ mask)) * width
            copy = pltpu.make_async_copy(
                tiles.at[number], out_ref.at[:, pl.ds(pl.multiple_of(column, width), width)], sems.at[number]
            )
            copy.start()
            copies.append(copy)
    if classes:
        labels, cross_ref = refs[len(slots)], outs[-1]
        onehot = (labels[...] == lax.broadcasted_iota(jnp.int32, (classes, ntok), 0)).astype(F32)
        counts = jnp.sum(onehot, axis=1, keepdims=True)
        sums = jnp.dot(onehot.astype(BF16), own_ref[...], preferred_element_type=F32)
        cross_ref[...] = sums / jnp.maximum(counts, 1.0)
    for copy in copies:
        copy.wait()


def gram_part(resid_cols, stacks, slots, n_tok, n_hid, before, labels=None):
    ntok, width = resid_cols.shape
    here = sum(len(places) for places in slots)
    gram_shape = pltpu.HBM((width, width * n_tok * n_hid), F32)
    extra, extra_specs = ([], []) if labels is None else ([labels[None, :]], [WHOLE])
    if before is not None:
        extra, extra_specs = extra + [before], extra_specs + [ANYWHERE]
    return run(
        functools.partial(gram_kernel, slots, n_hid, ntok, 0 if labels is None else CLASSES), "gram",
        [gram_shape] + ([] if labels is None else [jax.ShapeDtypeStruct((CLASSES, width), F32)]),
        [resid_cols, *stacks, *extra],
        2 * ntok * width * width * here, 4 * width * width * here,
        in_specs=[WHOLE] * (1 + len(stacks)) + extra_specs,
        out_specs=[ANYWHERE] + ([] if labels is None else [WHOLE]),
        input_output_aliases={} if before is None else {len(stacks) + len(extra): 0},
        scratch_shapes=[pltpu.VMEM((here, width, width), F32), pltpu.SemaphoreType.DMA((here,))],
    )


def class_means(resid_cols, labels):
    onehot = (labels[:, None] == jnp.arange(CLASSES, dtype=jnp.int32)[None, :]).astype(BF16)
    counts = jnp.sum(onehot.astype(F32), axis=0)
    class_sums = lax.dot_general(
        resid_cols, onehot, (((0,), (0,)), ((), ())), preferred_element_type=F32
    )
    return class_sums / jnp.maximum(counts, 1.0)[None, :]


def on_line(n_tok, n_hid, resid_in, norm_gain, gate_weight, up_weight, down_weight, labels):
    rows, block = resid_in.shape
    ntok, panel = rows * n_hid, block // n_hid
    depth, shard_ff = gate_weight.shape
    tiles = shard_ff // TILE
    ends = [TILE * (tiles * k // 3) for k in range(4)]
    chip_masks = list(range(2, n_hid, 2))

    def part(weight, k):
        return weight, 0, depth, ends[k], ends[k + 1] - ends[k]

    near = [resid_in] + [swap(resid_in, "hid", n_hid, mask) for mask in chip_masks]
    gate_0, up_0, own_x, gain = fetch(
        [
            part(gate_weight, 0),
            part(up_weight, 0),
            (resid_in, 0, rows, 0, block),
            (norm_gain[None, :], 0, 1, 0, block),
        ],
        (), "fetch_first",
    )
    relayed = copy_after(near[1], (gain,))
    far = [swap(piece, "hid", n_hid, 1) for piece in [near[0], relayed, *near[2:]]]
    masks = [0] + chip_masks + [1] + [mask + 1 for mask in chip_masks]
    lhs, x_cols, squares = run(
        functools.partial(tokens_kernel, masks, panel), "tokens",
        (
            jax.ShapeDtypeStruct((ntok, block), BF16),
            jax.ShapeDtypeStruct((ntok, panel), F32),
            jax.ShapeDtypeStruct((ntok, 1), F32),
        ),
        [own_x, *near[1:], *far, gain],
        4 * ntok * block, 4 * ntok * block,
        out_specs=(WHOLE, WHOLE, WHOLE),
        scratch_shapes=[pltpu.VMEM((ntok, block), BF16)],
    )

    widths = [ends[k + 1] - ends[k] for k in range(3)]
    send_0, keep_0 = gate_up(lhs, gate_0, up_0, squares, n_tok)
    got_0 = swap(send_0, "tok", n_tok, 1)
    gate_1, up_1 = fetch([part(gate_weight, 1), part(up_weight, 1)], (send_0,), "fetch_gate_up")
    send_1, keep_1 = gate_up(lhs, gate_1, up_1, None, n_tok)
    got_1 = swap(send_1, "tok", n_tok, 1)
    sum_0 = pair_total(keep_0, got_0, 2 * widths[0], (send_1,))
    over_0 = swap(sum_0, "tok", n_tok, 2)
    gate_2, up_2 = fetch([part(gate_weight, 2), part(up_weight, 2)], (sum_0,), "fetch_gate_up")
    send_2, keep_2 = gate_up(lhs, gate_2, up_2, None, n_tok)
    got_2 = swap(send_2, "tok", n_tok, 1)
    sum_1 = pair_total(keep_1, got_1, 2 * widths[1], (send_2,))
    over_1 = swap(sum_1, "tok", n_tok, 2)
    down_b, = fetch([(down_weight, ends[2], widths[2], 0, block)], (sum_1,), "fetch_down")
    sum_2 = pair_total(keep_2, got_2, 2 * widths[2], (down_b,))
    over_2 = swap(sum_2, "tok", n_tok, 2)
    down_a, = fetch([(down_weight, 0, ends[2], 0, block)], (sum_2,), "fetch_down")

    a_own, scale = hidden_rows([(keep_0, got_0, over_0), (keep_1, got_1, over_1)], widths[:2], None, (down_a,))
    a_two = swap(a_own, "tok", n_tok, 2)
    a_one = swap(a_own, "tok", n_tok, 1)
    b_own, _ = hidden_rows([(keep_2, got_2, over_2)], widths[2:], scale, ())
    b_two = swap(b_own, "tok", n_tok, 2)
    b_one = swap(b_own, "tok", n_tok, 1)
    a_three = swap(copy_after(a_two, (b_two, b_one, a_one)), "tok", n_tok, 1)
    b_three = swap(b_two, "tok", n_tok, 1)
    hidden_a = [a_own, a_one, a_two, a_three]
    hidden_b = [b_own, b_one, b_two, b_three]

    here = [0] + chip_masks
    there = [mask + 1 for mask in here]
    other = down(hidden_b, down_b, there, panel, BF16, down(hidden_a, down_a, there, panel, F32))
    mine = down(hidden_b, down_b, here, panel, F32, down(hidden_a, down_a, here, panel, F32, after=(other,)))
    other = swap(other, "hid", n_hid, 1)
    summed, *sends = run(
        chip_sum_kernel, "chip_sum",
        [jax.ShapeDtypeStruct((ntok, panel), F32)] + [jax.ShapeDtypeStruct((ntok, panel), BF16)] * len(chip_masks),
        [mine, other], mine.size, 8 * mine.size,
        out_specs=[WHOLE] * len(here),
    )
    for mask, value in reversed(list(zip(chip_masks, sends))):
        summed = summed + swap(value, "hid", n_hid, mask).astype(F32)
    resid_cols = (x_cols + summed).astype(BF16)

    column = [swap(resid_cols, "tok", n_tok, d) for d in range(1, n_tok)]
    across = swap(resid_cols, "hid", n_hid, 6)
    line = stack_after([resid_cols, *column], (across,))
    beside = [swap(line, "hid", n_hid, mask) for mask in (2, 4)]
    across_line = [swap(across, "tok", n_tok, d) for d in range(1, n_tok)]
    line_far = swap(line, "hid", n_hid, 1)
    across_far = swap(across, "hid", n_hid, 1)
    line_slots = [[(d, mask) for d in range(n_tok)] for mask in range(n_hid)]
    gram, cross = gram_part(
        resid_cols, [line, line_far, across[None], across_far[None]],
        [line_slots[0], line_slots[1], [(0, 6)], [(0, 7)]], n_tok, n_hid, None, labels,
    )
    done = pltpu.with_memory_space_constraint(gram, pltpu.HBM)
    near = stack_after([*beside, *across_line], (done,))
    far = swap(near, "hid", n_hid, 1)
    for stack, core in ((near, 0), (far, 1)):
        slots = line_slots[2 + core] + line_slots[4 + core] + line_slots[6 + core][1:]
        gram, = gram_part(resid_cols, [stack], [slots], n_tok, n_hid, gram)
    return (gram, cross.T)


def plain(n_tok, n_hid, resid_in, norm_gain, gate_weight, up_weight, down_weight, labels):
    x = lax.all_gather(resid_in, "hid", axis=0, tiled=True).astype(F32)
    ntok, block = x.shape
    total_sq = lax.psum(jnp.sum(x * x, axis=1), "tok")
    normed = (x * lax.rsqrt(total_sq / float(D) + 1e-05)[:, None] * norm_gain[None, :]).astype(BF16)

    def summed_over_tok(weight):
        product = jnp.dot(normed, weight, preferred_element_type=F32).astype(BF16)
        return lax.psum_scatter(product, "tok", scatter_dimension=0, tiled=True).astype(F32)

    hidden = (jax.nn.silu(summed_over_tok(gate_weight)) * summed_over_tok(up_weight)).astype(BF16)
    hidden = lax.all_gather(hidden, "tok", axis=0, tiled=True)
    partial_out = jnp.dot(hidden, down_weight, preferred_element_type=F32).astype(BF16)
    summed = lax.psum_scatter(partial_out, "hid", scatter_dimension=1, tiled=True).astype(F32)
    panel = block // n_hid
    x_cols = lax.dynamic_slice_in_dim(x, lax.axis_index("hid") * panel, panel, 1)
    resid_cols = (x_cols + summed).astype(BF16)
    everyone = lax.all_gather(resid_cols, ("tok", "hid"), axis=1, tiled=True)
    gram = lax.dot_general(
        resid_cols, everyone, (((0,), (0,)), ((), ())), preferred_element_type=F32
    ) / float(ntok)
    return (gram, class_means(resid_cols, labels))


def on_device(n_tok, n_hid, resid_in, norm_gain, gate_weight, *rest):
    panel = resid_in.shape[1] // n_hid
    fits = n_tok == 4 and n_hid == 8 and panel % 128 == 0 and gate_weight.shape[1] % TILE == 0 and gate_weight.shape[1] >= 3 * TILE
    body = on_line if fits else plain
    return body(n_tok, n_hid, resid_in, norm_gain, gate_weight, *rest)


def solution(mesh):
    return jax.shard_map(
        functools.partial(on_device, mesh.shape["tok"], mesh.shape["hid"]),
        mesh=mesh,
        in_specs=(
            P("hid", "tok"),
            P("tok"),
            P("tok", "hid"),
            P("tok", "hid"),
            P("hid", "tok"),
            P(),
        ),
        out_specs=(P(("tok", "hid"), None), P(("tok", "hid"), None)),
        check_vma=False,
    )
```

```python
import functools
import jax
import jax.numpy as jnp
from jax import lax
from jax.experimental import pallas as pl
from jax.experimental.pallas import tpu as pltpu
from jax.sharding import PartitionSpec as P

D = 8192
CLASSES = 64
TILE = 256
BF16 = jnp.bfloat16
F32 = jnp.float32
WHOLE = pl.BlockSpec(memory_space=pltpu.VMEM)
ANYWHERE = pl.BlockSpec(memory_space=pl.ANY)
SIDE = 128


def swap(value, axis, size, mask):
    return lax.ppermute(value, axis, [(i, i ^ mask) for i in range(size)])


def run(body, name, out_shape, operands, flops, bytes_accessed, in_specs=None, out_specs=WHOLE, **more):
    return pl.pallas_call(
        body,
        out_shape=out_shape,
        in_specs=[WHOLE] * len(operands) if in_specs is None else in_specs,
        out_specs=out_specs,
        compiler_params=pltpu.CompilerParams(vmem_limit_bytes=16 * 1024 * 1024),
        cost_estimate=pl.CostEstimate(flops=flops, bytes_accessed=bytes_accessed, transcendentals=0),
        name=name,
        **more,
    )(*operands)


def fetch(pieces, after, name):
    count = len(pieces)
    copies = []
    for number, (array, row, rows, column, columns) in enumerate(pieces):
        step = min(rows, 256)
        copies += [(number, at, step, row + at, column, columns) for at in range(0, rows, step)]

    def body(*refs):
        sources, targets, sems = refs[:count], refs[-1 - count:-1], refs[-1]
        started = []
        for sem, (number, at, step, row, column, columns) in enumerate(copies):
            copy = pltpu.make_async_copy(
                sources[number].at[pl.ds(row, step), pl.ds(column, columns)],
                targets[number].at[pl.ds(at, step), :],
                sems.at[sem],
            )
            copy.start()
            started.append(copy)
        for copy in started:
            copy.wait()

    size = sum(rows * columns * array.dtype.itemsize for array, _, rows, _, columns in pieces)
    return run(
        body, name,
        [pltpu.VMEM((rows, columns), array.dtype) for array, _, rows, _, columns in pieces],
        [pltpu.with_memory_space_constraint(piece[0], pltpu.HBM) for piece in pieces] + list(after),
        0, 0,
        in_specs=[ANYWHERE] * (count + len(after)),
        out_specs=[WHOLE] * count,
        scratch_shapes=[pltpu.SemaphoreType.DMA((len(copies),))],
    )


def tokens_kernel(masks, panel, *refs):
    blocks, gain, (lhs, cols, squares, x) = refs[:len(masks)], refs[len(masks)], refs[-4:]
    h = lax.axis_index("hid")
    rows = blocks[0].shape[0]
    for mask, block in zip(masks, blocks):
        x[pl.ds(pl.multiple_of((h ^ mask) * rows, rows), rows), :] = block[...]
    values = x[...].astype(F32)
    lhs[...] = (values * gain[...]).astype(BF16)
    squares[...] = jnp.sum(values * values, axis=1, keepdims=True)
    cols[...] = x[:, pl.ds(pl.multiple_of(h * panel, panel), panel)].astype(F32)


def split(value):
    lane = lax.broadcasted_iota(jnp.int32, (value.shape[0], SIDE), 1)
    out = jnp.zeros((value.shape[0], SIDE), F32)
    for part in range(3):
        rounded = value.astype(BF16).astype(F32)
        out = jnp.where(lane == part, rounded, out)
        value = value - rounded
    return out


def joined(parts):
    return jnp.sum(parts.astype(F32), axis=1, keepdims=True)


def gate_up_kernel(lhs_ref, gate_ref, up_ref, *refs):
    send_ref, keep_ref, both, side = refs[-4:]
    places = ((keep_ref, 0), (send_ref, 0), (keep_ref, 1), (send_ref, 1))
    rows = send_ref.shape[1]
    z = lax.axis_index("tok")
    lhs = lhs_ref[...]

    def hand_out(source, start, width):
        for d, (out, slot) in enumerate(places):
            at = pl.multiple_of((z ^ d) * rows, rows)
            out[slot, :, start:start + width] = source[pl.ds(at, rows), :].astype(BF16)

    for tile in range(gate_ref.shape[1] // TILE):
        cols = slice(tile * TILE, (tile + 1) * TILE)
        both[:, :TILE] = jnp.dot(lhs, gate_ref[:, cols], preferred_element_type=F32)
        both[:, TILE:] = jnp.dot(lhs, up_ref[:, cols], preferred_element_type=F32)
        hand_out(both, 2 * tile * TILE, 2 * TILE)
    if send_ref.shape[2] > 2 * gate_ref.shape[1]:
        side[...] = split(refs[0][...])
        hand_out(side, 2 * gate_ref.shape[1], SIDE)


def gate_up(lhs, gate, up, squares, n_tok, after=()):
    ntok, depth = lhs.shape
    width = gate.shape[1]
    rows = ntok // n_tok
    extra = [] if squares is None else [squares]
    shape = jax.ShapeDtypeStruct((2, rows, 2 * width + SIDE * len(extra)), BF16)
    return run(
        gate_up_kernel, "gate_up", [shape, shape], [lhs, gate, up, *extra, *after],
        0, 0,
        in_specs=[WHOLE] * (3 + len(extra)) + [ANYWHERE] * len(after),
        out_specs=[WHOLE] * 2,
        scratch_shapes=[pltpu.VMEM((ntok, 2 * TILE), F32), pltpu.VMEM((ntok, SIDE), F32)],
    )


def pair_total(keep, got, main, after):
    def body(keep_ref, got_ref, *refs):
        out = refs[-1]
        out[:, :main] = (keep_ref[1, :, :main].astype(F32) + got_ref[1, :, :main].astype(F32)).astype(BF16)
        if out.shape[1] > main:
            out[:, main:] = split(joined(keep_ref[1, :, main:]) + joined(got_ref[1, :, main:])).astype(BF16)

    size = keep.size // 2
    return run(
        body, "pair_total", jax.ShapeDtypeStruct(keep.shape[1:], BF16), [keep, got, *after],
        size, 6 * size, in_specs=[WHOLE] * 2 + [ANYWHERE] * len(after),
    )


def copy_after(value, after):
    def body(value_ref, *refs):
        refs[-1][...] = value_ref[...]

    return run(
        body, "copy", jax.ShapeDtypeStruct(value.shape, value.dtype), [value, *after],
        0, 4 * value.size, in_specs=[WHOLE] + [ANYWHERE] * len(after),
    )


def stack_after(blocks, after):
    stacks = [block if block.ndim == 3 else block[None] for block in blocks]
    total = sum(stack.shape[0] for stack in stacks)

    def body(*refs):
        at = 0
        for ref in refs[:len(stacks)]:
            refs[-1][at:at + ref.shape[0]] = ref[...]
            at += ref.shape[0]

    shape = jax.ShapeDtypeStruct((total, *stacks[0].shape[1:]), blocks[0].dtype)
    return run(
        body, "stack", shape, [*stacks, *after], 0, 4 * sum(stack.size for stack in stacks),
        in_specs=[WHOLE] * len(stacks) + [ANYWHERE] * len(after),
    )


def hidden_rows(chunks, widths, scale, after):
    rows = chunks[0][0].shape[1]
    given = [] if scale is None else [scale]

    def body(*refs):
        out_ref, scale_ref = refs[-2:]
        keep_ref, got_ref, over_ref = refs[:3]
        if scale is None:
            tail = slice(2 * widths[0], 2 * widths[0] + SIDE)
            squares = joined(keep_ref[0, :, tail]) + joined(got_ref[0, :, tail]) + joined(over_ref[:, tail])
            factor = lax.rsqrt(squares / float(D) + 1e-05)
        else:
            factor = refs[3 * len(chunks)][...]
        scale_ref[...] = factor
        start = 0
        for k, width in enumerate(widths):
            keep_ref, got_ref, over_ref = refs[3 * k:3 * k + 3]

            def total(at):
                cols = slice(at, at + TILE)
                return (
                    keep_ref[0, :, cols].astype(F32) + got_ref[0, :, cols].astype(F32) + over_ref[:, cols].astype(F32)
                ) * factor

            for at in range(0, width, TILE):
                gate, up = total(2 * at), total(2 * at + TILE)
                out_ref[:, start + at:start + at + TILE] = (jax.nn.silu(gate) * up).astype(BF16)
            start += width

    size = rows * sum(widths)
    return run(
        body, "hidden",
        [jax.ShapeDtypeStruct((rows, sum(widths)), BF16), jax.ShapeDtypeStruct((rows, 1), F32)],
        [part for chunk in chunks for part in chunk] + given + list(after), 20 * size, 14 * size,
        in_specs=[WHOLE] * (3 * len(chunks) + len(given)) + [ANYWHERE] * len(after),
        out_specs=[WHOLE] * 2,
    )


def down_kernel(masks, panel, n_blocks, add, *refs):
    blocks, weight, lhs, out = refs[:n_blocks], refs[n_blocks], refs[-1], refs[-2]
    before = refs[n_blocks + 1] if add else None
    z = lax.axis_index("tok")
    h = lax.axis_index("hid")
    rows = blocks[0].shape[0]
    for d, block in enumerate(blocks):
        lhs[pl.ds(pl.multiple_of((z ^ d) * rows, rows), rows), :] = block[...]
    values = lhs[...]
    for slot, mask in enumerate(masks):
        column = pl.multiple_of((h ^ mask) * panel, panel)
        total = jnp.dot(values, weight[:, pl.ds(column, panel)], preferred_element_type=F32)
        if before is not None:
            total = total + before[slot]
        out[slot] = total.astype(out.dtype)


def down(blocks, weight, masks, panel, kind, before=None, after=()):
    rows, depth = blocks[0].shape
    ntok = rows * len(blocks)
    return run(
        functools.partial(down_kernel, masks, panel, len(blocks), before is not None), "down",
        jax.ShapeDtypeStruct((len(masks), ntok, panel), kind),
        [*blocks, weight] + ([] if before is None else [before]) + list(after),
        2 * ntok * depth * panel * len(masks), 2 * depth * panel * len(masks),
        in_specs=[WHOLE] * (len(blocks) + 1 + (before is not None)) + [ANYWHERE] * len(after),
        scratch_shapes=[pltpu.VMEM((ntok, depth), BF16)],
    )


def chip_sum_kernel(mine_ref, other_ref, own_ref, *outs):
    own_ref[...] = mine_ref[0] + other_ref[0].astype(F32)
    for e, out in enumerate(outs):
        out[...] = (mine_ref[e + 1] + other_ref[e + 1].astype(F32)).astype(BF16)


def gram_kernel(slots, n_hid, ntok, classes, own_ref, *refs):
    stacks = refs[:len(slots)]
    outs, (tiles, sems) = refs[:-2], refs[-2:]
    out_ref = outs[-2] if classes else outs[-1]
    z = lax.axis_index("tok")
    h = lax.axis_index("hid")
    width = own_ref.shape[1]
    left = own_ref[...].T
    copies = []
    for stack, places in zip(stacks, slots):
        for at, (d, mask) in enumerate(places):
            number = len(copies)
            tiles[number] = jnp.dot(left, stack[at], preferred_element_type=F32) * (1.0 / ntok)
            column = ((z ^ d) * n_hid + (h ^ mask)) * width
            copy = pltpu.make_async_copy(
                tiles.at[number], out_ref.at[:, pl.ds(pl.multiple_of(column, width), width)], sems.at[number]
            )
            copy.start()
            copies.append(copy)
    if classes:
        labels, cross_ref = refs[len(slots)], outs[-1]
        onehot = (labels[...] == lax.broadcasted_iota(jnp.int32, (classes, ntok), 0)).astype(F32)
        counts = jnp.sum(onehot, axis=1, keepdims=True)
        sums = jnp.dot(onehot.astype(BF16), own_ref[...], preferred_element_type=F32)
        cross_ref[...] = sums / jnp.maximum(counts, 1.0)
    for copy in copies:
        copy.wait()


def gram_part(resid_cols, stacks, slots, n_tok, n_hid, before, labels=None):
    ntok, width = resid_cols.shape
    here = sum(len(places) for places in slots)
    gram_shape = pltpu.HBM((width, width * n_tok * n_hid), F32)
    extra, extra_specs = ([], []) if labels is None else ([labels[None, :]], [WHOLE])
    if before is not None:
        extra, extra_specs = extra + [before], extra_specs + [ANYWHERE]
    return run(
        functools.partial(gram_kernel, slots, n_hid, ntok, 0 if labels is None else CLASSES), "gram",
        [gram_shape] + ([] if labels is None else [jax.ShapeDtypeStruct((CLASSES, width), F32)]),
        [resid_cols, *stacks, *extra],
        2 * ntok * width * width * here, 4 * width * width * here,
        in_specs=[WHOLE] * (1 + len(stacks)) + extra_specs,
        out_specs=[ANYWHERE] + ([] if labels is None else [WHOLE]),
        input_output_aliases={} if before is None else {len(stacks) + len(extra): 0},
        scratch_shapes=[pltpu.VMEM((here, width, width), F32), pltpu.SemaphoreType.DMA((here,))],
    )


def class_means(resid_cols, labels):
    onehot = (labels[:, None] == jnp.arange(CLASSES, dtype=jnp.int32)[None, :]).astype(BF16)
    counts = jnp.sum(onehot.astype(F32), axis=0)
    class_sums = lax.dot_general(
        resid_cols, onehot, (((0,), (0,)), ((), ())), preferred_element_type=F32
    )
    return class_sums / jnp.maximum(counts, 1.0)[None, :]


def on_line(n_tok, n_hid, resid_in, norm_gain, gate_weight, up_weight, down_weight, labels):
    rows, block = resid_in.shape
    ntok, panel = rows * n_hid, block // n_hid
    depth, shard_ff = gate_weight.shape
    tiles = shard_ff // TILE
    ends = [0, TILE * (3 * tiles // 7), TILE * (11 * tiles // 14), shard_ff]
    chip_masks = list(range(2, n_hid, 2))

    def part(weight, k):
        return weight, 0, depth, ends[k], ends[k + 1] - ends[k]

    near = [resid_in] + [swap(resid_in, "hid", n_hid, mask) for mask in chip_masks]
    gate_0, up_0, own_x, gain = fetch(
        [
            part(gate_weight, 0),
            part(up_weight, 0),
            (resid_in, 0, rows, 0, block),
            (norm_gain[None, :], 0, 1, 0, block),
        ],
        (), "fetch_first",
    )
    relayed = copy_after(near[1], (gain,))
    far = [swap(piece, "hid", n_hid, 1) for piece in [near[0], relayed, *near[2:]]]
    masks = [0] + chip_masks + [1] + [mask + 1 for mask in chip_masks]
    lhs, x_cols, squares = run(
        functools.partial(tokens_kernel, masks, panel), "tokens",
        (
            jax.ShapeDtypeStruct((ntok, block), BF16),
            jax.ShapeDtypeStruct((ntok, panel), F32),
            jax.ShapeDtypeStruct((ntok, 1), F32),
        ),
        [own_x, *near[1:], *far, gain],
        4 * ntok * block, 4 * ntok * block,
        out_specs=(WHOLE, WHOLE, WHOLE),
        scratch_shapes=[pltpu.VMEM((ntok, block), BF16)],
    )

    widths = [ends[k + 1] - ends[k] for k in range(3)]
    send_0, keep_0 = gate_up(lhs, gate_0, up_0, squares, n_tok)
    got_0 = swap(send_0, "tok", n_tok, 1)
    gate_1, up_1 = fetch([part(gate_weight, 1), part(up_weight, 1)], (send_0,), "fetch_gate_up")
    send_1, keep_1 = gate_up(lhs, gate_1, up_1, None, n_tok)
    got_1 = swap(send_1, "tok", n_tok, 1)
    sum_0 = pair_total(keep_0, got_0, 2 * widths[0], (send_1,))
    over_0 = swap(sum_0, "tok", n_tok, 2)
    gate_2, up_2 = fetch([part(gate_weight, 2), part(up_weight, 2)], (sum_0,), "fetch_gate_up")
    send_2, keep_2 = gate_up(lhs, gate_2, up_2, None, n_tok)
    got_2 = swap(send_2, "tok", n_tok, 1)
    sum_1 = pair_total(keep_1, got_1, 2 * widths[1], (send_2,))
    over_1 = swap(sum_1, "tok", n_tok, 2)
    sum_2 = pair_total(keep_2, got_2, 2 * widths[2], (sum_1,))
    over_2 = swap(sum_2, "tok", n_tok, 2)

    a_own, scale = hidden_rows([(keep_0, got_0, over_0)], widths[:1], None, (sum_1,))
    a_two = swap(a_own, "tok", n_tok, 2)
    a_one = swap(a_own, "tok", n_tok, 1)
    a_three = swap(a_two, "tok", n_tok, 1)
    down_b, = fetch([(down_weight, ends[1], shard_ff - ends[1], 0, block)], (sum_2,), "fetch_down")
    down_a, = fetch([(down_weight, 0, ends[1], 0, block)], (down_b,), "fetch_down")
    b_own, _ = hidden_rows([(keep_1, got_1, over_1), (keep_2, got_2, over_2)], widths[1:], scale, (a_one, a_two, down_b))
    b_two = swap(b_own, "tok", n_tok, 2)
    b_one = swap(b_own, "tok", n_tok, 1)
    b_three = swap(b_two, "tok", n_tok, 1)
    hidden_a = [a_own, a_one, a_two, a_three]
    hidden_b = [b_own, b_one, b_two, b_three]

    here = [0] + chip_masks
    there = [mask + 1 for mask in here]
    other = down(hidden_b, down_b, there, panel, BF16, down(hidden_a, down_a, there, panel, F32))
    mine = down(hidden_b, down_b, here, panel, F32, down(hidden_a, down_a, here, panel, F32, after=(other,)))
    other = swap(other, "hid", n_hid, 1)
    summed, *sends = run(
        chip_sum_kernel, "chip_sum",
        [jax.ShapeDtypeStruct((ntok, panel), F32)] + [jax.ShapeDtypeStruct((ntok, panel), BF16)] * len(chip_masks),
        [mine, other], mine.size, 8 * mine.size,
        out_specs=[WHOLE] * len(here),
    )
    for mask, value in reversed(list(zip(chip_masks, sends))):
        summed = summed + swap(value, "hid", n_hid, mask).astype(F32)
    resid_cols = (x_cols + summed).astype(BF16)

    column = [swap(resid_cols, "tok", n_tok, d) for d in range(1, n_tok)]
    across = swap(resid_cols, "hid", n_hid, 6)
    line = stack_after([resid_cols, *column], (across,))
    beside = [swap(line, "hid", n_hid, mask) for mask in (2, 4)]
    across_line = [swap(across, "tok", n_tok, d) for d in (1, 2)] + [swap(column[2], "hid", n_hid, 6)]
    line_far = swap(line, "hid", n_hid, 1)
    across_far = swap(across, "hid", n_hid, 1)
    line_slots = [[(d, mask) for d in range(n_tok)] for mask in range(n_hid)]
    gram, cross = gram_part(
        resid_cols, [line, line_far, across[None], across_far[None]],
        [line_slots[0], line_slots[1], [(0, 6)], [(0, 7)]], n_tok, n_hid, None, labels,
    )
    done = pltpu.with_memory_space_constraint(gram, pltpu.HBM)
    near = stack_after([*beside, *across_line], (done,))
    far = swap(near, "hid", n_hid, 1)
    for stack, core in ((near, 0), (far, 1)):
        slots = line_slots[2 + core] + line_slots[4 + core] + line_slots[6 + core][1:]
        gram, = gram_part(resid_cols, [stack], [slots], n_tok, n_hid, gram)
    return (gram, cross.T)


def plain(n_tok, n_hid, resid_in, norm_gain, gate_weight, up_weight, down_weight, labels):
    x = lax.all_gather(resid_in, "hid", axis=0, tiled=True).astype(F32)
    ntok, block = x.shape
    total_sq = lax.psum(jnp.sum(x * x, axis=1), "tok")
    normed = (x * lax.rsqrt(total_sq / float(D) + 1e-05)[:, None] * norm_gain[None, :]).astype(BF16)

    def summed_over_tok(weight):
        product = jnp.dot(normed, weight, preferred_element_type=F32).astype(BF16)
        return lax.psum_scatter(product, "tok", scatter_dimension=0, tiled=True).astype(F32)

    hidden = (jax.nn.silu(summed_over_tok(gate_weight)) * summed_over_tok(up_weight)).astype(BF16)
    hidden = lax.all_gather(hidden, "tok", axis=0, tiled=True)
    partial_out = jnp.dot(hidden, down_weight, preferred_element_type=F32).astype(BF16)
    summed = lax.psum_scatter(partial_out, "hid", scatter_dimension=1, tiled=True).astype(F32)
    panel = block // n_hid
    x_cols = lax.dynamic_slice_in_dim(x, lax.axis_index("hid") * panel, panel, 1)
    resid_cols = (x_cols + summed).astype(BF16)
    everyone = lax.all_gather(resid_cols, ("tok", "hid"), axis=1, tiled=True)
    gram = lax.dot_general(
        resid_cols, everyone, (((0,), (0,)), ((), ())), preferred_element_type=F32
    ) / float(ntok)
    return (gram, class_means(resid_cols, labels))


def on_device(n_tok, n_hid, resid_in, norm_gain, gate_weight, *rest):
    panel = resid_in.shape[1] // n_hid
    fits = n_tok == 4 and n_hid == 8 and panel % 128 == 0 and gate_weight.shape[1] % TILE == 0 and gate_weight.shape[1] >= 3 * TILE
    body = on_line if fits else plain
    return body(n_tok, n_hid, resid_in, norm_gain, gate_weight, *rest)


def solution(mesh):
    return jax.shard_map(
        functools.partial(on_device, mesh.shape["tok"], mesh.shape["hid"]),
        mesh=mesh,
        in_specs=(
            P("hid", "tok"),
            P("tok"),
            P("tok", "hid"),
            P("tok", "hid"),
            P("hid", "tok"),
            P(),
        ),
        out_specs=(P(("tok", "hid"), None), P(("tok", "hid"), None)),
        check_vma=False,
    )
```

```python
import functools
import jax
import jax.numpy as jnp
from jax import lax
from jax.experimental import pallas as pl
from jax.experimental.pallas import tpu as pltpu
from jax.sharding import PartitionSpec as P

D = 8192
CLASSES = 64
TILE = 256
BF16 = jnp.bfloat16
F32 = jnp.float32
WHOLE = pl.BlockSpec(memory_space=pltpu.VMEM)
ANYWHERE = pl.BlockSpec(memory_space=pl.ANY)
SIDE = 128


def swap(value, axis, size, mask):
    return lax.ppermute(value, axis, [(i, i ^ mask) for i in range(size)])


def run(body, name, out_shape, operands, flops, bytes_accessed, in_specs=None, out_specs=WHOLE, **more):
    return pl.pallas_call(
        body,
        out_shape=out_shape,
        in_specs=[WHOLE] * len(operands) if in_specs is None else in_specs,
        out_specs=out_specs,
        compiler_params=pltpu.CompilerParams(vmem_limit_bytes=16 * 1024 * 1024),
        cost_estimate=pl.CostEstimate(flops=flops, bytes_accessed=bytes_accessed, transcendentals=0),
        name=name,
        **more,
    )(*operands)


def fetch(pieces, after, name):
    count = len(pieces)
    copies = []
    for number, (array, row, rows, column, columns) in enumerate(pieces):
        step = min(rows, 256)
        copies += [(number, at, step, row + at, column, columns) for at in range(0, rows, step)]

    def body(*refs):
        sources, targets, sems = refs[:count], refs[-1 - count:-1], refs[-1]
        started = []
        for sem, (number, at, step, row, column, columns) in enumerate(copies):
            copy = pltpu.make_async_copy(
                sources[number].at[pl.ds(row, step), pl.ds(column, columns)],
                targets[number].at[pl.ds(at, step), :],
                sems.at[sem],
            )
            copy.start()
            started.append(copy)
        for copy in started:
            copy.wait()

    size = sum(rows * columns * array.dtype.itemsize for array, _, rows, _, columns in pieces)
    return run(
        body, name,
        [pltpu.VMEM((rows, columns), array.dtype) for array, _, rows, _, columns in pieces],
        [pltpu.with_memory_space_constraint(piece[0], pltpu.HBM) for piece in pieces] + list(after),
        0, 0,
        in_specs=[ANYWHERE] * (count + len(after)),
        out_specs=[WHOLE] * count,
        scratch_shapes=[pltpu.SemaphoreType.DMA((len(copies),))],
    )


def tokens_kernel(masks, panel, *refs):
    blocks, gain, (lhs, cols, squares, x) = refs[:len(masks)], refs[len(masks)], refs[-4:]
    h = lax.axis_index("hid")
    rows = blocks[0].shape[0]
    for mask, block in zip(masks, blocks):
        x[pl.ds(pl.multiple_of((h ^ mask) * rows, rows), rows), :] = block[...]
    values = x[...].astype(F32)
    lhs[...] = (values * gain[...]).astype(BF16)
    squares[...] = jnp.sum(values * values, axis=1, keepdims=True)
    cols[...] = x[:, pl.ds(pl.multiple_of(h * panel, panel), panel)].astype(F32)


def split(value):
    lane = lax.broadcasted_iota(jnp.int32, (value.shape[0], SIDE), 1)
    out = jnp.zeros((value.shape[0], SIDE), F32)
    for part in range(3):
        rounded = value.astype(BF16).astype(F32)
        out = jnp.where(lane == part, rounded, out)
        value = value - rounded
    return out


def joined(parts):
    return jnp.sum(parts.astype(F32), axis=1, keepdims=True)


def gate_up_kernel(lhs_ref, gate_ref, up_ref, *refs):
    send_ref, keep_ref, both, side = refs[-4:]
    places = ((keep_ref, 0), (send_ref, 0), (keep_ref, 1), (send_ref, 1))
    rows = send_ref.shape[1]
    z = lax.axis_index("tok")
    lhs = lhs_ref[...]

    def hand_out(source, start, width):
        for d, (out, slot) in enumerate(places):
            at = pl.multiple_of((z ^ d) * rows, rows)
            out[slot, :, start:start + width] = source[pl.ds(at, rows), :].astype(BF16)

    for tile in range(gate_ref.shape[1] // TILE):
        cols = slice(tile * TILE, (tile + 1) * TILE)
        both[:, :TILE] = jnp.dot(lhs, gate_ref[:, cols], preferred_element_type=F32)
        both[:, TILE:] = jnp.dot(lhs, up_ref[:, cols], preferred_element_type=F32)
        hand_out(both, 2 * tile * TILE, 2 * TILE)
    if send_ref.shape[2] > 2 * gate_ref.shape[1]:
        side[...] = split(refs[0][...])
        hand_out(side, 2 * gate_ref.shape[1], SIDE)


def gate_up(lhs, gate, up, squares, n_tok, after=()):
    ntok, depth = lhs.shape
    width = gate.shape[1]
    rows = ntok // n_tok
    extra = [] if squares is None else [squares]
    shape = jax.ShapeDtypeStruct((2, rows, 2 * width + SIDE * len(extra)), BF16)
    return run(
        gate_up_kernel, "gate_up", [shape, shape], [lhs, gate, up, *extra, *after],
        0, 0,
        in_specs=[WHOLE] * (3 + len(extra)) + [ANYWHERE] * len(after),
        out_specs=[WHOLE] * 2,
        scratch_shapes=[pltpu.VMEM((ntok, 2 * TILE), F32), pltpu.VMEM((ntok, SIDE), F32)],
    )


def pair_total(keep, got, main, after):
    def body(keep_ref, got_ref, *refs):
        out = refs[-1]
        out[:, :main] = (keep_ref[1, :, :main].astype(F32) + got_ref[1, :, :main].astype(F32)).astype(BF16)
        if out.shape[1] > main:
            out[:, main:] = split(joined(keep_ref[1, :, main:]) + joined(got_ref[1, :, main:])).astype(BF16)

    size = keep.size // 2
    return run(
        body, "pair_total", jax.ShapeDtypeStruct(keep.shape[1:], BF16), [keep, got, *after],
        size, 6 * size, in_specs=[WHOLE] * 2 + [ANYWHERE] * len(after),
    )


def copy_after(value, after):
    def body(value_ref, *refs):
        refs[-1][...] = value_ref[...]

    return run(
        body, "copy", jax.ShapeDtypeStruct(value.shape, value.dtype), [value, *after],
        0, 4 * value.size, in_specs=[WHOLE] + [ANYWHERE] * len(after),
    )


def stack_after(blocks, after):
    stacks = [block if block.ndim == 3 else block[None] for block in blocks]
    total = sum(stack.shape[0] for stack in stacks)

    def body(*refs):
        at = 0
        for ref in refs[:len(stacks)]:
            refs[-1][at:at + ref.shape[0]] = ref[...]
            at += ref.shape[0]

    shape = jax.ShapeDtypeStruct((total, *stacks[0].shape[1:]), blocks[0].dtype)
    return run(
        body, "stack", shape, [*stacks, *after], 0, 4 * sum(stack.size for stack in stacks),
        in_specs=[WHOLE] * len(stacks) + [ANYWHERE] * len(after),
    )


def hidden_rows(chunks, widths, scale, after):
    rows = chunks[0][0].shape[1]
    given = [] if scale is None else [scale]

    def body(*refs):
        out_ref, scale_ref = refs[-2:]
        keep_ref, got_ref, over_ref = refs[:3]
        if scale is None:
            tail = slice(2 * widths[0], 2 * widths[0] + SIDE)
            squares = joined(keep_ref[0, :, tail]) + joined(got_ref[0, :, tail]) + joined(over_ref[:, tail])
            factor = lax.rsqrt(squares / float(D) + 1e-05)
        else:
            factor = refs[3 * len(chunks)][...]
        scale_ref[...] = factor
        start = 0
        for k, width in enumerate(widths):
            keep_ref, got_ref, over_ref = refs[3 * k:3 * k + 3]

            def total(at):
                cols = slice(at, at + TILE)
                return (
                    keep_ref[0, :, cols].astype(F32) + got_ref[0, :, cols].astype(F32) + over_ref[:, cols].astype(F32)
                ) * factor

            for at in range(0, width, TILE):
                gate, up = total(2 * at), total(2 * at + TILE)
                out_ref[:, start + at:start + at + TILE] = (jax.nn.silu(gate) * up).astype(BF16)
            start += width

    size = rows * sum(widths)
    return run(
        body, "hidden",
        [jax.ShapeDtypeStruct((rows, sum(widths)), BF16), jax.ShapeDtypeStruct((rows, 1), F32)],
        [part for chunk in chunks for part in chunk] + given + list(after), 20 * size, 14 * size,
        in_specs=[WHOLE] * (3 * len(chunks) + len(given)) + [ANYWHERE] * len(after),
        out_specs=[WHOLE] * 2,
    )


def down_kernel(masks, panel, n_blocks, add, *refs):
    blocks, weight, lhs, out = refs[:n_blocks], refs[n_blocks], refs[-1], refs[-2]
    before = refs[n_blocks + 1] if add else None
    z = lax.axis_index("tok")
    h = lax.axis_index("hid")
    rows = blocks[0].shape[0]
    for d, block in enumerate(blocks):
        lhs[pl.ds(pl.multiple_of((z ^ d) * rows, rows), rows), :] = block[...]
    values = lhs[...]
    for slot, mask in enumerate(masks):
        column = pl.multiple_of((h ^ mask) * panel, panel)
        total = jnp.dot(values, weight[:, pl.ds(column, panel)], preferred_element_type=F32)
        if before is not None:
            total = total + before[slot]
        out[slot] = total.astype(out.dtype)


def down(blocks, weight, masks, panel, kind, before=None, after=()):
    rows, depth = blocks[0].shape
    ntok = rows * len(blocks)
    return run(
        functools.partial(down_kernel, masks, panel, len(blocks), before is not None), "down",
        jax.ShapeDtypeStruct((len(masks), ntok, panel), kind),
        [*blocks, weight] + ([] if before is None else [before]) + list(after),
        2 * ntok * depth * panel * len(masks), 2 * depth * panel * len(masks),
        in_specs=[WHOLE] * (len(blocks) + 1 + (before is not None)) + [ANYWHERE] * len(after),
        scratch_shapes=[pltpu.VMEM((ntok, depth), BF16)],
    )


def chip_sum_kernel(mine_ref, other_ref, own_ref, *outs):
    own_ref[...] = mine_ref[0] + other_ref[0].astype(F32)
    for e, out in enumerate(outs):
        out[...] = (mine_ref[e + 1] + other_ref[e + 1].astype(F32)).astype(BF16)


def gram_kernel(slots, n_hid, ntok, classes, own_ref, *refs):
    stacks = refs[:len(slots)]
    outs, (tiles, sems) = refs[:-2], refs[-2:]
    out_ref = outs[-2] if classes else outs[-1]
    z = lax.axis_index("tok")
    h = lax.axis_index("hid")
    width = own_ref.shape[1]
    left = own_ref[...].T
    copies = []
    for stack, places in zip(stacks, slots):
        for at, (d, mask) in enumerate(places):
            number = len(copies)
            tiles[number] = jnp.dot(left, stack[at], preferred_element_type=F32) * (1.0 / ntok)
            column = ((z ^ d) * n_hid + (h ^ mask)) * width
            copy = pltpu.make_async_copy(
                tiles.at[number], out_ref.at[:, pl.ds(pl.multiple_of(column, width), width)], sems.at[number]
            )
            copy.start()
            copies.append(copy)
    if classes:
        labels, cross_ref = refs[len(slots)], outs[-1]
        onehot = (labels[...] == lax.broadcasted_iota(jnp.int32, (classes, ntok), 0)).astype(F32)
        counts = jnp.sum(onehot, axis=1, keepdims=True)
        sums = jnp.dot(onehot.astype(BF16), own_ref[...], preferred_element_type=F32)
        cross_ref[...] = sums / jnp.maximum(counts, 1.0)
    for copy in copies:
        copy.wait()


def gram_part(resid_cols, stacks, slots, n_tok, n_hid, before, labels=None):
    ntok, width = resid_cols.shape
    here = sum(len(places) for places in slots)
    gram_shape = pltpu.HBM((width, width * n_tok * n_hid), F32)
    extra, extra_specs = ([], []) if labels is None else ([labels[None, :]], [WHOLE])
    if before is not None:
        extra, extra_specs = extra + [before], extra_specs + [ANYWHERE]
    return run(
        functools.partial(gram_kernel, slots, n_hid, ntok, 0 if labels is None else CLASSES), "gram",
        [gram_shape] + ([] if labels is None else [jax.ShapeDtypeStruct((CLASSES, width), F32)]),
        [resid_cols, *stacks, *extra],
        2 * ntok * width * width * here, 4 * width * width * here,
        in_specs=[WHOLE] * (1 + len(stacks)) + extra_specs,
        out_specs=[ANYWHERE] + ([] if labels is None else [WHOLE]),
        input_output_aliases={} if before is None else {len(stacks) + len(extra): 0},
        scratch_shapes=[pltpu.VMEM((here, width, width), F32), pltpu.SemaphoreType.DMA((here,))],
    )


def class_means(resid_cols, labels):
    onehot = (labels[:, None] == jnp.arange(CLASSES, dtype=jnp.int32)[None, :]).astype(BF16)
    counts = jnp.sum(onehot.astype(F32), axis=0)
    class_sums = lax.dot_general(
        resid_cols, onehot, (((0,), (0,)), ((), ())), preferred_element_type=F32
    )
    return class_sums / jnp.maximum(counts, 1.0)[None, :]


def on_line(n_tok, n_hid, resid_in, norm_gain, gate_weight, up_weight, down_weight, labels):
    rows, block = resid_in.shape
    ntok, panel = rows * n_hid, block // n_hid
    depth, shard_ff = gate_weight.shape
    tiles = shard_ff // TILE
    ends = [0, TILE * (3 * tiles // 7), TILE * (11 * tiles // 14), shard_ff]
    chip_masks = list(range(2, n_hid, 2))

    def part(weight, k):
        return weight, 0, depth, ends[k], ends[k + 1] - ends[k]

    near = [resid_in] + [swap(resid_in, "hid", n_hid, mask) for mask in chip_masks]
    gate_0, up_0, own_x, gain = fetch(
        [
            part(gate_weight, 0),
            part(up_weight, 0),
            (resid_in, 0, rows, 0, block),
            (norm_gain[None, :], 0, 1, 0, block),
        ],
        (), "fetch_first",
    )
    relayed = copy_after(near[1], (gain,))
    far = [swap(piece, "hid", n_hid, 1) for piece in [near[0], relayed, *near[2:]]]
    masks = [0] + chip_masks + [1] + [mask + 1 for mask in chip_masks]
    lhs, x_cols, squares = run(
        functools.partial(tokens_kernel, masks, panel), "tokens",
        (
            jax.ShapeDtypeStruct((ntok, block), BF16),
            jax.ShapeDtypeStruct((ntok, panel), F32),
            jax.ShapeDtypeStruct((ntok, 1), F32),
        ),
        [own_x, *near[1:], *far, gain],
        4 * ntok * block, 4 * ntok * block,
        out_specs=(WHOLE, WHOLE, WHOLE),
        scratch_shapes=[pltpu.VMEM((ntok, block), BF16)],
    )

    widths = [ends[k + 1] - ends[k] for k in range(3)]
    send_0, keep_0 = gate_up(lhs, gate_0, up_0, squares, n_tok)
    got_0 = swap(send_0, "tok", n_tok, 1)
    gate_1, up_1 = fetch([part(gate_weight, 1), part(up_weight, 1)], (send_0,), "fetch_gate_up")
    send_1, keep_1 = gate_up(lhs, gate_1, up_1, None, n_tok)
    got_1 = swap(send_1, "tok", n_tok, 1)
    sum_0 = pair_total(keep_0, got_0, 2 * widths[0], (send_1,))
    over_0 = swap(sum_0, "tok", n_tok, 2)
    gate_2, up_2 = fetch([part(gate_weight, 2), part(up_weight, 2)], (sum_0,), "fetch_gate_up")
    send_2, keep_2 = gate_up(lhs, gate_2, up_2, None, n_tok)
    got_2 = swap(send_2, "tok", n_tok, 1)
    sum_1 = pair_total(keep_1, got_1, 2 * widths[1], (send_2,))
    over_1 = swap(sum_1, "tok", n_tok, 2)
    sum_2 = pair_total(keep_2, got_2, 2 * widths[2], (sum_1,))
    over_2 = swap(sum_2, "tok", n_tok, 2)

    a_own, scale = hidden_rows([(keep_0, got_0, over_0)], widths[:1], None, (sum_1,))
    a_two = swap(a_own, "tok", n_tok, 2)
    a_one = swap(a_own, "tok", n_tok, 1)
    a_three = swap(a_two, "tok", n_tok, 1)
    down_b, = fetch([(down_weight, ends[1], shard_ff - ends[1], 0, block)], (sum_2,), "fetch_down")
    down_a, = fetch([(down_weight, 0, ends[1], 0, block)], (down_b,), "fetch_down")
    b_own, _ = hidden_rows([(keep_1, got_1, over_1), (keep_2, got_2, over_2)], widths[1:], scale, (a_one, a_two, down_b))
    b_two = swap(b_own, "tok", n_tok, 2)
    b_one = swap(b_own, "tok", n_tok, 1)
    b_three = swap(b_two, "tok", n_tok, 1)
    hidden_a = [a_own, a_one, a_two, a_three]
    hidden_b = [b_own, b_one, b_two, b_three]

    here = [0] + chip_masks
    there = [mask + 1 for mask in here]
    other = down(hidden_b, down_b, there, panel, BF16, down(hidden_a, down_a, there, panel, F32))
    mine = down(hidden_b, down_b, here, panel, F32, down(hidden_a, down_a, here, panel, F32, after=(other,)))
    other = swap(other, "hid", n_hid, 1)
    summed, *sends = run(
        chip_sum_kernel, "chip_sum",
        [jax.ShapeDtypeStruct((ntok, panel), F32)] + [jax.ShapeDtypeStruct((ntok, panel), BF16)] * len(chip_masks),
        [mine, other], mine.size, 8 * mine.size,
        out_specs=[WHOLE] * len(here),
    )
    for mask, value in reversed(list(zip(chip_masks, sends))):
        summed = summed + swap(value, "hid", n_hid, mask).astype(F32)
    resid_cols = (x_cols + summed).astype(BF16)

    column = [swap(resid_cols, "tok", n_tok, d) for d in range(1, n_tok)]
    across = swap(resid_cols, "hid", n_hid, 6)
    line = stack_after([resid_cols, *column], (across,))
    beside = [swap(line, "hid", n_hid, mask) for mask in (2, 4)]
    across_line = [
        swap(across, "tok", n_tok, 1),
        swap(stack_after(column[1:], (across,)), "hid", n_hid, 6),
    ]
    line_far = swap(line, "hid", n_hid, 1)
    across_far = swap(across, "hid", n_hid, 1)
    line_slots = [[(d, mask) for d in range(n_tok)] for mask in range(n_hid)]
    gram, cross = gram_part(
        resid_cols, [line, line_far, across[None], across_far[None]],
        [line_slots[0], line_slots[1], [(0, 6)], [(0, 7)]], n_tok, n_hid, None, labels,
    )
    done = pltpu.with_memory_space_constraint(gram, pltpu.HBM)
    near = stack_after([*beside, *across_line], (done,))
    far = swap(near, "hid", n_hid, 1)
    for stack, core in ((near, 0), (far, 1)):
        slots = line_slots[2 + core] + line_slots[4 + core] + line_slots[6 + core][1:]
        gram, = gram_part(resid_cols, [stack], [slots], n_tok, n_hid, gram)
    return (gram, cross.T)


def plain(n_tok, n_hid, resid_in, norm_gain, gate_weight, up_weight, down_weight, labels):
    x = lax.all_gather(resid_in, "hid", axis=0, tiled=True).astype(F32)
    ntok, block = x.shape
    total_sq = lax.psum(jnp.sum(x * x, axis=1), "tok")
    normed = (x * lax.rsqrt(total_sq / float(D) + 1e-05)[:, None] * norm_gain[None, :]).astype(BF16)

    def summed_over_tok(weight):
        product = jnp.dot(normed, weight, preferred_element_type=F32).astype(BF16)
        return lax.psum_scatter(product, "tok", scatter_dimension=0, tiled=True).astype(F32)

    hidden = (jax.nn.silu(summed_over_tok(gate_weight)) * summed_over_tok(up_weight)).astype(BF16)
    hidden = lax.all_gather(hidden, "tok", axis=0, tiled=True)
    partial_out = jnp.dot(hidden, down_weight, preferred_element_type=F32).astype(BF16)
    summed = lax.psum_scatter(partial_out, "hid", scatter_dimension=1, tiled=True).astype(F32)
    panel = block // n_hid
    x_cols = lax.dynamic_slice_in_dim(x, lax.axis_index("hid") * panel, panel, 1)
    resid_cols = (x_cols + summed).astype(BF16)
    everyone = lax.all_gather(resid_cols, ("tok", "hid"), axis=1, tiled=True)
    gram = lax.dot_general(
        resid_cols, everyone, (((0,), (0,)), ((), ())), preferred_element_type=F32
    ) / float(ntok)
    return (gram, class_means(resid_cols, labels))


def on_device(n_tok, n_hid, resid_in, norm_gain, gate_weight, *rest):
    panel = resid_in.shape[1] // n_hid
    fits = n_tok == 4 and n_hid == 8 and panel % 128 == 0 and gate_weight.shape[1] % TILE == 0 and gate_weight.shape[1] >= 3 * TILE
    body = on_line if fits else plain
    return body(n_tok, n_hid, resid_in, norm_gain, gate_weight, *rest)


def solution(mesh):
    return jax.shard_map(
        functools.partial(on_device, mesh.shape["tok"], mesh.shape["hid"]),
        mesh=mesh,
        in_specs=(
            P("hid", "tok"),
            P("tok"),
            P("tok", "hid"),
            P("tok", "hid"),
            P("hid", "tok"),
            P(),
        ),
        out_specs=(P(("tok", "hid"), None), P(("tok", "hid"), None)),
        check_vma=False,
    )
```

```python
import functools
import jax
import jax.numpy as jnp
from jax import lax
from jax.experimental import pallas as pl
from jax.experimental.pallas import tpu as pltpu
from jax.sharding import PartitionSpec as P

D = 8192
CLASSES = 64
TILE = 256
BF16 = jnp.bfloat16
F32 = jnp.float32
WHOLE = pl.BlockSpec(memory_space=pltpu.VMEM)
ANYWHERE = pl.BlockSpec(memory_space=pl.ANY)
SIDE = 128


def swap(value, axis, size, mask):
    return lax.ppermute(value, axis, [(i, i ^ mask) for i in range(size)])


def run(body, name, out_shape, operands, flops, bytes_accessed, in_specs=None, out_specs=WHOLE, **more):
    return pl.pallas_call(
        body,
        out_shape=out_shape,
        in_specs=[WHOLE] * len(operands) if in_specs is None else in_specs,
        out_specs=out_specs,
        compiler_params=pltpu.CompilerParams(vmem_limit_bytes=16 * 1024 * 1024),
        cost_estimate=pl.CostEstimate(flops=flops, bytes_accessed=bytes_accessed, transcendentals=0),
        name=name,
        **more,
    )(*operands)


def fetch(pieces, after, name):
    count = len(pieces)
    copies = []
    for number, (array, row, rows, column, columns) in enumerate(pieces):
        step = min(rows, 256)
        copies += [(number, at, step, row + at, column, columns) for at in range(0, rows, step)]

    def body(*refs):
        sources, targets, sems = refs[:count], refs[-1 - count:-1], refs[-1]
        started = []
        for sem, (number, at, step, row, column, columns) in enumerate(copies):
            copy = pltpu.make_async_copy(
                sources[number].at[pl.ds(row, step), pl.ds(column, columns)],
                targets[number].at[pl.ds(at, step), :],
                sems.at[sem],
            )
            copy.start()
            started.append(copy)
        for copy in started:
            copy.wait()

    size = sum(rows * columns * array.dtype.itemsize for array, _, rows, _, columns in pieces)
    return run(
        body, name,
        [pltpu.VMEM((rows, columns), array.dtype) for array, _, rows, _, columns in pieces],
        [pltpu.with_memory_space_constraint(piece[0], pltpu.HBM) for piece in pieces] + list(after),
        0, 0,
        in_specs=[ANYWHERE] * (count + len(after)),
        out_specs=[WHOLE] * count,
        scratch_shapes=[pltpu.SemaphoreType.DMA((len(copies),))],
    )


def tokens_kernel(masks, panel, *refs):
    blocks, gain, (lhs, cols, squares, x) = refs[:len(masks)], refs[len(masks)], refs[-4:]
    h = lax.axis_index("hid")
    rows = blocks[0].shape[0]
    for mask, block in zip(masks, blocks):
        x[pl.ds(pl.multiple_of((h ^ mask) * rows, rows), rows), :] = block[...]
    values = x[...].astype(F32)
    lhs[...] = (values * gain[...]).astype(BF16)
    squares[...] = jnp.sum(values * values, axis=1, keepdims=True)
    cols[...] = x[:, pl.ds(pl.multiple_of(h * panel, panel), panel)].astype(F32)


def split(value):
    lane = lax.broadcasted_iota(jnp.int32, (value.shape[0], SIDE), 1)
    out = jnp.zeros((value.shape[0], SIDE), F32)
    for part in range(3):
        rounded = value.astype(BF16).astype(F32)
        out = jnp.where(lane == part, rounded, out)
        value = value - rounded
    return out


def joined(parts):
    return jnp.sum(parts.astype(F32), axis=1, keepdims=True)


def gate_up_kernel(lhs_ref, gate_ref, up_ref, *refs):
    send_ref, keep_ref, both, side = refs[-4:]
    places = ((keep_ref, 0), (send_ref, 0), (keep_ref, 1), (send_ref, 1))
    rows = send_ref.shape[1]
    z = lax.axis_index("tok")
    lhs = lhs_ref[...]

    def hand_out(source, start, width):
        for d, (out, slot) in enumerate(places):
            at = pl.multiple_of((z ^ d) * rows, rows)
            out[slot, :, start:start + width] = source[pl.ds(at, rows), :].astype(BF16)

    for tile in range(gate_ref.shape[1] // TILE):
        cols = slice(tile * TILE, (tile + 1) * TILE)
        both[:, :TILE] = jnp.dot(lhs, gate_ref[:, cols], preferred_element_type=F32)
        both[:, TILE:] = jnp.dot(lhs, up_ref[:, cols], preferred_element_type=F32)
        hand_out(both, 2 * tile * TILE, 2 * TILE)
    if send_ref.shape[2] > 2 * gate_ref.shape[1]:
        side[...] = split(refs[0][...])
        hand_out(side, 2 * gate_ref.shape[1], SIDE)


def gate_up(lhs, gate, up, squares, n_tok, after=()):
    ntok, depth = lhs.shape
    width = gate.shape[1]
    rows = ntok // n_tok
    extra = [] if squares is None else [squares]
    shape = jax.ShapeDtypeStruct((2, rows, 2 * width + SIDE * len(extra)), BF16)
    return run(
        gate_up_kernel, "gate_up", [shape, shape], [lhs, gate, up, *extra, *after],
        0, 0,
        in_specs=[WHOLE] * (3 + len(extra)) + [ANYWHERE] * len(after),
        out_specs=[WHOLE] * 2,
        scratch_shapes=[pltpu.VMEM((ntok, 2 * TILE), F32), pltpu.VMEM((ntok, SIDE), F32)],
    )


def pair_total(keep, got, main, after):
    def body(keep_ref, got_ref, *refs):
        out = refs[-1]
        out[:, :main] = (keep_ref[1, :, :main].astype(F32) + got_ref[1, :, :main].astype(F32)).astype(BF16)
        if out.shape[1] > main:
            out[:, main:] = split(joined(keep_ref[1, :, main:]) + joined(got_ref[1, :, main:])).astype(BF16)

    size = keep.size // 2
    return run(
        body, "pair_total", jax.ShapeDtypeStruct(keep.shape[1:], BF16), [keep, got, *after],
        size, 6 * size, in_specs=[WHOLE] * 2 + [ANYWHERE] * len(after),
    )


def copy_after(value, after):
    def body(value_ref, *refs):
        refs[-1][...] = value_ref[...]

    return run(
        body, "copy", jax.ShapeDtypeStruct(value.shape, value.dtype), [value, *after],
        0, 4 * value.size, in_specs=[WHOLE] + [ANYWHERE] * len(after),
    )


def stack_after(blocks, after, extra=0):
    stacks = [block if block.ndim == 3 else block[None] for block in blocks]
    total = sum(stack.shape[0] for stack in stacks)
    rows = stacks[0].shape[1]

    def body(*refs):
        out = refs[len(stacks) + len(after)]
        at = 0
        for ref in refs[:len(stacks)]:
            out[at:at + ref.shape[0]] = ref[:, :rows, :]
            at += ref.shape[0]
        if extra:
            refs[-1][:rows, :] = out[at - 1]
            refs[-1][rows:, :] = out[at - 1, :extra, :]

    width, kind = blocks[0].shape[-1], blocks[0].dtype
    shapes = [jax.ShapeDtypeStruct((total, rows, width), kind)]
    shapes += [jax.ShapeDtypeStruct((rows + extra, width), kind)] if extra else []
    outs = run(
        body, "stack", shapes, [*stacks, *after], 0, 4 * sum(stack.size for stack in stacks),
        in_specs=[WHOLE] * len(stacks) + [ANYWHERE] * len(after),
        out_specs=[WHOLE] * len(shapes),
    )
    return outs if extra else outs[0]


def hidden_rows(chunks, widths, scale, after):
    rows = chunks[0][0].shape[1]
    given = [] if scale is None else [scale]

    def body(*refs):
        out_ref, scale_ref = refs[-2:]
        keep_ref, got_ref, over_ref = refs[:3]
        if scale is None:
            tail = slice(2 * widths[0], 2 * widths[0] + SIDE)
            squares = joined(keep_ref[0, :, tail]) + joined(got_ref[0, :, tail]) + joined(over_ref[:, tail])
            factor = lax.rsqrt(squares / float(D) + 1e-05)
        else:
            factor = refs[3 * len(chunks)][...]
        scale_ref[...] = factor
        start = 0
        for k, width in enumerate(widths):
            keep_ref, got_ref, over_ref = refs[3 * k:3 * k + 3]

            def total(at):
                cols = slice(at, at + TILE)
                return (
                    keep_ref[0, :, cols].astype(F32) + got_ref[0, :, cols].astype(F32) + over_ref[:, cols].astype(F32)
                ) * factor

            for at in range(0, width, TILE):
                gate, up = total(2 * at), total(2 * at + TILE)
                out_ref[:, start + at:start + at + TILE] = (jax.nn.silu(gate) * up).astype(BF16)
            start += width

    size = rows * sum(widths)
    return run(
        body, "hidden",
        [jax.ShapeDtypeStruct((rows, sum(widths)), BF16), jax.ShapeDtypeStruct((rows, 1), F32)],
        [part for chunk in chunks for part in chunk] + given + list(after), 20 * size, 14 * size,
        in_specs=[WHOLE] * (3 * len(chunks) + len(given)) + [ANYWHERE] * len(after),
        out_specs=[WHOLE] * 2,
    )


def down_kernel(masks, panel, n_blocks, add, *refs):
    blocks, weight, lhs, out = refs[:n_blocks], refs[n_blocks], refs[-1], refs[-2]
    before = refs[n_blocks + 1] if add else None
    z = lax.axis_index("tok")
    h = lax.axis_index("hid")
    rows = blocks[0].shape[0]
    for d, block in enumerate(blocks):
        lhs[pl.ds(pl.multiple_of((z ^ d) * rows, rows), rows), :] = block[...]
    values = lhs[...]
    for slot, mask in enumerate(masks):
        column = pl.multiple_of((h ^ mask) * panel, panel)
        total = jnp.dot(values, weight[:, pl.ds(column, panel)], preferred_element_type=F32)
        if before is not None:
            total = total + before[slot]
        out[slot] = total.astype(out.dtype)


def down(blocks, weight, masks, panel, kind, before=None, after=()):
    rows, depth = blocks[0].shape
    ntok = rows * len(blocks)
    return run(
        functools.partial(down_kernel, masks, panel, len(blocks), before is not None), "down",
        jax.ShapeDtypeStruct((len(masks), ntok, panel), kind),
        [*blocks, weight] + ([] if before is None else [before]) + list(after),
        2 * ntok * depth * panel * len(masks), 2 * depth * panel * len(masks),
        in_specs=[WHOLE] * (len(blocks) + 1 + (before is not None)) + [ANYWHERE] * len(after),
        scratch_shapes=[pltpu.VMEM((ntok, depth), BF16)],
    )


def chip_sum_kernel(mine_ref, other_ref, own_ref, *outs):
    own_ref[...] = mine_ref[0] + other_ref[0].astype(F32)
    for e, out in enumerate(outs):
        out[...] = (mine_ref[e + 1] + other_ref[e + 1].astype(F32)).astype(BF16)


def gram_kernel(slots, n_hid, ntok, classes, own_ref, *refs):
    stacks = refs[:len(slots)]
    outs, (tiles, sems) = refs[:-2], refs[-2:]
    out_ref = outs[-2] if classes else outs[-1]
    z = lax.axis_index("tok")
    h = lax.axis_index("hid")
    width = own_ref.shape[1]
    left = own_ref[...].T
    copies = []
    for stack, places in zip(stacks, slots):
        for at, (d, mask) in enumerate(places):
            number = len(copies)
            tiles[number] = jnp.dot(left, stack[at], preferred_element_type=F32) * (1.0 / ntok)
            column = ((z ^ d) * n_hid + (h ^ mask)) * width
            copy = pltpu.make_async_copy(
                tiles.at[number], out_ref.at[:, pl.ds(pl.multiple_of(column, width), width)], sems.at[number]
            )
            copy.start()
            copies.append(copy)
    if classes:
        labels, cross_ref = refs[len(slots)], outs[-1]
        onehot = (labels[...] == lax.broadcasted_iota(jnp.int32, (classes, ntok), 0)).astype(F32)
        counts = jnp.sum(onehot, axis=1, keepdims=True)
        sums = jnp.dot(onehot.astype(BF16), own_ref[...], preferred_element_type=F32)
        cross_ref[...] = sums / jnp.maximum(counts, 1.0)
    for copy in copies:
        copy.wait()


def gram_part(resid_cols, stacks, slots, n_tok, n_hid, before, labels=None):
    ntok, width = resid_cols.shape
    here = sum(len(places) for places in slots)
    gram_shape = pltpu.HBM((width, width * n_tok * n_hid), F32)
    extra, extra_specs = ([], []) if labels is None else ([labels[None, :]], [WHOLE])
    if before is not None:
        extra, extra_specs = extra + [before], extra_specs + [ANYWHERE]
    return run(
        functools.partial(gram_kernel, slots, n_hid, ntok, 0 if labels is None else CLASSES), "gram",
        [gram_shape] + ([] if labels is None else [jax.ShapeDtypeStruct((CLASSES, width), F32)]),
        [resid_cols, *stacks, *extra],
        2 * ntok * width * width * here, 4 * width * width * here,
        in_specs=[WHOLE] * (1 + len(stacks)) + extra_specs,
        out_specs=[ANYWHERE] + ([] if labels is None else [WHOLE]),
        input_output_aliases={} if before is None else {len(stacks) + len(extra): 0},
        scratch_shapes=[pltpu.VMEM((here, width, width), F32), pltpu.SemaphoreType.DMA((here,))],
    )


def class_means(resid_cols, labels):
    onehot = (labels[:, None] == jnp.arange(CLASSES, dtype=jnp.int32)[None, :]).astype(BF16)
    counts = jnp.sum(onehot.astype(F32), axis=0)
    class_sums = lax.dot_general(
        resid_cols, onehot, (((0,), (0,)), ((), ())), preferred_element_type=F32
    )
    return class_sums / jnp.maximum(counts, 1.0)[None, :]


def on_line(n_tok, n_hid, resid_in, norm_gain, gate_weight, up_weight, down_weight, labels):
    rows, block = resid_in.shape
    ntok, panel = rows * n_hid, block // n_hid
    depth, shard_ff = gate_weight.shape
    tiles = shard_ff // TILE
    ends = [0, TILE * (3 * tiles // 7), TILE * (11 * tiles // 14), shard_ff]
    chip_masks = list(range(2, n_hid, 2))

    def part(weight, k):
        return weight, 0, depth, ends[k], ends[k + 1] - ends[k]

    near = [resid_in] + [swap(resid_in, "hid", n_hid, mask) for mask in chip_masks]
    gate_0, up_0, own_x, gain = fetch(
        [
            part(gate_weight, 0),
            part(up_weight, 0),
            (resid_in, 0, rows, 0, block),
            (norm_gain[None, :], 0, 1, 0, block),
        ],
        (), "fetch_first",
    )
    relayed = copy_after(near[1], (gain,))
    far = [swap(piece, "hid", n_hid, 1) for piece in [near[0], relayed, *near[2:]]]
    masks = [0] + chip_masks + [1] + [mask + 1 for mask in chip_masks]
    lhs, x_cols, squares = run(
        functools.partial(tokens_kernel, masks, panel), "tokens",
        (
            jax.ShapeDtypeStruct((ntok, block), BF16),
            jax.ShapeDtypeStruct((ntok, panel), F32),
            jax.ShapeDtypeStruct((ntok, 1), F32),
        ),
        [own_x, *near[1:], *far, gain],
        4 * ntok * block, 4 * ntok * block,
        out_specs=(WHOLE, WHOLE, WHOLE),
        scratch_shapes=[pltpu.VMEM((ntok, block), BF16)],
    )

    widths = [ends[k + 1] - ends[k] for k in range(3)]
    send_0, keep_0 = gate_up(lhs, gate_0, up_0, squares, n_tok)
    got_0 = swap(send_0, "tok", n_tok, 1)
    gate_1, up_1 = fetch([part(gate_weight, 1), part(up_weight, 1)], (send_0,), "fetch_gate_up")
    send_1, keep_1 = gate_up(lhs, gate_1, up_1, None, n_tok)
    got_1 = swap(send_1, "tok", n_tok, 1)
    sum_0 = pair_total(keep_0, got_0, 2 * widths[0], (send_1,))
    over_0 = swap(sum_0, "tok", n_tok, 2)
    gate_2, up_2 = fetch([part(gate_weight, 2), part(up_weight, 2)], (sum_0,), "fetch_gate_up")
    send_2, keep_2 = gate_up(lhs, gate_2, up_2, None, n_tok)
    got_2 = swap(send_2, "tok", n_tok, 1)
    sum_1 = pair_total(keep_1, got_1, 2 * widths[1], (send_2,))
    over_1 = swap(sum_1, "tok", n_tok, 2)
    sum_2 = pair_total(keep_2, got_2, 2 * widths[2], (sum_1,))
    over_2 = swap(sum_2, "tok", n_tok, 2)

    a_own, scale = hidden_rows([(keep_0, got_0, over_0)], widths[:1], None, (sum_1,))
    a_two = swap(a_own, "tok", n_tok, 2)
    a_one = swap(a_own, "tok", n_tok, 1)
    a_three = swap(a_two, "tok", n_tok, 1)
    down_b, = fetch([(down_weight, ends[1], shard_ff - ends[1], 0, block)], (sum_2,), "fetch_down")
    down_a, = fetch([(down_weight, 0, ends[1], 0, block)], (down_b,), "fetch_down")
    b_own, _ = hidden_rows([(keep_1, got_1, over_1), (keep_2, got_2, over_2)], widths[1:], scale, (a_one, a_two, down_b))
    b_two = swap(b_own, "tok", n_tok, 2)
    b_one = swap(b_own, "tok", n_tok, 1)
    b_three = swap(b_two, "tok", n_tok, 1)
    hidden_a = [a_own, a_one, a_two, a_three]
    hidden_b = [b_own, b_one, b_two, b_three]

    here = [0] + chip_masks
    there = [mask + 1 for mask in here]
    other = down(hidden_b, down_b, there, panel, BF16, down(hidden_a, down_a, there, panel, F32))
    mine = down(hidden_b, down_b, here, panel, F32, down(hidden_a, down_a, here, panel, F32, after=(other,)))
    other = swap(other, "hid", n_hid, 1)
    summed, *sends = run(
        chip_sum_kernel, "chip_sum",
        [jax.ShapeDtypeStruct((ntok, panel), F32)] + [jax.ShapeDtypeStruct((ntok, panel), BF16)] * len(chip_masks),
        [mine, other], mine.size, 8 * mine.size,
        out_specs=[WHOLE] * len(here),
    )
    for mask, value in reversed(list(zip(chip_masks, sends))):
        summed = summed + swap(value, "hid", n_hid, mask).astype(F32)
    resid_cols = (x_cols + summed).astype(BF16)

    column = [swap(resid_cols, "tok", n_tok, d) for d in range(1, n_tok)]
    across = swap(resid_cols, "hid", n_hid, 6)
    line, farthest = stack_after([resid_cols, *column], (across,), 16)
    beside = [swap(line, "hid", n_hid, mask) for mask in (2, 4)]
    across_line = [swap(across, "tok", n_tok, d) for d in (1, 2)] + [swap(farthest, "hid", n_hid, 6)]
    line_far = swap(line, "hid", n_hid, 1)
    across_far = swap(across, "hid", n_hid, 1)
    line_slots = [[(d, mask) for d in range(n_tok)] for mask in range(n_hid)]
    gram, cross = gram_part(
        resid_cols, [line, line_far, across[None], across_far[None]],
        [line_slots[0], line_slots[1], [(0, 6)], [(0, 7)]], n_tok, n_hid, None, labels,
    )
    done = pltpu.with_memory_space_constraint(gram, pltpu.HBM)
    near = stack_after([*beside, *across_line], (done,))
    far = swap(near, "hid", n_hid, 1)
    for stack, core in ((near, 0), (far, 1)):
        slots = line_slots[2 + core] + line_slots[4 + core] + line_slots[6 + core][1:]
        gram, = gram_part(resid_cols, [stack], [slots], n_tok, n_hid, gram)
    return (gram, cross.T)


def plain(n_tok, n_hid, resid_in, norm_gain, gate_weight, up_weight, down_weight, labels):
    x = lax.all_gather(resid_in, "hid", axis=0, tiled=True).astype(F32)
    ntok, block = x.shape
    total_sq = lax.psum(jnp.sum(x * x, axis=1), "tok")
    normed = (x * lax.rsqrt(total_sq / float(D) + 1e-05)[:, None] * norm_gain[None, :]).astype(BF16)

    def summed_over_tok(weight):
        product = jnp.dot(normed, weight, preferred_element_type=F32).astype(BF16)
        return lax.psum_scatter(product, "tok", scatter_dimension=0, tiled=True).astype(F32)

    hidden = (jax.nn.silu(summed_over_tok(gate_weight)) * summed_over_tok(up_weight)).astype(BF16)
    hidden = lax.all_gather(hidden, "tok", axis=0, tiled=True)
    partial_out = jnp.dot(hidden, down_weight, preferred_element_type=F32).astype(BF16)
    summed = lax.psum_scatter(partial_out, "hid", scatter_dimension=1, tiled=True).astype(F32)
    panel = block // n_hid
    x_cols = lax.dynamic_slice_in_dim(x, lax.axis_index("hid") * panel, panel, 1)
    resid_cols = (x_cols + summed).astype(BF16)
    everyone = lax.all_gather(resid_cols, ("tok", "hid"), axis=1, tiled=True)
    gram = lax.dot_general(
        resid_cols, everyone, (((0,), (0,)), ((), ())), preferred_element_type=F32
    ) / float(ntok)
    return (gram, class_means(resid_cols, labels))


def on_device(n_tok, n_hid, resid_in, norm_gain, gate_weight, *rest):
    panel = resid_in.shape[1] // n_hid
    fits = n_tok == 4 and n_hid == 8 and panel % 128 == 0 and gate_weight.shape[1] % TILE == 0 and gate_weight.shape[1] >= 3 * TILE
    body = on_line if fits else plain
    return body(n_tok, n_hid, resid_in, norm_gain, gate_weight, *rest)


def solution(mesh):
    return jax.shard_map(
        functools.partial(on_device, mesh.shape["tok"], mesh.shape["hid"]),
        mesh=mesh,
        in_specs=(
            P("hid", "tok"),
            P("tok"),
            P("tok", "hid"),
            P("tok", "hid"),
            P("hid", "tok"),
            P(),
        ),
        out_specs=(P(("tok", "hid"), None), P(("tok", "hid"), None)),
        check_vma=False,
    )
```

```python
import functools
import jax
import jax.numpy as jnp
from jax import lax
from jax.experimental import pallas as pl
from jax.experimental.pallas import tpu as pltpu
from jax.sharding import PartitionSpec as P

D = 8192
CLASSES = 64
TILE = 256
BF16 = jnp.bfloat16
F32 = jnp.float32
WHOLE = pl.BlockSpec(memory_space=pltpu.VMEM)
ANYWHERE = pl.BlockSpec(memory_space=pl.ANY)
SIDE = 128


def swap(value, axis, size, mask):
    return lax.ppermute(value, axis, [(i, i ^ mask) for i in range(size)])


def run(body, name, out_shape, operands, flops, bytes_accessed, in_specs=None, out_specs=WHOLE, **more):
    return pl.pallas_call(
        body,
        out_shape=out_shape,
        in_specs=[WHOLE] * len(operands) if in_specs is None else in_specs,
        out_specs=out_specs,
        compiler_params=pltpu.CompilerParams(vmem_limit_bytes=16 * 1024 * 1024),
        cost_estimate=pl.CostEstimate(flops=flops, bytes_accessed=bytes_accessed, transcendentals=0),
        name=name,
        **more,
    )(*operands)


def fetch(pieces, after, name):
    count = len(pieces)
    copies = []
    for number, (array, row, rows, column, columns) in enumerate(pieces):
        step = min(rows, 256)
        copies += [(number, at, step, row + at, column, columns) for at in range(0, rows, step)]

    def body(*refs):
        sources, targets, sems = refs[:count], refs[-1 - count:-1], refs[-1]
        started = []
        for sem, (number, at, step, row, column, columns) in enumerate(copies):
            copy = pltpu.make_async_copy(
                sources[number].at[pl.ds(row, step), pl.ds(column, columns)],
                targets[number].at[pl.ds(at, step), :],
                sems.at[sem],
            )
            copy.start()
            started.append(copy)
        for copy in started:
            copy.wait()

    size = sum(rows * columns * array.dtype.itemsize for array, _, rows, _, columns in pieces)
    return run(
        body, name,
        [pltpu.VMEM((rows, columns), array.dtype) for array, _, rows, _, columns in pieces],
        [pltpu.with_memory_space_constraint(piece[0], pltpu.HBM) for piece in pieces] + list(after),
        0, 0,
        in_specs=[ANYWHERE] * (count + len(after)),
        out_specs=[WHOLE] * count,
        scratch_shapes=[pltpu.SemaphoreType.DMA((len(copies),))],
    )


def tokens_kernel(masks, panel, *refs):
    blocks, gain, (lhs, cols, squares, x) = refs[:len(masks)], refs[len(masks)], refs[-4:]
    h = lax.axis_index("hid")
    rows = blocks[0].shape[0]
    for mask, block in zip(masks, blocks):
        x[pl.ds(pl.multiple_of((h ^ mask) * rows, rows), rows), :] = block[...]
    values = x[...].astype(F32)
    lhs[...] = (values * gain[...]).astype(BF16)
    squares[...] = jnp.sum(values * values, axis=1, keepdims=True)
    cols[...] = x[:, pl.ds(pl.multiple_of(h * panel, panel), panel)].astype(F32)


def split(value):
    lane = lax.broadcasted_iota(jnp.int32, (value.shape[0], SIDE), 1)
    out = jnp.zeros((value.shape[0], SIDE), F32)
    for part in range(3):
        rounded = value.astype(BF16).astype(F32)
        out = jnp.where(lane == part, rounded, out)
        value = value - rounded
    return out


def joined(parts):
    return jnp.sum(parts.astype(F32), axis=1, keepdims=True)


def gate_up_kernel(lhs_ref, gate_ref, up_ref, *refs):
    send_ref, keep_ref, both, side = refs[-4:]
    places = ((keep_ref, 0), (send_ref, 0), (keep_ref, 1), (send_ref, 1))
    rows = send_ref.shape[1]
    z = lax.axis_index("tok")
    lhs = lhs_ref[...]

    def hand_out(source, start, width):
        for d, (out, slot) in enumerate(places):
            at = pl.multiple_of((z ^ d) * rows, rows)
            out[slot, :, start:start + width] = source[pl.ds(at, rows), :].astype(BF16)

    for tile in range(gate_ref.shape[1] // TILE):
        cols = slice(tile * TILE, (tile + 1) * TILE)
        both[:, :TILE] = jnp.dot(lhs, gate_ref[:, cols], preferred_element_type=F32)
        both[:, TILE:] = jnp.dot(lhs, up_ref[:, cols], preferred_element_type=F32)
        hand_out(both, 2 * tile * TILE, 2 * TILE)
    if send_ref.shape[2] > 2 * gate_ref.shape[1]:
        side[...] = split(refs[0][...])
        hand_out(side, 2 * gate_ref.shape[1], SIDE)


def gate_up(lhs, gate, up, squares, n_tok, after=()):
    ntok, depth = lhs.shape
    width = gate.shape[1]
    rows = ntok // n_tok
    extra = [] if squares is None else [squares]
    shape = jax.ShapeDtypeStruct((2, rows, 2 * width + SIDE * len(extra)), BF16)
    return run(
        gate_up_kernel, "gate_up", [shape, shape], [lhs, gate, up, *extra, *after],
        0, 0,
        in_specs=[WHOLE] * (3 + len(extra)) + [ANYWHERE] * len(after),
        out_specs=[WHOLE] * 2,
        scratch_shapes=[pltpu.VMEM((ntok, 2 * TILE), F32), pltpu.VMEM((ntok, SIDE), F32)],
    )


def pair_total(keep, got, main, after):
    def body(keep_ref, got_ref, *refs):
        out = refs[-1]
        out[:, :main] = (keep_ref[1, :, :main].astype(F32) + got_ref[1, :, :main].astype(F32)).astype(BF16)
        if out.shape[1] > main:
            out[:, main:] = split(joined(keep_ref[1, :, main:]) + joined(got_ref[1, :, main:])).astype(BF16)

    size = keep.size // 2
    return run(
        body, "pair_total", jax.ShapeDtypeStruct(keep.shape[1:], BF16), [keep, got, *after],
        size, 6 * size, in_specs=[WHOLE] * 2 + [ANYWHERE] * len(after),
    )


def copy_after(value, after):
    def body(value_ref, *refs):
        refs[-1][...] = value_ref[...]

    return run(
        body, "copy", jax.ShapeDtypeStruct(value.shape, value.dtype), [value, *after],
        0, 4 * value.size, in_specs=[WHOLE] + [ANYWHERE] * len(after),
    )


def stack_after(blocks, after, extra=0):
    stacks = [block if block.ndim == 3 else block[None] for block in blocks]
    total = sum(stack.shape[0] for stack in stacks)
    rows = stacks[0].shape[1]

    def body(*refs):
        out = refs[len(stacks) + len(after)]
        at = 0
        for ref in refs[:len(stacks)]:
            out[at:at + ref.shape[0]] = ref[:, :rows, :]
            at += ref.shape[0]
        if extra:
            refs[-1][:rows, :] = out[at - 1]
            refs[-1][rows:, :] = out[at - 1, :extra, :]

    width, kind = blocks[0].shape[-1], blocks[0].dtype
    shapes = [jax.ShapeDtypeStruct((total, rows, width), kind)]
    shapes += [jax.ShapeDtypeStruct((rows + extra, width), kind)] if extra else []
    outs = run(
        body, "stack", shapes, [*stacks, *after], 0, 4 * sum(stack.size for stack in stacks),
        in_specs=[WHOLE] * len(stacks) + [ANYWHERE] * len(after),
        out_specs=[WHOLE] * len(shapes),
    )
    return outs if extra else outs[0]


def hidden_rows(chunks, widths, scale, after):
    rows = chunks[0][0].shape[1]
    given = [] if scale is None else [scale]

    def body(*refs):
        out_ref, scale_ref = refs[-2:]
        keep_ref, got_ref, over_ref = refs[:3]
        if scale is None:
            tail = slice(2 * widths[0], 2 * widths[0] + SIDE)
            squares = joined(keep_ref[0, :, tail]) + joined(got_ref[0, :, tail]) + joined(over_ref[:, tail])
            factor = lax.rsqrt(squares / float(D) + 1e-05)
        else:
            factor = refs[3 * len(chunks)][...]
        scale_ref[...] = factor
        start = 0
        for k, width in enumerate(widths):
            keep_ref, got_ref, over_ref = refs[3 * k:3 * k + 3]

            def total(at):
                cols = slice(at, at + TILE)
                return (
                    keep_ref[0, :, cols].astype(F32) + got_ref[0, :, cols].astype(F32) + over_ref[:, cols].astype(F32)
                ) * factor

            for at in range(0, width, TILE):
                gate, up = total(2 * at), total(2 * at + TILE)
                out_ref[:, start + at:start + at + TILE] = (jax.nn.silu(gate) * up).astype(BF16)
            start += width

    size = rows * sum(widths)
    return run(
        body, "hidden",
        [jax.ShapeDtypeStruct((rows, sum(widths)), BF16), jax.ShapeDtypeStruct((rows, 1), F32)],
        [part for chunk in chunks for part in chunk] + given + list(after), 20 * size, 14 * size,
        in_specs=[WHOLE] * (3 * len(chunks) + len(given)) + [ANYWHERE] * len(after),
        out_specs=[WHOLE] * 2,
    )


def down_kernel(masks, panel, n_blocks, add, *refs):
    blocks, weight, lhs, out = refs[:n_blocks], refs[n_blocks], refs[-1], refs[-2]
    before = refs[n_blocks + 1] if add else None
    z = lax.axis_index("tok")
    h = lax.axis_index("hid")
    rows = blocks[0].shape[0]
    for d, block in enumerate(blocks):
        lhs[pl.ds(pl.multiple_of((z ^ d) * rows, rows), rows), :] = block[...]
    values = lhs[...]
    for slot, mask in enumerate(masks):
        column = pl.multiple_of((h ^ mask) * panel, panel)
        total = jnp.dot(values, weight[:, pl.ds(column, panel)], preferred_element_type=F32)
        if before is not None:
            total = total + before[slot]
        out[slot] = total.astype(out.dtype)


def down(blocks, weight, masks, panel, kind, before=None, after=()):
    rows, depth = blocks[0].shape
    ntok = rows * len(blocks)
    return run(
        functools.partial(down_kernel, masks, panel, len(blocks), before is not None), "down",
        jax.ShapeDtypeStruct((len(masks), ntok, panel), kind),
        [*blocks, weight] + ([] if before is None else [before]) + list(after),
        2 * ntok * depth * panel * len(masks), 2 * depth * panel * len(masks),
        in_specs=[WHOLE] * (len(blocks) + 1 + (before is not None)) + [ANYWHERE] * len(after),
        scratch_shapes=[pltpu.VMEM((ntok, depth), BF16)],
    )


def chip_sum_kernel(mine_ref, other_ref, own_ref, *outs):
    own_ref[...] = mine_ref[0] + other_ref[0].astype(F32)
    for e, out in enumerate(outs):
        out[...] = (mine_ref[e + 1] + other_ref[e + 1].astype(F32)).astype(BF16)


def gram_kernel(slots, n_hid, ntok, classes, own_ref, *refs):
    stacks = refs[:len(slots)]
    outs, (tiles, sems) = refs[:-2], refs[-2:]
    out_ref = outs[-2] if classes else outs[-1]
    z = lax.axis_index("tok")
    h = lax.axis_index("hid")
    width = own_ref.shape[1]
    left = own_ref[...].T
    copies = []
    for stack, places in zip(stacks, slots):
        for at, (d, mask) in enumerate(places):
            number = len(copies)
            tiles[number] = jnp.dot(left, stack[at], preferred_element_type=F32) * (1.0 / ntok)
            column = ((z ^ d) * n_hid + (h ^ mask)) * width
            copy = pltpu.make_async_copy(
                tiles.at[number], out_ref.at[:, pl.ds(pl.multiple_of(column, width), width)], sems.at[number]
            )
            copy.start()
            copies.append(copy)
    if classes:
        labels, cross_ref = refs[len(slots)], outs[-1]
        onehot = (labels[...] == lax.broadcasted_iota(jnp.int32, (classes, ntok), 0)).astype(F32)
        counts = jnp.sum(onehot, axis=1, keepdims=True)
        sums = jnp.dot(onehot.astype(BF16), own_ref[...], preferred_element_type=F32)
        cross_ref[...] = sums / jnp.maximum(counts, 1.0)
    for copy in copies:
        copy.wait()


def gram_part(resid_cols, stacks, slots, n_tok, n_hid, before, labels=None):
    ntok, width = resid_cols.shape
    here = sum(len(places) for places in slots)
    gram_shape = pltpu.HBM((width, width * n_tok * n_hid), F32)
    extra, extra_specs = ([], []) if labels is None else ([labels[None, :]], [WHOLE])
    if before is not None:
        extra, extra_specs = extra + [before], extra_specs + [ANYWHERE]
    return run(
        functools.partial(gram_kernel, slots, n_hid, ntok, 0 if labels is None else CLASSES), "gram",
        [gram_shape] + ([] if labels is None else [jax.ShapeDtypeStruct((CLASSES, width), F32)]),
        [resid_cols, *stacks, *extra],
        2 * ntok * width * width * here, 4 * width * width * here,
        in_specs=[WHOLE] * (1 + len(stacks)) + extra_specs,
        out_specs=[ANYWHERE] + ([] if labels is None else [WHOLE]),
        input_output_aliases={} if before is None else {len(stacks) + len(extra): 0},
        scratch_shapes=[pltpu.VMEM((here, width, width), F32), pltpu.SemaphoreType.DMA((here,))],
    )


def class_means(resid_cols, labels):
    onehot = (labels[:, None] == jnp.arange(CLASSES, dtype=jnp.int32)[None, :]).astype(BF16)
    counts = jnp.sum(onehot.astype(F32), axis=0)
    class_sums = lax.dot_general(
        resid_cols, onehot, (((0,), (0,)), ((), ())), preferred_element_type=F32
    )
    return class_sums / jnp.maximum(counts, 1.0)[None, :]


def on_line(n_tok, n_hid, resid_in, norm_gain, gate_weight, up_weight, down_weight, labels):
    rows, block = resid_in.shape
    ntok, panel = rows * n_hid, block // n_hid
    depth, shard_ff = gate_weight.shape
    tiles = shard_ff // TILE
    ends = [0, TILE * (3 * tiles // 7), TILE * (11 * tiles // 14), shard_ff]
    chip_masks = list(range(2, n_hid, 2))

    def part(weight, k):
        return weight, 0, depth, ends[k], ends[k + 1] - ends[k]

    near = [resid_in] + [swap(resid_in, "hid", n_hid, mask) for mask in chip_masks]
    gate_0, up_0, own_x, gain = fetch(
        [
            part(gate_weight, 0),
            part(up_weight, 0),
            (resid_in, 0, rows, 0, block),
            (norm_gain[None, :], 0, 1, 0, block),
        ],
        (), "fetch_first",
    )
    relayed = copy_after(near[1], (gain,))
    far = [swap(piece, "hid", n_hid, 1) for piece in [near[0], relayed, *near[2:]]]
    masks = [0] + chip_masks + [1] + [mask + 1 for mask in chip_masks]
    lhs, x_cols, squares = run(
        functools.partial(tokens_kernel, masks, panel), "tokens",
        (
            jax.ShapeDtypeStruct((ntok, block), BF16),
            jax.ShapeDtypeStruct((ntok, panel), F32),
            jax.ShapeDtypeStruct((ntok, 1), F32),
        ),
        [own_x, *near[1:], *far, gain],
        4 * ntok * block, 4 * ntok * block,
        out_specs=(WHOLE, WHOLE, WHOLE),
        scratch_shapes=[pltpu.VMEM((ntok, block), BF16)],
    )

    widths = [ends[k + 1] - ends[k] for k in range(3)]
    send_0, keep_0 = gate_up(lhs, gate_0, up_0, squares, n_tok)
    got_0 = swap(send_0, "tok", n_tok, 1)
    gate_1, up_1 = fetch([part(gate_weight, 1), part(up_weight, 1)], (send_0,), "fetch_gate_up")
    send_1, keep_1 = gate_up(lhs, gate_1, up_1, None, n_tok)
    got_1 = swap(send_1, "tok", n_tok, 1)
    sum_0 = pair_total(keep_0, got_0, 2 * widths[0], (send_1,))
    over_0 = swap(sum_0, "tok", n_tok, 2)
    gate_2, up_2 = fetch([part(gate_weight, 2), part(up_weight, 2)], (sum_0,), "fetch_gate_up")
    send_2, keep_2 = gate_up(lhs, gate_2, up_2, None, n_tok)
    got_2 = swap(send_2, "tok", n_tok, 1)
    sum_1 = pair_total(keep_1, got_1, 2 * widths[1], (send_2,))
    over_1 = swap(sum_1, "tok", n_tok, 2)
    down_b, = fetch([(down_weight, ends[1], shard_ff - ends[1], 0, block)], (sum_1,), "fetch_down")
    sum_2 = pair_total(keep_2, got_2, 2 * widths[2], (down_b,))
    over_2 = swap(sum_2, "tok", n_tok, 2)

    a_own, scale = hidden_rows([(keep_0, got_0, over_0)], widths[:1], None, (sum_1,))
    a_two = swap(a_own, "tok", n_tok, 2)
    a_one = swap(a_own, "tok", n_tok, 1)
    a_three = swap(a_two, "tok", n_tok, 1)
    down_a, = fetch([(down_weight, 0, ends[1], 0, block)], (sum_2,), "fetch_down")
    b_own, _ = hidden_rows([(keep_1, got_1, over_1), (keep_2, got_2, over_2)], widths[1:], scale, (a_one, a_three, down_a))
    b_two = swap(b_own, "tok", n_tok, 2)
    b_one = swap(b_own, "tok", n_tok, 1)
    b_three = swap(b_two, "tok", n_tok, 1)
    hidden_a = [a_own, a_one, a_two, a_three]
    hidden_b = [b_own, b_one, b_two, b_three]

    here = [0] + chip_masks
    there = [mask + 1 for mask in here]
    other = down(hidden_b, down_b, there, panel, BF16, down(hidden_a, down_a, there, panel, F32))
    mine = down(hidden_b, down_b, here, panel, F32, down(hidden_a, down_a, here, panel, F32, after=(other,)))
    other = swap(other, "hid", n_hid, 1)
    summed, *sends = run(
        chip_sum_kernel, "chip_sum",
        [jax.ShapeDtypeStruct((ntok, panel), F32)] + [jax.ShapeDtypeStruct((ntok, panel), BF16)] * len(chip_masks),
        [mine, other], mine.size, 8 * mine.size,
        out_specs=[WHOLE] * len(here),
    )
    for mask, value in reversed(list(zip(chip_masks, sends))):
        summed = summed + swap(value, "hid", n_hid, mask).astype(F32)
    resid_cols = (x_cols + summed).astype(BF16)

    column = [swap(resid_cols, "tok", n_tok, d) for d in range(1, n_tok)]
    across = swap(resid_cols, "hid", n_hid, 6)
    line, farthest = stack_after([resid_cols, *column], (across,), 16)
    beside = [swap(line, "hid", n_hid, mask) for mask in (2, 4)]
    across_line = [swap(across, "tok", n_tok, d) for d in (1, 2)] + [swap(farthest, "hid", n_hid, 6)]
    line_far = swap(line, "hid", n_hid, 1)
    across_far = swap(across, "hid", n_hid, 1)
    line_slots = [[(d, mask) for d in range(n_tok)] for mask in range(n_hid)]
    gram, cross = gram_part(
        resid_cols, [line, line_far, across[None], across_far[None]],
        [line_slots[0], line_slots[1], [(0, 6)], [(0, 7)]], n_tok, n_hid, None, labels,
    )
    done = pltpu.with_memory_space_constraint(gram, pltpu.HBM)
    near = stack_after([*beside, *across_line], (done,))
    far = swap(near, "hid", n_hid, 1)
    for stack, core in ((near, 0), (far, 1)):
        slots = line_slots[2 + core] + line_slots[4 + core] + line_slots[6 + core][1:]
        gram, = gram_part(resid_cols, [stack], [slots], n_tok, n_hid, gram)
    return (gram, cross.T)


def plain(n_tok, n_hid, resid_in, norm_gain, gate_weight, up_weight, down_weight, labels):
    x = lax.all_gather(resid_in, "hid", axis=0, tiled=True).astype(F32)
    ntok, block = x.shape
    total_sq = lax.psum(jnp.sum(x * x, axis=1), "tok")
    normed = (x * lax.rsqrt(total_sq / float(D) + 1e-05)[:, None] * norm_gain[None, :]).astype(BF16)

    def summed_over_tok(weight):
        product = jnp.dot(normed, weight, preferred_element_type=F32).astype(BF16)
        return lax.psum_scatter(product, "tok", scatter_dimension=0, tiled=True).astype(F32)

    hidden = (jax.nn.silu(summed_over_tok(gate_weight)) * summed_over_tok(up_weight)).astype(BF16)
    hidden = lax.all_gather(hidden, "tok", axis=0, tiled=True)
    partial_out = jnp.dot(hidden, down_weight, preferred_element_type=F32).astype(BF16)
    summed = lax.psum_scatter(partial_out, "hid", scatter_dimension=1, tiled=True).astype(F32)
    panel = block // n_hid
    x_cols = lax.dynamic_slice_in_dim(x, lax.axis_index("hid") * panel, panel, 1)
    resid_cols = (x_cols + summed).astype(BF16)
    everyone = lax.all_gather(resid_cols, ("tok", "hid"), axis=1, tiled=True)
    gram = lax.dot_general(
        resid_cols, everyone, (((0,), (0,)), ((), ())), preferred_element_type=F32
    ) / float(ntok)
    return (gram, class_means(resid_cols, labels))


def on_device(n_tok, n_hid, resid_in, norm_gain, gate_weight, *rest):
    panel = resid_in.shape[1] // n_hid
    fits = n_tok == 4 and n_hid == 8 and panel % 128 == 0 and gate_weight.shape[1] % TILE == 0 and gate_weight.shape[1] >= 3 * TILE
    body = on_line if fits else plain
    return body(n_tok, n_hid, resid_in, norm_gain, gate_weight, *rest)


def solution(mesh):
    return jax.shard_map(
        functools.partial(on_device, mesh.shape["tok"], mesh.shape["hid"]),
        mesh=mesh,
        in_specs=(
            P("hid", "tok"),
            P("tok"),
            P("tok", "hid"),
            P("tok", "hid"),
            P("hid", "tok"),
            P(),
        ),
        out_specs=(P(("tok", "hid"), None), P(("tok", "hid"), None)),
        check_vma=False,
    )
```

```python
import functools
import jax
import jax.numpy as jnp
from jax import lax
from jax.experimental import pallas as pl
from jax.experimental.pallas import tpu as pltpu
from jax.sharding import PartitionSpec as P

D = 8192
CLASSES = 64
TILE = 256
BF16 = jnp.bfloat16
F32 = jnp.float32
WHOLE = pl.BlockSpec(memory_space=pltpu.VMEM)
ANYWHERE = pl.BlockSpec(memory_space=pl.ANY)
SIDE = 128


def swap(value, axis, size, mask):
    return lax.ppermute(value, axis, [(i, i ^ mask) for i in range(size)])


def run(body, name, out_shape, operands, flops, bytes_accessed, in_specs=None, out_specs=WHOLE, **more):
    return pl.pallas_call(
        body,
        out_shape=out_shape,
        in_specs=[WHOLE] * len(operands) if in_specs is None else in_specs,
        out_specs=out_specs,
        compiler_params=pltpu.CompilerParams(vmem_limit_bytes=16 * 1024 * 1024),
        cost_estimate=pl.CostEstimate(flops=flops, bytes_accessed=bytes_accessed, transcendentals=0),
        name=name,
        **more,
    )(*operands)


def fetch(pieces, after, name):
    count = len(pieces)
    copies = []
    for number, (array, row, rows, column, columns) in enumerate(pieces):
        step = min(rows, 256)
        copies += [(number, at, step, row + at, column, columns) for at in range(0, rows, step)]

    def body(*refs):
        sources, targets, sems = refs[:count], refs[-1 - count:-1], refs[-1]
        started = []
        for sem, (number, at, step, row, column, columns) in enumerate(copies):
            copy = pltpu.make_async_copy(
                sources[number].at[pl.ds(row, step), pl.ds(column, columns)],
                targets[number].at[pl.ds(at, step), :],
                sems.at[sem],
            )
            copy.start()
            started.append(copy)
        for copy in started:
            copy.wait()

    size = sum(rows * columns * array.dtype.itemsize for array, _, rows, _, columns in pieces)
    return run(
        body, name,
        [pltpu.VMEM((rows, columns), array.dtype) for array, _, rows, _, columns in pieces],
        [pltpu.with_memory_space_constraint(piece[0], pltpu.HBM) for piece in pieces] + list(after),
        0, 0,
        in_specs=[ANYWHERE] * (count + len(after)),
        out_specs=[WHOLE] * count,
        scratch_shapes=[pltpu.SemaphoreType.DMA((len(copies),))],
    )


def tokens_kernel(masks, panel, *refs):
    blocks, gain, (lhs, cols, squares, x) = refs[:len(masks)], refs[len(masks)], refs[-4:]
    h = lax.axis_index("hid")
    rows = blocks[0].shape[0]
    for mask, block in zip(masks, blocks):
        x[pl.ds(pl.multiple_of((h ^ mask) * rows, rows), rows), :] = block[...]
    values = x[...].astype(F32)
    lhs[...] = (values * gain[...]).astype(BF16)
    squares[...] = jnp.sum(values * values, axis=1, keepdims=True)
    cols[...] = x[:, pl.ds(pl.multiple_of(h * panel, panel), panel)].astype(F32)


def split(value):
    lane = lax.broadcasted_iota(jnp.int32, (value.shape[0], SIDE), 1)
    out = jnp.zeros((value.shape[0], SIDE), F32)
    for part in range(3):
        rounded = value.astype(BF16).astype(F32)
        out = jnp.where(lane == part, rounded, out)
        value = value - rounded
    return out


def joined(parts):
    return jnp.sum(parts.astype(F32), axis=1, keepdims=True)


def gate_up_kernel(lhs_ref, gate_ref, up_ref, *refs):
    send_ref, keep_ref, both, side = refs[-4:]
    places = ((keep_ref, 0), (send_ref, 0), (keep_ref, 1), (send_ref, 1))
    rows = send_ref.shape[1]
    z = lax.axis_index("tok")
    lhs = lhs_ref[...]

    def hand_out(source, start, width):
        for d, (out, slot) in enumerate(places):
            at = pl.multiple_of((z ^ d) * rows, rows)
            out[slot, :, start:start + width] = source[pl.ds(at, rows), :].astype(BF16)

    for tile in range(gate_ref.shape[1] // TILE):
        cols = slice(tile * TILE, (tile + 1) * TILE)
        both[:, :TILE] = jnp.dot(lhs, gate_ref[:, cols], preferred_element_type=F32)
        both[:, TILE:] = jnp.dot(lhs, up_ref[:, cols], preferred_element_type=F32)
        hand_out(both, 2 * tile * TILE, 2 * TILE)
    if send_ref.shape[2] > 2 * gate_ref.shape[1]:
        side[...] = split(refs[0][...])
        hand_out(side, 2 * gate_ref.shape[1], SIDE)


def gate_up(lhs, gate, up, squares, n_tok, after=()):
    ntok, depth = lhs.shape
    width = gate.shape[1]
    rows = ntok // n_tok
    extra = [] if squares is None else [squares]
    shape = jax.ShapeDtypeStruct((2, rows, 2 * width + SIDE * len(extra)), BF16)
    return run(
        gate_up_kernel, "gate_up", [shape, shape], [lhs, gate, up, *extra, *after],
        0, 0,
        in_specs=[WHOLE] * (3 + len(extra)) + [ANYWHERE] * len(after),
        out_specs=[WHOLE] * 2,
        scratch_shapes=[pltpu.VMEM((ntok, 2 * TILE), F32), pltpu.VMEM((ntok, SIDE), F32)],
    )


def pair_total(keep, got, main, after):
    def body(keep_ref, got_ref, *refs):
        out = refs[-1]
        out[:, :main] = (keep_ref[1, :, :main].astype(F32) + got_ref[1, :, :main].astype(F32)).astype(BF16)
        if out.shape[1] > main:
            out[:, main:] = split(joined(keep_ref[1, :, main:]) + joined(got_ref[1, :, main:])).astype(BF16)

    size = keep.size // 2
    return run(
        body, "pair_total", jax.ShapeDtypeStruct(keep.shape[1:], BF16), [keep, got, *after],
        size, 6 * size, in_specs=[WHOLE] * 2 + [ANYWHERE] * len(after),
    )


def copy_after(value, after):
    def body(value_ref, *refs):
        refs[-1][...] = value_ref[...]

    return run(
        body, "copy", jax.ShapeDtypeStruct(value.shape, value.dtype), [value, *after],
        0, 4 * value.size, in_specs=[WHOLE] + [ANYWHERE] * len(after),
    )


def stack_after(blocks, after, extra=0):
    stacks = [block if block.ndim == 3 else block[None] for block in blocks]
    total = sum(stack.shape[0] for stack in stacks)
    rows = stacks[0].shape[1]

    def body(*refs):
        out = refs[len(stacks) + len(after)]
        at = 0
        for ref in refs[:len(stacks)]:
            out[at:at + ref.shape[0]] = ref[:, :rows, :]
            at += ref.shape[0]
        if extra:
            refs[-1][:rows, :] = out[at - 1]
            refs[-1][rows:, :] = out[at - 1, :extra, :]

    width, kind = blocks[0].shape[-1], blocks[0].dtype
    shapes = [jax.ShapeDtypeStruct((total, rows, width), kind)]
    shapes += [jax.ShapeDtypeStruct((rows + extra, width), kind)] if extra else []
    outs = run(
        body, "stack", shapes, [*stacks, *after], 0, 4 * sum(stack.size for stack in stacks),
        in_specs=[WHOLE] * len(stacks) + [ANYWHERE] * len(after),
        out_specs=[WHOLE] * len(shapes),
    )
    return outs if extra else outs[0]


def hidden_rows(chunks, widths, scale, after):
    rows = chunks[0][0].shape[1]
    given = [] if scale is None else [scale]

    def body(*refs):
        out_ref, scale_ref = refs[-2:]
        keep_ref, got_ref, over_ref = refs[:3]
        if scale is None:
            tail = slice(2 * widths[0], 2 * widths[0] + SIDE)
            squares = joined(keep_ref[0, :, tail]) + joined(got_ref[0, :, tail]) + joined(over_ref[:, tail])
            factor = lax.rsqrt(squares / float(D) + 1e-05)
        else:
            factor = refs[3 * len(chunks)][...]
        scale_ref[...] = factor
        start = 0
        for k, width in enumerate(widths):
            keep_ref, got_ref, over_ref = refs[3 * k:3 * k + 3]

            def total(at):
                cols = slice(at, at + TILE)
                return (
                    keep_ref[0, :, cols].astype(F32) + got_ref[0, :, cols].astype(F32) + over_ref[:, cols].astype(F32)
                ) * factor

            for at in range(0, width, TILE):
                gate, up = total(2 * at), total(2 * at + TILE)
                out_ref[:, start + at:start + at + TILE] = (jax.nn.silu(gate) * up).astype(BF16)
            start += width

    size = rows * sum(widths)
    return run(
        body, "hidden",
        [jax.ShapeDtypeStruct((rows, sum(widths)), BF16), jax.ShapeDtypeStruct((rows, 1), F32)],
        [part for chunk in chunks for part in chunk] + given + list(after), 20 * size, 14 * size,
        in_specs=[WHOLE] * (3 * len(chunks) + len(given)) + [ANYWHERE] * len(after),
        out_specs=[WHOLE] * 2,
    )


def down_kernel(masks, panel, n_blocks, add, *refs):
    blocks, weight, lhs, out = refs[:n_blocks], refs[n_blocks], refs[-1], refs[-2]
    before = refs[n_blocks + 1] if add else None
    z = lax.axis_index("tok")
    h = lax.axis_index("hid")
    rows = blocks[0].shape[0]
    for d, block in enumerate(blocks):
        lhs[pl.ds(pl.multiple_of((z ^ d) * rows, rows), rows), :] = block[...]
    values = lhs[...]
    for slot, mask in enumerate(masks):
        column = pl.multiple_of((h ^ mask) * panel, panel)
        total = jnp.dot(values, weight[:, pl.ds(column, panel)], preferred_element_type=F32)
        if before is not None:
            total = total + before[slot]
        out[slot] = total.astype(out.dtype)


def down(blocks, weight, masks, panel, kind, before=None, after=()):
    rows, depth = blocks[0].shape
    ntok = rows * len(blocks)
    return run(
        functools.partial(down_kernel, masks, panel, len(blocks), before is not None), "down",
        jax.ShapeDtypeStruct((len(masks), ntok, panel), kind),
        [*blocks, weight] + ([] if before is None else [before]) + list(after),
        2 * ntok * depth * panel * len(masks), 2 * depth * panel * len(masks),
        in_specs=[WHOLE] * (len(blocks) + 1 + (before is not None)) + [ANYWHERE] * len(after),
        scratch_shapes=[pltpu.VMEM((ntok, depth), BF16)],
    )


def chip_sum_kernel(mine_ref, other_ref, own_ref, *outs):
    own_ref[...] = mine_ref[0] + other_ref[0].astype(F32)
    for e, out in enumerate(outs):
        out[...] = (mine_ref[e + 1] + other_ref[e + 1].astype(F32)).astype(BF16)


def gram_kernel(slots, n_hid, ntok, classes, own_ref, *refs):
    stacks = refs[:len(slots)]
    outs, (tiles, sems) = refs[:-2], refs[-2:]
    out_ref = outs[-2] if classes else outs[-1]
    z = lax.axis_index("tok")
    h = lax.axis_index("hid")
    width = own_ref.shape[1]
    left = own_ref[...].T
    copies = []
    for stack, places in zip(stacks, slots):
        for at, (d, mask) in enumerate(places):
            number = len(copies)
            tiles[number] = jnp.dot(left, stack[at], preferred_element_type=F32) * (1.0 / ntok)
            column = ((z ^ d) * n_hid + (h ^ mask)) * width
            copy = pltpu.make_async_copy(
                tiles.at[number], out_ref.at[:, pl.ds(pl.multiple_of(column, width), width)], sems.at[number]
            )
            copy.start()
            copies.append(copy)
    if classes:
        labels, cross_ref = refs[len(slots)], outs[-1]
        onehot = (labels[...] == lax.broadcasted_iota(jnp.int32, (classes, ntok), 0)).astype(F32)
        counts = jnp.sum(onehot, axis=1, keepdims=True)
        sums = jnp.dot(onehot.astype(BF16), own_ref[...], preferred_element_type=F32)
        cross_ref[...] = sums / jnp.maximum(counts, 1.0)
    for copy in copies:
        copy.wait()


def gram_part(resid_cols, stacks, slots, n_tok, n_hid, before, labels=None):
    ntok, width = resid_cols.shape
    here = sum(len(places) for places in slots)
    gram_shape = pltpu.HBM((width, width * n_tok * n_hid), F32)
    extra, extra_specs = ([], []) if labels is None else ([labels[None, :]], [WHOLE])
    if before is not None:
        extra, extra_specs = extra + [before], extra_specs + [ANYWHERE]
    return run(
        functools.partial(gram_kernel, slots, n_hid, ntok, 0 if labels is None else CLASSES), "gram",
        [gram_shape] + ([] if labels is None else [jax.ShapeDtypeStruct((CLASSES, width), F32)]),
        [resid_cols, *stacks, *extra],
        2 * ntok * width * width * here, 4 * width * width * here,
        in_specs=[WHOLE] * (1 + len(stacks)) + extra_specs,
        out_specs=[ANYWHERE] + ([] if labels is None else [WHOLE]),
        input_output_aliases={} if before is None else {len(stacks) + len(extra): 0},
        scratch_shapes=[pltpu.VMEM((here, width, width), F32), pltpu.SemaphoreType.DMA((here,))],
    )


def class_means(resid_cols, labels):
    onehot = (labels[:, None] == jnp.arange(CLASSES, dtype=jnp.int32)[None, :]).astype(BF16)
    counts = jnp.sum(onehot.astype(F32), axis=0)
    class_sums = lax.dot_general(
        resid_cols, onehot, (((0,), (0,)), ((), ())), preferred_element_type=F32
    )
    return class_sums / jnp.maximum(counts, 1.0)[None, :]


def on_line(n_tok, n_hid, resid_in, norm_gain, gate_weight, up_weight, down_weight, labels):
    rows, block = resid_in.shape
    ntok, panel = rows * n_hid, block // n_hid
    depth, shard_ff = gate_weight.shape
    tiles = shard_ff // TILE
    ends = [0, TILE * (4 * tiles // 7), shard_ff]
    chip_masks = list(range(2, n_hid, 2))

    def part(weight, k):
        return weight, 0, depth, ends[k], ends[k + 1] - ends[k]

    near = [resid_in] + [swap(resid_in, "hid", n_hid, mask) for mask in chip_masks]
    gate_0, up_0, own_x, gain = fetch(
        [
            part(gate_weight, 0),
            part(up_weight, 0),
            (resid_in, 0, rows, 0, block),
            (norm_gain[None, :], 0, 1, 0, block),
        ],
        (), "fetch_first",
    )
    relayed = copy_after(near[1], (gain,))
    far = [swap(piece, "hid", n_hid, 1) for piece in [near[0], relayed, *near[2:]]]
    masks = [0] + chip_masks + [1] + [mask + 1 for mask in chip_masks]
    lhs, x_cols, squares = run(
        functools.partial(tokens_kernel, masks, panel), "tokens",
        (
            jax.ShapeDtypeStruct((ntok, block), BF16),
            jax.ShapeDtypeStruct((ntok, panel), F32),
            jax.ShapeDtypeStruct((ntok, 1), F32),
        ),
        [own_x, *near[1:], *far, gain],
        4 * ntok * block, 4 * ntok * block,
        out_specs=(WHOLE, WHOLE, WHOLE),
        scratch_shapes=[pltpu.VMEM((ntok, block), BF16)],
    )

    widths = [ends[k + 1] - ends[k] for k in range(2)]
    send_0, keep_0 = gate_up(lhs, gate_0, up_0, squares, n_tok)
    got_0 = swap(send_0, "tok", n_tok, 1)
    gate_1, up_1 = fetch([part(gate_weight, 1), part(up_weight, 1)], (send_0,), "fetch_gate_up")
    send_1, keep_1 = gate_up(lhs, gate_1, up_1, None, n_tok)
    got_1 = swap(send_1, "tok", n_tok, 1)
    sum_0 = pair_total(keep_0, got_0, 2 * widths[0], (send_1,))
    over_0 = swap(sum_0, "tok", n_tok, 2)
    down_a, down_b = fetch(
        [(down_weight, 0, ends[1], 0, block), (down_weight, ends[1], widths[1], 0, block)], (sum_0,), "fetch_down"
    )
    sum_1 = pair_total(keep_1, got_1, 2 * widths[1], (down_a,))
    over_1 = swap(sum_1, "tok", n_tok, 2)

    a_own, scale = hidden_rows([(keep_0, got_0, over_0)], widths[:1], None, (sum_1,))
    a_two = swap(a_own, "tok", n_tok, 2)
    a_one = swap(a_own, "tok", n_tok, 1)
    a_three = swap(a_two, "tok", n_tok, 1)
    b_own, _ = hidden_rows([(keep_1, got_1, over_1)], widths[1:], scale, (a_one, a_two))
    b_two = swap(b_own, "tok", n_tok, 2)
    b_one = swap(b_own, "tok", n_tok, 1)
    b_three = swap(b_two, "tok", n_tok, 1)
    hidden_a = [a_own, a_one, a_two, a_three]
    hidden_b = [b_own, b_one, b_two, b_three]

    here = [0] + chip_masks
    there = [mask + 1 for mask in here]
    other = down(hidden_b, down_b, there, panel, BF16, down(hidden_a, down_a, there, panel, F32))
    mine = down(hidden_b, down_b, here, panel, F32, down(hidden_a, down_a, here, panel, F32, after=(other,)))
    other = swap(other, "hid", n_hid, 1)
    summed, *sends = run(
        chip_sum_kernel, "chip_sum",
        [jax.ShapeDtypeStruct((ntok, panel), F32)] + [jax.ShapeDtypeStruct((ntok, panel), BF16)] * len(chip_masks),
        [mine, other], mine.size, 8 * mine.size,
        out_specs=[WHOLE] * len(here),
    )
    for mask, value in reversed(list(zip(chip_masks, sends))):
        summed = summed + swap(value, "hid", n_hid, mask).astype(F32)
    resid_cols = (x_cols + summed).astype(BF16)

    column = [swap(resid_cols, "tok", n_tok, d) for d in range(1, n_tok)]
    across = swap(resid_cols, "hid", n_hid, 6)
    line, farthest = stack_after([resid_cols, *column], (across,), 16)
    beside = [swap(line, "hid", n_hid, mask) for mask in (2, 4)]
    across_line = [swap(across, "tok", n_tok, d) for d in (1, 2)] + [swap(farthest, "hid", n_hid, 6)]
    line_far = swap(line, "hid", n_hid, 1)
    across_far = swap(across, "hid", n_hid, 1)
    line_slots = [[(d, mask) for d in range(n_tok)] for mask in range(n_hid)]
    gram, cross = gram_part(
        resid_cols, [line, line_far, across[None], across_far[None]],
        [line_slots[0], line_slots[1], [(0, 6)], [(0, 7)]], n_tok, n_hid, None, labels,
    )
    done = pltpu.with_memory_space_constraint(gram, pltpu.HBM)
    near = stack_after([*beside, *across_line], (done,))
    far = swap(near, "hid", n_hid, 1)
    for stack, core in ((near, 0), (far, 1)):
        slots = line_slots[2 + core] + line_slots[4 + core] + line_slots[6 + core][1:]
        gram, = gram_part(resid_cols, [stack], [slots], n_tok, n_hid, gram)
    return (gram, cross.T)


def plain(n_tok, n_hid, resid_in, norm_gain, gate_weight, up_weight, down_weight, labels):
    x = lax.all_gather(resid_in, "hid", axis=0, tiled=True).astype(F32)
    ntok, block = x.shape
    total_sq = lax.psum(jnp.sum(x * x, axis=1), "tok")
    normed = (x * lax.rsqrt(total_sq / float(D) + 1e-05)[:, None] * norm_gain[None, :]).astype(BF16)

    def summed_over_tok(weight):
        product = jnp.dot(normed, weight, preferred_element_type=F32).astype(BF16)
        return lax.psum_scatter(product, "tok", scatter_dimension=0, tiled=True).astype(F32)

    hidden = (jax.nn.silu(summed_over_tok(gate_weight)) * summed_over_tok(up_weight)).astype(BF16)
    hidden = lax.all_gather(hidden, "tok", axis=0, tiled=True)
    partial_out = jnp.dot(hidden, down_weight, preferred_element_type=F32).astype(BF16)
    summed = lax.psum_scatter(partial_out, "hid", scatter_dimension=1, tiled=True).astype(F32)
    panel = block // n_hid
    x_cols = lax.dynamic_slice_in_dim(x, lax.axis_index("hid") * panel, panel, 1)
    resid_cols = (x_cols + summed).astype(BF16)
    everyone = lax.all_gather(resid_cols, ("tok", "hid"), axis=1, tiled=True)
    gram = lax.dot_general(
        resid_cols, everyone, (((0,), (0,)), ((), ())), preferred_element_type=F32
    ) / float(ntok)
    return (gram, class_means(resid_cols, labels))


def on_device(n_tok, n_hid, resid_in, norm_gain, gate_weight, *rest):
    panel = resid_in.shape[1] // n_hid
    fits = n_tok == 4 and n_hid == 8 and panel % 128 == 0 and gate_weight.shape[1] % TILE == 0 and gate_weight.shape[1] >= 3 * TILE
    body = on_line if fits else plain
    return body(n_tok, n_hid, resid_in, norm_gain, gate_weight, *rest)


def solution(mesh):
    return jax.shard_map(
        functools.partial(on_device, mesh.shape["tok"], mesh.shape["hid"]),
        mesh=mesh,
        in_specs=(
            P("hid", "tok"),
            P("tok"),
            P("tok", "hid"),
            P("tok", "hid"),
            P("hid", "tok"),
            P(),
        ),
        out_specs=(P(("tok", "hid"), None), P(("tok", "hid"), None)),
        check_vma=False,
    )
```

```python
import functools
import jax
import jax.numpy as jnp
from jax import lax
from jax.experimental import pallas as pl
from jax.experimental.pallas import tpu as pltpu
from jax.sharding import PartitionSpec as P

D = 8192
CLASSES = 64
TILE = 256
BF16 = jnp.bfloat16
F32 = jnp.float32
WHOLE = pl.BlockSpec(memory_space=pltpu.VMEM)
ANYWHERE = pl.BlockSpec(memory_space=pl.ANY)
SIDE = 128


def swap(value, axis, size, mask):
    return lax.ppermute(value, axis, [(i, i ^ mask) for i in range(size)])


def run(body, name, out_shape, operands, flops, bytes_accessed, in_specs=None, out_specs=WHOLE, **more):
    return pl.pallas_call(
        body,
        out_shape=out_shape,
        in_specs=[WHOLE] * len(operands) if in_specs is None else in_specs,
        out_specs=out_specs,
        compiler_params=pltpu.CompilerParams(vmem_limit_bytes=16 * 1024 * 1024),
        cost_estimate=pl.CostEstimate(flops=flops, bytes_accessed=bytes_accessed, transcendentals=0),
        name=name,
        **more,
    )(*operands)


def fetch(pieces, after, name):
    count = len(pieces)
    copies = []
    for number, (array, row, rows, column, columns) in enumerate(pieces):
        step = min(rows, 256)
        copies += [(number, at, step, row + at, column, columns) for at in range(0, rows, step)]

    def body(*refs):
        sources, targets, sems = refs[:count], refs[-1 - count:-1], refs[-1]
        started = []
        for sem, (number, at, step, row, column, columns) in enumerate(copies):
            copy = pltpu.make_async_copy(
                sources[number].at[pl.ds(row, step), pl.ds(column, columns)],
                targets[number].at[pl.ds(at, step), :],
                sems.at[sem],
            )
            copy.start()
            started.append(copy)
        for copy in started:
            copy.wait()

    size = sum(rows * columns * array.dtype.itemsize for array, _, rows, _, columns in pieces)
    return run(
        body, name,
        [pltpu.VMEM((rows, columns), array.dtype) for array, _, rows, _, columns in pieces],
        [pltpu.with_memory_space_constraint(piece[0], pltpu.HBM) for piece in pieces] + list(after),
        0, 0,
        in_specs=[ANYWHERE] * (count + len(after)),
        out_specs=[WHOLE] * count,
        scratch_shapes=[pltpu.SemaphoreType.DMA((len(copies),))],
    )


def tokens_kernel(masks, panel, *refs):
    blocks, gain, (lhs, cols, squares, x) = refs[:len(masks)], refs[len(masks)], refs[-4:]
    h = lax.axis_index("hid")
    rows = blocks[0].shape[0]
    for mask, block in zip(masks, blocks):
        x[pl.ds(pl.multiple_of((h ^ mask) * rows, rows), rows), :] = block[...]
    values = x[...].astype(F32)
    lhs[...] = (values * gain[...]).astype(BF16)
    squares[...] = jnp.sum(values * values, axis=1, keepdims=True)
    cols[...] = x[:, pl.ds(pl.multiple_of(h * panel, panel), panel)].astype(F32)


def split(value):
    lane = lax.broadcasted_iota(jnp.int32, (value.shape[0], SIDE), 1)
    out = jnp.zeros((value.shape[0], SIDE), F32)
    for part in range(3):
        rounded = value.astype(BF16).astype(F32)
        out = jnp.where(lane == part, rounded, out)
        value = value - rounded
    return out


def joined(parts):
    return jnp.sum(parts.astype(F32), axis=1, keepdims=True)


def gate_up_kernel(lhs_ref, gate_ref, up_ref, *refs):
    send_ref, keep_ref, both, side = refs[-4:]
    places = ((keep_ref, 0), (send_ref, 0), (keep_ref, 1), (send_ref, 1))
    rows = send_ref.shape[1]
    z = lax.axis_index("tok")
    lhs = lhs_ref[...]

    def hand_out(source, start, width):
        for d, (out, slot) in enumerate(places):
            at = pl.multiple_of((z ^ d) * rows, rows)
            out[slot, :, start:start + width] = source[pl.ds(at, rows), :].astype(BF16)

    for tile in range(gate_ref.shape[1] // TILE):
        cols = slice(tile * TILE, (tile + 1) * TILE)
        both[:, :TILE] = jnp.dot(lhs, gate_ref[:, cols], preferred_element_type=F32)
        both[:, TILE:] = jnp.dot(lhs, up_ref[:, cols], preferred_element_type=F32)
        hand_out(both, 2 * tile * TILE, 2 * TILE)
    if send_ref.shape[2] > 2 * gate_ref.shape[1]:
        side[...] = split(refs[0][...])
        hand_out(side, 2 * gate_ref.shape[1], SIDE)


def gate_up(lhs, gate, up, squares, n_tok, after=()):
    ntok, depth = lhs.shape
    width = gate.shape[1]
    rows = ntok // n_tok
    extra = [] if squares is None else [squares]
    shape = jax.ShapeDtypeStruct((2, rows, 2 * width + SIDE * len(extra)), BF16)
    return run(
        gate_up_kernel, "gate_up", [shape, shape], [lhs, gate, up, *extra, *after],
        0, 0,
        in_specs=[WHOLE] * (3 + len(extra)) + [ANYWHERE] * len(after),
        out_specs=[WHOLE] * 2,
        scratch_shapes=[pltpu.VMEM((ntok, 2 * TILE), F32), pltpu.VMEM((ntok, SIDE), F32)],
    )


def pair_total(keep, got, main, after):
    def body(keep_ref, got_ref, *refs):
        out = refs[-1]
        out[:, :main] = (keep_ref[1, :, :main].astype(F32) + got_ref[1, :, :main].astype(F32)).astype(BF16)
        if out.shape[1] > main:
            out[:, main:] = split(joined(keep_ref[1, :, main:]) + joined(got_ref[1, :, main:])).astype(BF16)

    size = keep.size // 2
    return run(
        body, "pair_total", jax.ShapeDtypeStruct(keep.shape[1:], BF16), [keep, got, *after],
        size, 6 * size, in_specs=[WHOLE] * 2 + [ANYWHERE] * len(after),
    )


def copy_after(value, after):
    def body(value_ref, *refs):
        refs[-1][...] = value_ref[...]

    return run(
        body, "copy", jax.ShapeDtypeStruct(value.shape, value.dtype), [value, *after],
        0, 4 * value.size, in_specs=[WHOLE] + [ANYWHERE] * len(after),
    )


def stack_after(blocks, after, extra=0):
    stacks = [block if block.ndim == 3 else block[None] for block in blocks]
    total = sum(stack.shape[0] for stack in stacks)
    rows = stacks[0].shape[1]

    def body(*refs):
        out = refs[len(stacks) + len(after)]
        at = 0
        for ref in refs[:len(stacks)]:
            out[at:at + ref.shape[0]] = ref[:, :rows, :]
            at += ref.shape[0]
        if extra:
            refs[-1][:rows, :] = out[at - 1]
            refs[-1][rows:, :] = out[at - 1, :extra, :]

    width, kind = blocks[0].shape[-1], blocks[0].dtype
    shapes = [jax.ShapeDtypeStruct((total, rows, width), kind)]
    shapes += [jax.ShapeDtypeStruct((rows + extra, width), kind)] if extra else []
    outs = run(
        body, "stack", shapes, [*stacks, *after], 0, 4 * sum(stack.size for stack in stacks),
        in_specs=[WHOLE] * len(stacks) + [ANYWHERE] * len(after),
        out_specs=[WHOLE] * len(shapes),
    )
    return outs if extra else outs[0]


def hidden_rows(chunks, widths, scale, after):
    rows = chunks[0][0].shape[1]
    given = [] if scale is None else [scale]

    def body(*refs):
        out_ref, scale_ref = refs[-2:]
        keep_ref, got_ref, over_ref = refs[:3]
        if scale is None:
            tail = slice(2 * widths[0], 2 * widths[0] + SIDE)
            squares = joined(keep_ref[0, :, tail]) + joined(got_ref[0, :, tail]) + joined(over_ref[:, tail])
            factor = lax.rsqrt(squares / float(D) + 1e-05)
        else:
            factor = refs[3 * len(chunks)][...]
        scale_ref[...] = factor
        start = 0
        for k, width in enumerate(widths):
            keep_ref, got_ref, over_ref = refs[3 * k:3 * k + 3]

            def total(at):
                cols = slice(at, at + TILE)
                return (
                    keep_ref[0, :, cols].astype(F32) + got_ref[0, :, cols].astype(F32) + over_ref[:, cols].astype(F32)
                ) * factor

            for at in range(0, width, TILE):
                gate, up = total(2 * at), total(2 * at + TILE)
                out_ref[:, start + at:start + at + TILE] = (jax.nn.silu(gate) * up).astype(BF16)
            start += width

    size = rows * sum(widths)
    return run(
        body, "hidden",
        [jax.ShapeDtypeStruct((rows, sum(widths)), BF16), jax.ShapeDtypeStruct((rows, 1), F32)],
        [part for chunk in chunks for part in chunk] + given + list(after), 20 * size, 14 * size,
        in_specs=[WHOLE] * (3 * len(chunks) + len(given)) + [ANYWHERE] * len(after),
        out_specs=[WHOLE] * 2,
    )


def down_kernel(masks, panel, n_blocks, add, *refs):
    blocks, weight, lhs, out = refs[:n_blocks], refs[n_blocks], refs[-1], refs[-2]
    before = refs[n_blocks + 1] if add else None
    z = lax.axis_index("tok")
    h = lax.axis_index("hid")
    rows = blocks[0].shape[0]
    for d, block in enumerate(blocks):
        lhs[pl.ds(pl.multiple_of((z ^ d) * rows, rows), rows), :] = block[...]
    values = lhs[...]
    for slot, mask in enumerate(masks):
        column = pl.multiple_of((h ^ mask) * panel, panel)
        total = jnp.dot(values, weight[:, pl.ds(column, panel)], preferred_element_type=F32)
        if before is not None:
            total = total + before[slot]
        out[slot] = total.astype(out.dtype)


def down(blocks, weight, masks, panel, kind, before=None, after=()):
    rows, depth = blocks[0].shape
    ntok = rows * len(blocks)
    return run(
        functools.partial(down_kernel, masks, panel, len(blocks), before is not None), "down",
        jax.ShapeDtypeStruct((len(masks), ntok, panel), kind),
        [*blocks, weight] + ([] if before is None else [before]) + list(after),
        2 * ntok * depth * panel * len(masks), 2 * depth * panel * len(masks),
        in_specs=[WHOLE] * (len(blocks) + 1 + (before is not None)) + [ANYWHERE] * len(after),
        scratch_shapes=[pltpu.VMEM((ntok, depth), BF16)],
    )


def chip_sum_kernel(mine_ref, other_ref, own_ref, *outs):
    own_ref[...] = mine_ref[0] + other_ref[0].astype(F32)
    for e, out in enumerate(outs):
        out[...] = (mine_ref[e + 1] + other_ref[e + 1].astype(F32)).astype(BF16)


def gram_kernel(slots, n_hid, ntok, classes, own_ref, *refs):
    stacks = refs[:len(slots)]
    outs, (tiles, sems) = refs[:-2], refs[-2:]
    out_ref = outs[-2] if classes else outs[-1]
    z = lax.axis_index("tok")
    h = lax.axis_index("hid")
    width = own_ref.shape[1]
    left = own_ref[...].T
    copies = []
    for stack, places in zip(stacks, slots):
        for at, (d, mask) in enumerate(places):
            number = len(copies)
            tiles[number] = jnp.dot(left, stack[at], preferred_element_type=F32) * (1.0 / ntok)
            column = ((z ^ d) * n_hid + (h ^ mask)) * width
            copy = pltpu.make_async_copy(
                tiles.at[number], out_ref.at[:, pl.ds(pl.multiple_of(column, width), width)], sems.at[number]
            )
            copy.start()
            copies.append(copy)
    if classes:
        labels, cross_ref = refs[len(slots)], outs[-1]
        onehot = (labels[...] == lax.broadcasted_iota(jnp.int32, (classes, ntok), 0)).astype(F32)
        counts = jnp.sum(onehot, axis=1, keepdims=True)
        sums = jnp.dot(onehot.astype(BF16), own_ref[...], preferred_element_type=F32)
        cross_ref[...] = sums / jnp.maximum(counts, 1.0)
    for copy in copies:
        copy.wait()


def gram_part(resid_cols, stacks, slots, n_tok, n_hid, before, labels=None):
    ntok, width = resid_cols.shape
    here = sum(len(places) for places in slots)
    gram_shape = pltpu.HBM((width, width * n_tok * n_hid), F32)
    extra, extra_specs = ([], []) if labels is None else ([labels[None, :]], [WHOLE])
    if before is not None:
        extra, extra_specs = extra + [before], extra_specs + [ANYWHERE]
    return run(
        functools.partial(gram_kernel, slots, n_hid, ntok, 0 if labels is None else CLASSES), "gram",
        [gram_shape] + ([] if labels is None else [jax.ShapeDtypeStruct((CLASSES, width), F32)]),
        [resid_cols, *stacks, *extra],
        2 * ntok * width * width * here, 4 * width * width * here,
        in_specs=[WHOLE] * (1 + len(stacks)) + extra_specs,
        out_specs=[ANYWHERE] + ([] if labels is None else [WHOLE]),
        input_output_aliases={} if before is None else {len(stacks) + len(extra): 0},
        scratch_shapes=[pltpu.VMEM((here, width, width), F32), pltpu.SemaphoreType.DMA((here,))],
    )


def class_means(resid_cols, labels):
    onehot = (labels[:, None] == jnp.arange(CLASSES, dtype=jnp.int32)[None, :]).astype(BF16)
    counts = jnp.sum(onehot.astype(F32), axis=0)
    class_sums = lax.dot_general(
        resid_cols, onehot, (((0,), (0,)), ((), ())), preferred_element_type=F32
    )
    return class_sums / jnp.maximum(counts, 1.0)[None, :]


def on_line(n_tok, n_hid, resid_in, norm_gain, gate_weight, up_weight, down_weight, labels):
    rows, block = resid_in.shape
    ntok, panel = rows * n_hid, block // n_hid
    depth, shard_ff = gate_weight.shape
    tiles = shard_ff // TILE
    ends = [TILE * (tiles * k // 3) for k in range(4)]
    chip_masks = list(range(2, n_hid, 2))

    def part(weight, k):
        return weight, 0, depth, ends[k], ends[k + 1] - ends[k]

    near = [resid_in] + [swap(resid_in, "hid", n_hid, mask) for mask in chip_masks]
    gate_0, up_0, own_x, gain = fetch(
        [
            part(gate_weight, 0),
            part(up_weight, 0),
            (resid_in, 0, rows, 0, block),
            (norm_gain[None, :], 0, 1, 0, block),
        ],
        (), "fetch_first",
    )
    relayed = copy_after(near[1], (gain,))
    far = [swap(piece, "hid", n_hid, 1) for piece in [near[0], relayed, *near[2:]]]
    masks = [0] + chip_masks + [1] + [mask + 1 for mask in chip_masks]
    lhs, x_cols, squares = run(
        functools.partial(tokens_kernel, masks, panel), "tokens",
        (
            jax.ShapeDtypeStruct((ntok, block), BF16),
            jax.ShapeDtypeStruct((ntok, panel), F32),
            jax.ShapeDtypeStruct((ntok, 1), F32),
        ),
        [own_x, *near[1:], *far, gain],
        4 * ntok * block, 4 * ntok * block,
        out_specs=(WHOLE, WHOLE, WHOLE),
        scratch_shapes=[pltpu.VMEM((ntok, block), BF16)],
    )

    widths = [ends[k + 1] - ends[k] for k in range(3)]
    send_0, keep_0 = gate_up(lhs, gate_0, up_0, squares, n_tok)
    got_0 = swap(send_0, "tok", n_tok, 1)
    gate_1, up_1 = fetch([part(gate_weight, 1), part(up_weight, 1)], (send_0,), "fetch_gate_up")
    send_1, keep_1 = gate_up(lhs, gate_1, up_1, None, n_tok)
    got_1 = swap(send_1, "tok", n_tok, 1)
    sum_0 = pair_total(keep_0, got_0, 2 * widths[0], (send_1,))
    over_0 = swap(sum_0, "tok", n_tok, 2)
    gate_2, up_2 = fetch([part(gate_weight, 2), part(up_weight, 2)], (sum_0,), "fetch_gate_up")
    send_2, keep_2 = gate_up(lhs, gate_2, up_2, None, n_tok)
    got_2 = swap(send_2, "tok", n_tok, 1)
    sum_1 = pair_total(keep_1, got_1, 2 * widths[1], (send_2,))
    over_1 = swap(sum_1, "tok", n_tok, 2)
    down_b, = fetch([(down_weight, ends[2], widths[2], 0, block)], (sum_1,), "fetch_down")
    sum_2 = pair_total(keep_2, got_2, 2 * widths[2], (down_b,))
    over_2 = swap(sum_2, "tok", n_tok, 2)
    down_a, = fetch([(down_weight, 0, ends[2], 0, block)], (sum_2,), "fetch_down")

    a_own, scale = hidden_rows([(keep_0, got_0, over_0), (keep_1, got_1, over_1)], widths[:2], None, (down_a,))
    a_two = swap(a_own, "tok", n_tok, 2)
    a_one = swap(a_own, "tok", n_tok, 1)
    b_own, _ = hidden_rows([(keep_2, got_2, over_2)], widths[2:], scale, ())
    b_two = swap(b_own, "tok", n_tok, 2)
    b_one = swap(b_own, "tok", n_tok, 1)
    a_three = swap(copy_after(a_two, (b_two, b_one, a_one)), "tok", n_tok, 1)
    b_three = swap(b_two, "tok", n_tok, 1)
    hidden_a = [a_own, a_one, a_two, a_three]
    hidden_b = [b_own, b_one, b_two, b_three]

    here = [0] + chip_masks
    there = [mask + 1 for mask in here]
    other = down(hidden_b, down_b, there, panel, BF16, down(hidden_a, down_a, there, panel, F32))
    mine = down(hidden_b, down_b, here, panel, F32, down(hidden_a, down_a, here, panel, F32, after=(other,)))
    other = swap(other, "hid", n_hid, 1)
    summed, *sends = run(
        chip_sum_kernel, "chip_sum",
        [jax.ShapeDtypeStruct((ntok, panel), F32)] + [jax.ShapeDtypeStruct((ntok, panel), BF16)] * len(chip_masks),
        [mine, other], mine.size, 8 * mine.size,
        out_specs=[WHOLE] * len(here),
    )
    for mask, value in reversed(list(zip(chip_masks, sends))):
        summed = summed + swap(value, "hid", n_hid, mask).astype(F32)
    resid_cols = (x_cols + summed).astype(BF16)

    column = [swap(resid_cols, "tok", n_tok, d) for d in range(1, n_tok)]
    across = swap(resid_cols, "hid", n_hid, 6)
    line, farthest = stack_after([resid_cols, *column], (across,), 16)
    beside = [swap(line, "hid", n_hid, mask) for mask in (2, 4)]
    across_line = [swap(across, "tok", n_tok, d) for d in (1, 2)] + [swap(farthest, "hid", n_hid, 6)]
    line_far = swap(line, "hid", n_hid, 1)
    across_far = swap(across, "hid", n_hid, 1)
    line_slots = [[(d, mask) for d in range(n_tok)] for mask in range(n_hid)]
    gram, cross = gram_part(
        resid_cols, [line, line_far, across[None], across_far[None]],
        [line_slots[0], line_slots[1], [(0, 6)], [(0, 7)]], n_tok, n_hid, None, labels,
    )
    done = pltpu.with_memory_space_constraint(gram, pltpu.HBM)
    near = stack_after([*beside, *across_line], (done,))
    far = swap(near, "hid", n_hid, 1)
    for stack, core in ((near, 0), (far, 1)):
        slots = line_slots[2 + core] + line_slots[4 + core] + line_slots[6 + core][1:]
        gram, = gram_part(resid_cols, [stack], [slots], n_tok, n_hid, gram)
    return (gram, cross.T)


def plain(n_tok, n_hid, resid_in, norm_gain, gate_weight, up_weight, down_weight, labels):
    x = lax.all_gather(resid_in, "hid", axis=0, tiled=True).astype(F32)
    ntok, block = x.shape
    total_sq = lax.psum(jnp.sum(x * x, axis=1), "tok")
    normed = (x * lax.rsqrt(total_sq / float(D) + 1e-05)[:, None] * norm_gain[None, :]).astype(BF16)

    def summed_over_tok(weight):
        product = jnp.dot(normed, weight, preferred_element_type=F32).astype(BF16)
        return lax.psum_scatter(product, "tok", scatter_dimension=0, tiled=True).astype(F32)

    hidden = (jax.nn.silu(summed_over_tok(gate_weight)) * summed_over_tok(up_weight)).astype(BF16)
    hidden = lax.all_gather(hidden, "tok", axis=0, tiled=True)
    partial_out = jnp.dot(hidden, down_weight, preferred_element_type=F32).astype(BF16)
    summed = lax.psum_scatter(partial_out, "hid", scatter_dimension=1, tiled=True).astype(F32)
    panel = block // n_hid
    x_cols = lax.dynamic_slice_in_dim(x, lax.axis_index("hid") * panel, panel, 1)
    resid_cols = (x_cols + summed).astype(BF16)
    everyone = lax.all_gather(resid_cols, ("tok", "hid"), axis=1, tiled=True)
    gram = lax.dot_general(
        resid_cols, everyone, (((0,), (0,)), ((), ())), preferred_element_type=F32
    ) / float(ntok)
    return (gram, class_means(resid_cols, labels))


def on_device(n_tok, n_hid, resid_in, norm_gain, gate_weight, *rest):
    panel = resid_in.shape[1] // n_hid
    fits = n_tok == 4 and n_hid == 8 and panel % 128 == 0 and gate_weight.shape[1] % TILE == 0 and gate_weight.shape[1] >= 3 * TILE
    body = on_line if fits else plain
    return body(n_tok, n_hid, resid_in, norm_gain, gate_weight, *rest)


def solution(mesh):
    return jax.shard_map(
        functools.partial(on_device, mesh.shape["tok"], mesh.shape["hid"]),
        mesh=mesh,
        in_specs=(
            P("hid", "tok"),
            P("tok"),
            P("tok", "hid"),
            P("tok", "hid"),
            P("hid", "tok"),
            P(),
        ),
        out_specs=(P(("tok", "hid"), None), P(("tok", "hid"), None)),
        check_vma=False,
    )
```

```python
import functools
import jax
import jax.numpy as jnp
from jax import lax
from jax.experimental import pallas as pl
from jax.experimental.pallas import tpu as pltpu
from jax.sharding import PartitionSpec as P

D = 8192
CLASSES = 64
TILE = 256
BF16 = jnp.bfloat16
F32 = jnp.float32
WHOLE = pl.BlockSpec(memory_space=pltpu.VMEM)
ANYWHERE = pl.BlockSpec(memory_space=pl.ANY)
SIDE = 128


def swap(value, axis, size, mask):
    return lax.ppermute(value, axis, [(i, i ^ mask) for i in range(size)])


def run(body, name, out_shape, operands, flops, bytes_accessed, in_specs=None, out_specs=WHOLE, **more):
    return pl.pallas_call(
        body,
        out_shape=out_shape,
        in_specs=[WHOLE] * len(operands) if in_specs is None else in_specs,
        out_specs=out_specs,
        compiler_params=pltpu.CompilerParams(vmem_limit_bytes=16 * 1024 * 1024),
        cost_estimate=pl.CostEstimate(flops=flops, bytes_accessed=bytes_accessed, transcendentals=0),
        name=name,
        **more,
    )(*operands)


def fetch(pieces, after, name):
    count = len(pieces)
    copies = []
    for number, (array, row, rows, column, columns) in enumerate(pieces):
        step = min(rows, 256)
        copies += [(number, at, step, row + at, column, columns) for at in range(0, rows, step)]

    def body(*refs):
        sources, targets, sems = refs[:count], refs[-1 - count:-1], refs[-1]
        started = []
        for sem, (number, at, step, row, column, columns) in enumerate(copies):
            copy = pltpu.make_async_copy(
                sources[number].at[pl.ds(row, step), pl.ds(column, columns)],
                targets[number].at[pl.ds(at, step), :],
                sems.at[sem],
            )
            copy.start()
            started.append(copy)
        for copy in started:
            copy.wait()

    size = sum(rows * columns * array.dtype.itemsize for array, _, rows, _, columns in pieces)
    return run(
        body, name,
        [pltpu.VMEM((rows, columns), array.dtype) for array, _, rows, _, columns in pieces],
        [pltpu.with_memory_space_constraint(piece[0], pltpu.HBM) for piece in pieces] + list(after),
        0, 0,
        in_specs=[ANYWHERE] * (count + len(after)),
        out_specs=[WHOLE] * count,
        scratch_shapes=[pltpu.SemaphoreType.DMA((len(copies),))],
    )


def tokens_kernel(masks, panel, *refs):
    blocks, gain, (lhs, cols, squares, x) = refs[:len(masks)], refs[len(masks)], refs[-4:]
    h = lax.axis_index("hid")
    rows = blocks[0].shape[0]
    for mask, block in zip(masks, blocks):
        x[pl.ds(pl.multiple_of((h ^ mask) * rows, rows), rows), :] = block[...]
    values = x[...].astype(F32)
    lhs[...] = (values * gain[...]).astype(BF16)
    squares[...] = jnp.sum(values * values, axis=1, keepdims=True)
    cols[...] = x[:, pl.ds(pl.multiple_of(h * panel, panel), panel)].astype(F32)


def split(value):
    lane = lax.broadcasted_iota(jnp.int32, (value.shape[0], SIDE), 1)
    out = jnp.zeros((value.shape[0], SIDE), F32)
    for part in range(3):
        rounded = value.astype(BF16).astype(F32)
        out = jnp.where(lane == part, rounded, out)
        value = value - rounded
    return out


def joined(parts):
    return jnp.sum(parts.astype(F32), axis=1, keepdims=True)


def gate_up_kernel(lhs_ref, gate_ref, up_ref, *refs):
    send_ref, keep_ref, both, side = refs[-4:]
    places = ((keep_ref, 0), (send_ref, 0), (keep_ref, 1), (send_ref, 1))
    rows = send_ref.shape[1]
    z = lax.axis_index("tok")
    lhs = lhs_ref[...]

    def hand_out(source, start, width):
        for d, (out, slot) in enumerate(places):
            at = pl.multiple_of((z ^ d) * rows, rows)
            out[slot, :, start:start + width] = source[pl.ds(at, rows), :].astype(BF16)

    for tile in range(gate_ref.shape[1] // TILE):
        cols = slice(tile * TILE, (tile + 1) * TILE)
        both[:, :TILE] = jnp.dot(lhs, gate_ref[:, cols], preferred_element_type=F32)
        both[:, TILE:] = jnp.dot(lhs, up_ref[:, cols], preferred_element_type=F32)
        hand_out(both, 2 * tile * TILE, 2 * TILE)
    if send_ref.shape[2] > 2 * gate_ref.shape[1]:
        side[...] = split(refs[0][...])
        hand_out(side, 2 * gate_ref.shape[1], SIDE)


def gate_up(lhs, gate, up, squares, n_tok, after=()):
    ntok, depth = lhs.shape
    width = gate.shape[1]
    rows = ntok // n_tok
    extra = [] if squares is None else [squares]
    shape = jax.ShapeDtypeStruct((2, rows, 2 * width + SIDE * len(extra)), BF16)
    return run(
        gate_up_kernel, "gate_up", [shape, shape], [lhs, gate, up, *extra, *after],
        0, 0,
        in_specs=[WHOLE] * (3 + len(extra)) + [ANYWHERE] * len(after),
        out_specs=[WHOLE] * 2,
        scratch_shapes=[pltpu.VMEM((ntok, 2 * TILE), F32), pltpu.VMEM((ntok, SIDE), F32)],
    )


def pair_total(keep, got, main, after):
    def body(keep_ref, got_ref, *refs):
        out = refs[-1]
        out[:, :main] = (keep_ref[1, :, :main].astype(F32) + got_ref[1, :, :main].astype(F32)).astype(BF16)
        if out.shape[1] > main:
            out[:, main:] = split(joined(keep_ref[1, :, main:]) + joined(got_ref[1, :, main:])).astype(BF16)

    size = keep.size // 2
    return run(
        body, "pair_total", jax.ShapeDtypeStruct(keep.shape[1:], BF16), [keep, got, *after],
        size, 6 * size, in_specs=[WHOLE] * 2 + [ANYWHERE] * len(after),
    )


def copy_after(value, after):
    def body(value_ref, *refs):
        refs[-1][...] = value_ref[...]

    return run(
        body, "copy", jax.ShapeDtypeStruct(value.shape, value.dtype), [value, *after],
        0, 4 * value.size, in_specs=[WHOLE] + [ANYWHERE] * len(after),
    )


def stack_after(blocks, after, extra=0):
    stacks = [block if block.ndim == 3 else block[None] for block in blocks]
    total = sum(stack.shape[0] for stack in stacks)
    rows = stacks[0].shape[1]

    def body(*refs):
        out = refs[len(stacks) + len(after)]
        at = 0
        for ref in refs[:len(stacks)]:
            out[at:at + ref.shape[0]] = ref[:, :rows, :]
            at += ref.shape[0]
        if extra:
            refs[-1][:rows, :] = out[at - 1]
            refs[-1][rows:, :] = out[at - 1, :extra, :]

    width, kind = blocks[0].shape[-1], blocks[0].dtype
    shapes = [jax.ShapeDtypeStruct((total, rows, width), kind)]
    shapes += [jax.ShapeDtypeStruct((rows + extra, width), kind)] if extra else []
    outs = run(
        body, "stack", shapes, [*stacks, *after], 0, 4 * sum(stack.size for stack in stacks),
        in_specs=[WHOLE] * len(stacks) + [ANYWHERE] * len(after),
        out_specs=[WHOLE] * len(shapes),
    )
    return outs if extra else outs[0]


def hidden_rows(chunks, widths, scale, after):
    rows = chunks[0][0].shape[1]
    given = [] if scale is None else [scale]

    def body(*refs):
        out_ref, scale_ref = refs[-2:]
        keep_ref, got_ref, over_ref = refs[:3]
        if scale is None:
            tail = slice(2 * widths[0], 2 * widths[0] + SIDE)
            squares = joined(keep_ref[0, :, tail]) + joined(got_ref[0, :, tail]) + joined(over_ref[:, tail])
            factor = lax.rsqrt(squares / float(D) + 1e-05)
        else:
            factor = refs[3 * len(chunks)][...]
        scale_ref[...] = factor
        start = 0
        for k, width in enumerate(widths):
            keep_ref, got_ref, over_ref = refs[3 * k:3 * k + 3]

            def total(at):
                cols = slice(at, at + TILE)
                return (
                    keep_ref[0, :, cols].astype(F32) + got_ref[0, :, cols].astype(F32) + over_ref[:, cols].astype(F32)
                ) * factor

            for at in range(0, width, TILE):
                gate, up = total(2 * at), total(2 * at + TILE)
                out_ref[:, start + at:start + at + TILE] = (jax.nn.silu(gate) * up).astype(BF16)
            start += width

    size = rows * sum(widths)
    return run(
        body, "hidden",
        [jax.ShapeDtypeStruct((rows, sum(widths)), BF16), jax.ShapeDtypeStruct((rows, 1), F32)],
        [part for chunk in chunks for part in chunk] + given + list(after), 20 * size, 14 * size,
        in_specs=[WHOLE] * (3 * len(chunks) + len(given)) + [ANYWHERE] * len(after),
        out_specs=[WHOLE] * 2,
    )


def down_kernel(masks, panel, n_blocks, add, *refs):
    blocks, weight, lhs, out = refs[:n_blocks], refs[n_blocks], refs[-1], refs[-2]
    before = refs[n_blocks + 1] if add else None
    z = lax.axis_index("tok")
    h = lax.axis_index("hid")
    rows = blocks[0].shape[0]
    for d, block in zip((0, 2, 1, 3), blocks):
        lhs[pl.ds(pl.multiple_of((z ^ d) * rows, rows), rows), :] = block[...]
    values = lhs[...]
    for slot, mask in enumerate(masks):
        column = pl.multiple_of((h ^ mask) * panel, panel)
        total = jnp.dot(values, weight[:, pl.ds(column, panel)], preferred_element_type=F32)
        if before is not None:
            total = total + before[slot]
        out[slot] = total.astype(out.dtype)


def down(blocks, weight, masks, panel, kind, before=None, after=()):
    rows, depth = blocks[0].shape
    ntok = rows * len(blocks)
    return run(
        functools.partial(down_kernel, masks, panel, len(blocks), before is not None), "down",
        jax.ShapeDtypeStruct((len(masks), ntok, panel), kind),
        [*blocks, weight] + ([] if before is None else [before]) + list(after),
        2 * ntok * depth * panel * len(masks), 2 * depth * panel * len(masks),
        in_specs=[WHOLE] * (len(blocks) + 1 + (before is not None)) + [ANYWHERE] * len(after),
        scratch_shapes=[pltpu.VMEM((ntok, depth), BF16)],
    )


def chip_sum_kernel(mine_ref, other_ref, own_ref, *outs):
    own_ref[...] = mine_ref[0] + other_ref[0].astype(F32)
    for e, out in enumerate(outs):
        out[...] = (mine_ref[e + 1] + other_ref[e + 1].astype(F32)).astype(BF16)


def gram_kernel(slots, n_hid, ntok, classes, own_ref, *refs):
    stacks = refs[:len(slots)]
    outs, (tiles, sems) = refs[:-2], refs[-2:]
    out_ref = outs[-2] if classes else outs[-1]
    z = lax.axis_index("tok")
    h = lax.axis_index("hid")
    width = own_ref.shape[1]
    left = own_ref[...].T
    copies = []
    for stack, places in zip(stacks, slots):
        for at, (d, mask) in enumerate(places):
            number = len(copies)
            tiles[number] = jnp.dot(left, stack[at], preferred_element_type=F32) * (1.0 / ntok)
            column = ((z ^ d) * n_hid + (h ^ mask)) * width
            copy = pltpu.make_async_copy(
                tiles.at[number], out_ref.at[:, pl.ds(pl.multiple_of(column, width), width)], sems.at[number]
            )
            copy.start()
            copies.append(copy)
    if classes:
        labels, cross_ref = refs[len(slots)], outs[-1]
        onehot = (labels[...] == lax.broadcasted_iota(jnp.int32, (classes, ntok), 0)).astype(F32)
        counts = jnp.sum(onehot, axis=1, keepdims=True)
        sums = jnp.dot(onehot.astype(BF16), own_ref[...], preferred_element_type=F32)
        cross_ref[...] = sums / jnp.maximum(counts, 1.0)
    for copy in copies:
        copy.wait()


def gram_part(resid_cols, stacks, slots, n_tok, n_hid, before, labels=None):
    ntok, width = resid_cols.shape
    here = sum(len(places) for places in slots)
    gram_shape = pltpu.HBM((width, width * n_tok * n_hid), F32)
    extra, extra_specs = ([], []) if labels is None else ([labels[None, :]], [WHOLE])
    if before is not None:
        extra, extra_specs = extra + [before], extra_specs + [ANYWHERE]
    return run(
        functools.partial(gram_kernel, slots, n_hid, ntok, 0 if labels is None else CLASSES), "gram",
        [gram_shape] + ([] if labels is None else [jax.ShapeDtypeStruct((CLASSES, width), F32)]),
        [resid_cols, *stacks, *extra],
        2 * ntok * width * width * here, 4 * width * width * here,
        in_specs=[WHOLE] * (1 + len(stacks)) + extra_specs,
        out_specs=[ANYWHERE] + ([] if labels is None else [WHOLE]),
        input_output_aliases={} if before is None else {len(stacks) + len(extra): 0},
        scratch_shapes=[pltpu.VMEM((here, width, width), F32), pltpu.SemaphoreType.DMA((here,))],
    )


def class_means(resid_cols, labels):
    onehot = (labels[:, None] == jnp.arange(CLASSES, dtype=jnp.int32)[None, :]).astype(BF16)
    counts = jnp.sum(onehot.astype(F32), axis=0)
    class_sums = lax.dot_general(
        resid_cols, onehot, (((0,), (0,)), ((), ())), preferred_element_type=F32
    )
    return class_sums / jnp.maximum(counts, 1.0)[None, :]


def on_line(n_tok, n_hid, resid_in, norm_gain, gate_weight, up_weight, down_weight, labels):
    rows, block = resid_in.shape
    ntok, panel = rows * n_hid, block // n_hid
    depth, shard_ff = gate_weight.shape
    tiles = shard_ff // TILE
    ends = [TILE * (tiles * k // 3) for k in range(4)]
    chip_masks = list(range(2, n_hid, 2))

    def part(weight, k):
        return weight, 0, depth, ends[k], ends[k + 1] - ends[k]

    near = [resid_in] + [swap(resid_in, "hid", n_hid, mask) for mask in chip_masks]
    gate_0, up_0, own_x, gain = fetch(
        [
            part(gate_weight, 0),
            part(up_weight, 0),
            (resid_in, 0, rows, 0, block),
            (norm_gain[None, :], 0, 1, 0, block),
        ],
        (), "fetch_first",
    )
    relayed = copy_after(near[1], (gain,))
    far = [swap(piece, "hid", n_hid, 1) for piece in [near[0], relayed, *near[2:]]]
    masks = [0] + chip_masks + [1] + [mask + 1 for mask in chip_masks]
    lhs, x_cols, squares = run(
        functools.partial(tokens_kernel, masks, panel), "tokens",
        (
            jax.ShapeDtypeStruct((ntok, block), BF16),
            jax.ShapeDtypeStruct((ntok, panel), F32),
            jax.ShapeDtypeStruct((ntok, 1), F32),
        ),
        [own_x, *near[1:], *far, gain],
        4 * ntok * block, 4 * ntok * block,
        out_specs=(WHOLE, WHOLE, WHOLE),
        scratch_shapes=[pltpu.VMEM((ntok, block), BF16)],
    )

    widths = [ends[k + 1] - ends[k] for k in range(3)]
    send_0, keep_0 = gate_up(lhs, gate_0, up_0, squares, n_tok)
    got_0 = swap(send_0, "tok", n_tok, 1)
    gate_1, up_1 = fetch([part(gate_weight, 1), part(up_weight, 1)], (send_0,), "fetch_gate_up")
    send_1, keep_1 = gate_up(lhs, gate_1, up_1, None, n_tok)
    got_1 = swap(send_1, "tok", n_tok, 1)
    sum_0 = pair_total(keep_0, got_0, 2 * widths[0], (send_1,))
    over_0 = swap(sum_0, "tok", n_tok, 2)
    gate_2, up_2 = fetch([part(gate_weight, 2), part(up_weight, 2)], (sum_0,), "fetch_gate_up")
    send_2, keep_2 = gate_up(lhs, gate_2, up_2, None, n_tok)
    got_2 = swap(send_2, "tok", n_tok, 1)
    sum_1 = pair_total(keep_1, got_1, 2 * widths[1], (send_2,))
    over_1 = swap(sum_1, "tok", n_tok, 2)
    down_b, = fetch([(down_weight, ends[2], widths[2], 0, block)], (sum_1,), "fetch_down")
    sum_2 = pair_total(keep_2, got_2, 2 * widths[2], (down_b,))
    over_2 = swap(sum_2, "tok", n_tok, 2)
    down_a, = fetch([(down_weight, 0, ends[2], 0, block)], (sum_2,), "fetch_down")

    a_own, scale = hidden_rows([(keep_0, got_0, over_0), (keep_1, got_1, over_1)], widths[:2], None, (down_a,))
    a_two = swap(a_own, "tok", n_tok, 2)
    a_one = swap(a_own, "tok", n_tok, 1)
    b_own, _ = hidden_rows([(keep_2, got_2, over_2)], widths[2:], scale, ())
    b_two = swap(b_own, "tok", n_tok, 2)
    b_one = swap(b_own, "tok", n_tok, 1)
    a_three = swap(copy_after(a_two, (b_two, b_one, a_one)), "tok", n_tok, 1)
    b_three = swap(b_two, "tok", n_tok, 1)
    hidden_a = [a_own, a_two, a_one, a_three]
    hidden_b = [b_own, b_two, b_one, b_three]

    here = [0] + chip_masks
    there = [mask + 1 for mask in here]
    other = down(hidden_b, down_b, there, panel, BF16, down(hidden_a, down_a, there, panel, F32))
    mine = down(hidden_b, down_b, here, panel, F32, down(hidden_a, down_a, here, panel, F32, after=(other,)))
    other = swap(other, "hid", n_hid, 1)
    summed, *sends = run(
        chip_sum_kernel, "chip_sum",
        [jax.ShapeDtypeStruct((ntok, panel), F32)] + [jax.ShapeDtypeStruct((ntok, panel), BF16)] * len(chip_masks),
        [mine, other], mine.size, 8 * mine.size,
        out_specs=[WHOLE] * len(here),
    )
    for mask, value in reversed(list(zip(chip_masks, sends))):
        summed = summed + swap(value, "hid", n_hid, mask).astype(F32)
    resid_cols = (x_cols + summed).astype(BF16)

    column = [swap(resid_cols, "tok", n_tok, d) for d in range(1, n_tok)]
    across = swap(resid_cols, "hid", n_hid, 6)
    line, farthest = stack_after([resid_cols, *column], (across,), 16)
    beside = [swap(line, "hid", n_hid, mask) for mask in (2, 4)]
    across_line = [swap(across, "tok", n_tok, d) for d in (1, 2)] + [swap(farthest, "hid", n_hid, 6)]
    line_far = swap(line, "hid", n_hid, 1)
    across_far = swap(across, "hid", n_hid, 1)
    line_slots = [[(d, mask) for d in range(n_tok)] for mask in range(n_hid)]
    gram, cross = gram_part(
        resid_cols, [line, line_far, across[None], across_far[None]],
        [line_slots[0], line_slots[1], [(0, 6)], [(0, 7)]], n_tok, n_hid, None, labels,
    )
    done = pltpu.with_memory_space_constraint(gram, pltpu.HBM)
    near = stack_after([*beside, *across_line], (done,))
    far = swap(near, "hid", n_hid, 1)
    for stack, core in ((near, 0), (far, 1)):
        slots = line_slots[2 + core] + line_slots[4 + core] + line_slots[6 + core][1:]
        gram, = gram_part(resid_cols, [stack], [slots], n_tok, n_hid, gram)
    return (gram, cross.T)


def plain(n_tok, n_hid, resid_in, norm_gain, gate_weight, up_weight, down_weight, labels):
    x = lax.all_gather(resid_in, "hid", axis=0, tiled=True).astype(F32)
    ntok, block = x.shape
    total_sq = lax.psum(jnp.sum(x * x, axis=1), "tok")
    normed = (x * lax.rsqrt(total_sq / float(D) + 1e-05)[:, None] * norm_gain[None, :]).astype(BF16)

    def summed_over_tok(weight):
        product = jnp.dot(normed, weight, preferred_element_type=F32).astype(BF16)
        return lax.psum_scatter(product, "tok", scatter_dimension=0, tiled=True).astype(F32)

    hidden = (jax.nn.silu(summed_over_tok(gate_weight)) * summed_over_tok(up_weight)).astype(BF16)
    hidden = lax.all_gather(hidden, "tok", axis=0, tiled=True)
    partial_out = jnp.dot(hidden, down_weight, preferred_element_type=F32).astype(BF16)
    summed = lax.psum_scatter(partial_out, "hid", scatter_dimension=1, tiled=True).astype(F32)
    panel = block // n_hid
    x_cols = lax.dynamic_slice_in_dim(x, lax.axis_index("hid") * panel, panel, 1)
    resid_cols = (x_cols + summed).astype(BF16)
    everyone = lax.all_gather(resid_cols, ("tok", "hid"), axis=1, tiled=True)
    gram = lax.dot_general(
        resid_cols, everyone, (((0,), (0,)), ((), ())), preferred_element_type=F32
    ) / float(ntok)
    return (gram, class_means(resid_cols, labels))


def on_device(n_tok, n_hid, resid_in, norm_gain, gate_weight, *rest):
    panel = resid_in.shape[1] // n_hid
    fits = n_tok == 4 and n_hid == 8 and panel % 128 == 0 and gate_weight.shape[1] % TILE == 0 and gate_weight.shape[1] >= 3 * TILE
    body = on_line if fits else plain
    return body(n_tok, n_hid, resid_in, norm_gain, gate_weight, *rest)


def solution(mesh):
    return jax.shard_map(
        functools.partial(on_device, mesh.shape["tok"], mesh.shape["hid"]),
        mesh=mesh,
        in_specs=(
            P("hid", "tok"),
            P("tok"),
            P("tok", "hid"),
            P("tok", "hid"),
            P("hid", "tok"),
            P(),
        ),
        out_specs=(P(("tok", "hid"), None), P(("tok", "hid"), None)),
        check_vma=False,
    )
```
